32 devices in a mesh: dp: 4 (over y, core), expert: 8 (over z, x).
Axes of the slice: x: 2, y: 2, z: 4, core: 2. Of those that a mesh axis runs over, the one named last changes fastest.
Arguments:
- tokens: bfloat16 [4096, 3072], P(('dp', 'expert')), may hold values from -6 to 6
- cotangent: bfloat16 [4096, 3072], P(('dp', 'expert')), may hold values from -0.3125 to 0.3125
- route_ids: int32 [4096, 2], P(('dp', 'expert')), may hold values from 0 to 7, all different within a row; in each aligned block of 128 rows (0 to 127, 128 to 255, ...) at most 36 rows name the same one
- route_probs: float32 [4096, 2], P(('dp', 'expert')), may hold values from 0.2 to 1
- gate_weight: bfloat16 [3072, 8192], P(None, 'expert'), may hold values from -0.109375 to 0.109375
- up_weight: bfloat16 [3072, 8192], P(None, 'expert'), may hold values from -0.109375 to 0.109375
- down_weight: bfloat16 [8192, 3072], P('expert'), may hold values from -0.0625 to 0.0625
Outputs:
- token_grad: bfloat16 [4096, 3072], P(('dp', 'expert'))
- gate_grad: bfloat16 [3072, 8192], P('dp', 'expert')
- up_grad: bfloat16 [3072, 8192], P('dp', 'expert')
- down_grad: bfloat16 [8192, 3072], P('expert', 'dp')
The draws below stay inside these ranges and needn't reach their ends.
Inputs may be any that keep to these rules, and one draw needn't show every extreme that they name: `route_ids`: in every block of 128 consecutive tokens (the tokens of one device) at most 36 tokens name any one expert, a bound that some block reaches; a token's 2 ids differ.
All inputs are finite; a program needn't handle non-finite values.
Results may differ from the reference program's by a relative error of at most 0.023.
Values may be sent and summed in bfloat16 or wider, within the bound.
No kernel may reach another device: no remote copies, remote signals or barrier semaphores. Data moves between devices by JAX's collectives and lax.ppermute only.
A program may use at most 128 MiB of HBM per device.

```python
import math
import jax
import jax.numpy as jnp
import numpy as np
from jax import lax

D = 3072
HID = 8192
EXPERTS = 8
TOP = 2
TOK_DEV = 128
CAP = 36
HID_DEV = 1024
TOKENS = 4096
N_DP = 4
N_EXPERT = 8


def shard_levels(own_key, extent, split, low, top_value):
    def one(dim, blocks):
        heights = jax.random.uniform(jax.random.fold_in(jax.random.fold_in(own_key, 6), dim), (blocks,), jnp.float32, low / len(split), top_value / len(split))
        return jnp.repeat(jnp.exp(heights), extent[dim] // blocks).reshape((-1,) + (1,) * (len(extent) - dim - 1))

    loudness = one(*split[0])
    for cut in split[1:]:
        loudness = loudness * one(*cut)
    return loudness


def assign_block(stream_key, own, number, rows, count, top, most, skew):
    order = jax.random.permutation(stream_key, count)
    heavy_load, ordinary = load_shares(count, rows * top, most, skew, True), load_shares(count, rows * top, most, skew, False)
    places = jnp.arange(count)

    def named(tallies, offset_by):
        used = int((tallies > 0).sum())
        fixed = max(1, used // 4)
        shifted = fixed + (places - fixed + offset_by * (used - fixed)) % max(1, count - fixed)
        return jnp.zeros((count,), jnp.int32).at[order[jnp.where(places < fixed, places, shifted)]].set(jnp.asarray(tallies, jnp.int32))

    tallies = jnp.where(number % 4 == 0, named(heavy_load, number // 4), named(ordinary, number - number // 4 - 1))
    mixed = jax.random.permutation(jax.random.fold_in(own, 3), count)
    source_of, sink = mixed[0:count // 2 * 2:2], mixed[1:count // 2 * 2:2]
    room = jnp.minimum(tallies[source_of] - 1, most - tallies[sink]) // 2
    room = jnp.where((source_of == order[0]) | (sink == order[0]) | (tallies[sink] == 0), 0, jnp.maximum(room, 0))
    shifted = jax.random.randint(jax.random.fold_in(own, 4), (count // 2,), 0, 1 << 20) % (room + 1)
    tallies = tallies.at[source_of].add(-shifted).at[sink].add(shifted)
    items = jnp.searchsorted(jnp.cumsum(tallies), jnp.arange(rows * top), side="right").astype(jnp.int32)
    listing = items.reshape(top, rows).T
    listing = listing[jax.random.permutation(jax.random.fold_in(own, 1), rows)]
    offset_by = jax.random.randint(jax.random.fold_in(own, 2), (rows, 1), 0, top)
    return jnp.take_along_axis(listing, (jnp.arange(top)[None, :] + offset_by) % top, axis=1)


def load_shares(count, total, bound, lean, full):
    loads = [(1 << 20) // math.isqrt(standing ** lean) + 1 for standing in range(1, count + 1)]
    largest = bound if full else min(bound, max(-(-total // count), total * loads[0] // sum(loads)))
    least = 1 if total - largest >= count - 1 else 0
    holding, surplus = [largest] + [least] * (count - 1), total - largest - least * (count - 1)
    while surplus > 0:
        candidates = [i for i in range(1, count) if holding[i] < largest] or [i for i in range(1, count) if holding[i] < bound]
        pool, remaining = sum([loads[i] for i in candidates]), surplus
        for i in candidates:
            more = min(bound - holding[i], max(1, remaining * loads[i] // pool), surplus)
            holding[i] = holding[i] + more
            surplus = surplus - more
    return np.array(holding)


def gaussian(key, shape, deviation, most, shards=(), held_as=jnp.bfloat16):
    entries = deviation * jax.random.normal(key, shape, jnp.float32)
    if shards:
        entries = entries * shard_levels(key, shape, shards, -0.22, 0.18)
    return jnp.clip(entries, -most, most).astype(held_as)


def setup_inputs(seed: int = 0) -> dict:
    key_of = jax.random.split(jax.random.key(seed), 8)
    tokens = gaussian(key_of[0], (TOKENS, D), 1.0, 6.0, ((0, 32),))
    cotangent = gaussian(key_of[1], (TOKENS, D), 0.05, 0.3125, ((0, 32),))
    route_ids_keys = jax.random.split(jax.random.fold_in(key_of[2], 1), TOKENS // TOK_DEV)
    route_ids_turns = jax.random.permutation(jax.random.fold_in(key_of[2], 3), TOKENS // TOK_DEV)
    route_ids = jax.vmap(lambda own, number: assign_block(jax.random.fold_in(key_of[2], 2), own, number, TOK_DEV, EXPERTS, TOP, CAP, 2))(route_ids_keys, route_ids_turns).reshape((TOKENS, TOP))
    route_probs = jnp.clip(0.2 + 0.8 * jax.random.uniform(key_of[3], (TOKENS, TOP), jnp.float32) ** shard_levels(key_of[3], (TOKENS, TOP), ((0, 32),), -0.2, 0.2), 0.2, 1.0)
    gate_weight = gaussian(key_of[4], (D, HID), D ** -0.5, 0.109375, ((1, 8),))
    up_weight = gaussian(key_of[5], (D, HID), D ** -0.5, 0.109375, ((1, 8),))
    down_weight = gaussian(key_of[6], (HID, D), HID ** -0.5, 0.0625, ((0, 8),))
    return dict(tokens=tokens, cotangent=cotangent, route_ids=route_ids, route_probs=route_probs, gate_weight=gate_weight, up_weight=up_weight, down_weight=down_weight)


def compact(block_tokens, block_cotan, block_ids, block_probs):
    hits = block_ids == 0
    chosen = jnp.any(hits, axis=1).astype(jnp.int32)
    share = jnp.sum(jnp.where(hits, block_probs, 0.0), axis=1).astype(jnp.float32)
    slots = (jnp.cumsum(chosen) - chosen).astype(jnp.int32)
    placer = ((slots[:, None] == jnp.arange(CAP, dtype=jnp.int32)[None, :]) & (chosen[:, None] == 1)).astype(jnp.float32)
    rows = jnp.dot(placer.T, block_tokens.astype(jnp.float32), precision=lax.Precision.HIGHEST).astype(jnp.bfloat16)
    cotan_rows = jnp.dot(placer.T, block_cotan.astype(jnp.float32), precision=lax.Precision.HIGHEST).astype(jnp.bfloat16)
    shares = jnp.sum(placer * share[:, None], axis=0)
    return rows, cotan_rows, shares, placer


def rounded(value):
    return lax.optimization_barrier(value.astype(jnp.bfloat16)).astype(jnp.float32)


def reference(tokens, cotangent, route_ids, route_probs, gate_weight, up_weight, down_weight):
    width = tokens.shape[1]
    grid_tokens = tokens.reshape(N_DP, N_EXPERT, TOK_DEV, width)
    grid_cotan = cotangent.reshape(N_DP, N_EXPERT, TOK_DEV, width)
    grid_ids = route_ids.reshape(N_DP, N_EXPERT, TOK_DEV, TOP)
    grid_probs = route_probs.reshape(N_DP, N_EXPERT, TOK_DEV, TOP)
    rows, cotan_rows, shares, placer = jax.vmap(jax.vmap(compact))(grid_tokens, grid_cotan, grid_ids, grid_probs)
    total_rows = N_EXPERT * CAP
    rows = rows.reshape(N_DP, total_rows, width)
    cotan_rows = cotan_rows.reshape(N_DP, total_rows, width)
    shares = shares.reshape(N_DP, total_rows)
    slice_gate = gate_weight.reshape(width, N_EXPERT, HID_DEV).transpose(1, 0, 2)
    slice_up = up_weight.reshape(width, N_EXPERT, HID_DEV).transpose(1, 0, 2)

    def row_pass(carry, inputs):
        gate_sum, up_sum, down_sum = carry
        row_block, cotan_block, share_block = inputs
        gate_pre = jnp.dot(row_block, gate_weight, preferred_element_type=jnp.float32)
        up_pre = jnp.dot(row_block, up_weight, preferred_element_type=jnp.float32)
        sigma = jax.nn.sigmoid(gate_pre)
        gate_act = gate_pre * sigma
        hidden = (gate_act * up_pre).astype(jnp.bfloat16)
        scaled = (share_block[:, None] * cotan_block.astype(jnp.float32)).astype(jnp.bfloat16)
        down_part = jnp.dot(hidden.T, scaled, preferred_element_type=jnp.float32)
        hidden_back = jnp.dot(scaled, down_weight.T, preferred_element_type=jnp.float32)
        gate_back = (hidden_back * up_pre * sigma * (1.0 + gate_pre * (1.0 - sigma))).astype(jnp.bfloat16)
        up_back = (hidden_back * gate_act).astype(jnp.bfloat16)
        gate_part = jnp.dot(row_block.T, gate_back, preferred_element_type=jnp.float32)
        up_part = jnp.dot(row_block.T, up_back, preferred_element_type=jnp.float32)
        gate_slices = gate_back.reshape(total_rows, N_EXPERT, HID_DEV).transpose(1, 0, 2)
        up_slices = up_back.reshape(total_rows, N_EXPERT, HID_DEV).transpose(1, 0, 2)

        def slice_term(total, pieces):
            gate_piece, up_piece, gate_cols, up_cols = pieces
            term = jnp.dot(gate_piece, gate_cols.T, preferred_element_type=jnp.float32)
            term = term + jnp.dot(up_piece, up_cols.T, preferred_element_type=jnp.float32)
            return total + rounded(term), None

        start = jnp.zeros((total_rows, width), jnp.float32)
        back_rows, _ = lax.scan(slice_term, start, (gate_slices, up_slices, slice_gate, slice_up))
        carry = (gate_sum + rounded(gate_part), up_sum + rounded(up_part), down_sum + rounded(down_part))
        return carry, back_rows

    empty_in = jnp.zeros((width, HID), jnp.float32)
    empty_down = jnp.zeros((HID, width), jnp.float32)
    sums, back_all = lax.scan(row_pass, (empty_in, empty_in, empty_down), (rows, cotan_rows, shares))
    back_all = back_all.reshape(N_DP, N_EXPERT, CAP, width)
    placed = jnp.einsum("abtc,abcd->abtd", placer, back_all, precision=lax.Precision.HIGHEST)
    token_grad = placed.reshape(TOKENS, width).astype(jnp.bfloat16)
    return token_grad, sums[0].astype(jnp.bfloat16), sums[1].astype(jnp.bfloat16), sums[2].astype(jnp.bfloat16)
```

```python
import functools

import jax
import jax.numpy as jnp
from jax import lax
from jax.experimental import pallas as pl
from jax.experimental.pallas import tpu as pltpu
from jax.sharding import PartitionSpec as P

CAP = 36
MAIN = 32
REST = CAP - MAIN
HALF = jnp.bfloat16
FULL = jnp.float32


def shape(dims, dtype=HALF):
    return jax.ShapeDtypeStruct(dims, dtype)


def params(mib):
    return pltpu.CompilerParams(vmem_limit_bytes=mib * 2**20)


def nt_dot(a, b):
    return lax.dot_general(a, b, (((1,), (1,)), ((), ())), preferred_element_type=FULL)


def tn_dot(a, b):
    return lax.dot_general(a, b, (((0,), (0,)), ((), ())), preferred_element_type=FULL)


def chosen_slots(ids):
    count = ids.shape[0]
    chosen = jnp.max((ids == 0).astype(FULL), axis=1, keepdims=True)
    chosen = jnp.broadcast_to(chosen, (count, 128))
    earlier = lax.broadcasted_iota(jnp.int32, (count, count), 1) < lax.broadcasted_iota(
        jnp.int32, (count, count), 0
    )
    slots = jnp.dot(
        earlier.astype(FULL).astype(HALF), chosen.astype(HALF), preferred_element_type=FULL
    )
    return chosen, slots


def pack_kernel(ids, probs, tokens, cotangent, out, pick_rows, pick_cotan, share):
    @pl.when(pl.program_id(0) == 0)
    def _():
        chosen, slots = chosen_slots(ids[...])
        column = lax.broadcasted_iota(jnp.int32, slots.shape, 1).astype(FULL)
        late = (slots >= MAIN).astype(FULL)
        row_place = slots + late * MAIN
        cotan_place = slots + MAIN + late * REST
        pick_rows[...] = jnp.where(row_place == column, chosen, 0.0).astype(HALF)
        pick_cotan[...] = jnp.where(cotan_place == column, chosen, 0.0).astype(HALF)
        total = jnp.sum(jnp.where(ids[...] == 0, probs[...], 0.0), axis=1, keepdims=True)
        share[...] = jnp.broadcast_to(total, share.shape)

    scaled = (share[:, 0:1] * cotangent[...].astype(FULL)).astype(HALF)
    packed = tn_dot(pick_rows[...], tokens[...]) + tn_dot(pick_cotan[...], scaled)
    out[...] = packed[0 : 2 * CAP].astype(HALF)


def pack(ids, probs, tokens, cotangent):
    count, width = tokens.shape
    step = 768
    return pl.pallas_call(
        pack_kernel,
        grid=(width // step,),
        in_specs=[
            pl.BlockSpec(ids.shape, lambda j: (0, 0)),
            pl.BlockSpec(probs.shape, lambda j: (0, 0)),
            pl.BlockSpec((count, step), lambda j: (0, j)),
            pl.BlockSpec((count, step), lambda j: (0, j)),
        ],
        out_specs=pl.BlockSpec((2 * CAP, step), lambda j: (0, j)),
        out_shape=shape((2 * CAP, width)),
        scratch_shapes=[
            pltpu.VMEM((count, 128), HALF),
            pltpu.VMEM((count, 128), HALF),
            pltpu.VMEM((count, 128), FULL),
        ],
        compiler_params=params(32),
        name="pack",
    )(ids, probs, tokens, cotangent)


def unpack_kernel(ids, *refs):
    pieces, out = refs[:-1], refs[-1]
    chosen, slots = chosen_slots(ids[...])
    column = lax.broadcasted_iota(jnp.int32, slots.shape, 1).astype(FULL)
    depth = pieces[0].shape[0]
    place = jnp.where(slots == column, chosen, 0.0).astype(HALF)[:, 0:depth]
    total = pieces[0][...].astype(FULL)
    for piece in pieces[1:]:
        total = total + piece[...].astype(FULL)
    out[...] = jnp.dot(place, total.astype(HALF), preferred_element_type=FULL).astype(HALF)


def unpack(ids, pieces):
    count, (depth, width) = ids.shape[0], pieces[0].shape
    step = 1024
    return pl.pallas_call(
        unpack_kernel,
        grid=(width // step,),
        in_specs=[pl.BlockSpec(ids.shape, lambda j: (0, 0))]
        + [pl.BlockSpec((depth, step), lambda j: (0, j)) for _ in pieces],
        out_specs=pl.BlockSpec((count, step), lambda j: (0, j)),
        out_shape=shape((count, width)),
        compiler_params=params(32),
        name="unpack",
    )(ids, *pieces)


TILE = 256


def forward_kernel(n, back, place, *refs):
    blocks, (gate, up, down), refs = refs[:n], refs[n : n + 3], refs[n + 3 :]
    if back:
        acts, own, other, send, keep, rows, scaled, total = refs
    else:
        acts, own, other, rows, scaled = refs
    step = pl.program_id(0)
    width = rows.shape[1]
    part = own.shape[1] // 2

    @pl.when(step == 0)
    def _():
        for i, block in enumerate(blocks):
            rows[MAIN * i : MAIN * (i + 1), :] = block[0:MAIN, :]
            scaled[MAIN * i : MAIN * (i + 1), :] = block[MAIN : 2 * MAIN, :]
        first = lax.broadcasted_iota(jnp.int32, (2 * REST, width), 0) < REST
        tails = [block[2 * MAIN : 2 * CAP, :].astype(FULL) for block in blocks]
        row_tails, scaled_tails = [], []
        for a, b in zip(tails[0::2], tails[1::2]):
            row_tails.append(jnp.where(first, a, pltpu.roll(b, REST, 0)))
            scaled_tails.append(jnp.where(first, pltpu.roll(a, REST, 0), b))
        for i in range(0, n // 2, 2):
            here = slice(MAIN * n + 8 * i, MAIN * n + 8 * i + 16)
            rows[here, :] = jnp.concatenate(row_tails[i : i + 2], axis=0).astype(HALF)
            scaled[here, :] = jnp.concatenate(scaled_tails[i : i + 2], axis=0).astype(HALF)
        for out, index in ((own, 0), (other, 1)):
            columns = pl.ds(pl.multiple_of(place[index] * part, part), part)
            out[:, 0:part] = rows[:, columns]
            out[:, part : 2 * part] = scaled[:, columns]

    gate_pre = jnp.dot(rows[...], gate[...], preferred_element_type=FULL)
    up_pre = jnp.dot(rows[...], up[...], preferred_element_type=FULL)
    hidden_back = nt_dot(scaled[...], down[...])
    sigma = jax.nn.sigmoid(gate_pre)
    gate_act = gate_pre * sigma
    hidden = (gate_act * up_pre).astype(HALF)
    gate_back = (hidden_back * up_pre * sigma * (1.0 + gate_pre * (1.0 - sigma))).astype(HALF)
    up_back = (hidden_back * gate_act).astype(HALF)
    acts[:, 0:TILE] = hidden
    acts[:, TILE : 2 * TILE] = gate_back
    acts[:, 2 * TILE : 3 * TILE] = up_back
    if back:
        term = nt_dot(gate_back, gate[...]) + nt_dot(up_back, up[...])

        @pl.when(step == 0)
        def _():
            total[...] = term

        @pl.when(step > 0)
        def _():
            total[...] += term

        @pl.when(step == pl.num_programs(0) - 1)
        def _():
            mid, tail, half = MAIN * n // 2, MAIN * n, REST * n // 2
            keep[0:mid, :] = total[0:mid, :].astype(HALF)
            send[0:mid, :] = total[mid : 2 * mid, :].astype(HALF)
            keep[mid : mid + half, :] = total[tail : tail + half, :].astype(HALF)
            send[mid : mid + half, :] = total[tail + half : tail + 2 * half, :].astype(HALF)


def forward(blocks, gate, up, down, place, part, back):
    n, (width, hidden) = len(blocks), gate.shape
    count = CAP * n
    whole = lambda j, place: (0, 0)
    out_shape = [
        shape((count, 3 * hidden)),
        shape((count, 2 * part)),
        shape((count, 2 * part)),
    ]
    out_specs = [
        pl.BlockSpec((count, 3 * TILE), lambda j, place: (0, j)),
        pl.BlockSpec((count, 2 * part), whole),
        pl.BlockSpec((count, 2 * part), whole),
    ]
    scratch = [pltpu.VMEM((count, width), HALF), pltpu.VMEM((count, width), HALF)]
    if back:
        out_shape += [shape((count // 2, width))] * 2
        out_specs += [pl.BlockSpec((count // 2, width), whole)] * 2
        scratch += [pltpu.VMEM((count, width), FULL)]
    matmuls = 5 if back else 3
    return pl.pallas_call(
        functools.partial(forward_kernel, n, back),
        grid_spec=pltpu.PrefetchScalarGridSpec(
            num_scalar_prefetch=1,
            grid=(hidden // TILE,),
            in_specs=[pl.BlockSpec((2 * CAP, width), whole) for _ in blocks]
            + [
                pl.BlockSpec((width, TILE), lambda j, place: (0, j)),
                pl.BlockSpec((width, TILE), lambda j, place: (0, j)),
                pl.BlockSpec((TILE, width), lambda j, place: (j, 0)),
            ],
            out_specs=out_specs,
            scratch_shapes=scratch,
        ),
        out_shape=out_shape,
        compiler_params=params(56),
        cost_estimate=pl.CostEstimate(
            flops=2 * matmuls * count * width * hidden,
            bytes_accessed=6 * width * hidden + 4 * count * (width + part),
            transcendentals=count * hidden,
        ),
        name="forward_back" if back else "forward",
    )(place, *blocks, gate, up, down)


def grads_kernel(n, *refs):
    acts, parts, refs = refs[:n], refs[n : 2 * n], refs[2 * n :]
    gate_grad, up_grad, down_grad, act_rows, part_rows, done = refs
    copies, start = [], 0
    for i in range(n):
        count = acts[i].shape[0]
        for ref, buffer in ((acts[i], act_rows), (parts[i], part_rows)):
            copy = pltpu.make_async_copy(
                ref, buffer.at[pl.ds(start, count), :], done.at[len(copies)]
            )
            copy.start()
            copies.append(copy)
        start += count
    for copy in copies:
        copy.wait()
    part = part_rows.shape[1] // 2
    tiles = act_rows.shape[1] // (3 * TILE)
    for i in range(part // TILE):
        picked = part_rows[:, i * TILE : (i + 1) * TILE].T
        here = slice(i * TILE, (i + 1) * TILE)
        for j in range(tiles):
            at = 3 * TILE * j
            there = slice(j * TILE, (j + 1) * TILE)
            gate_grad[here, there] = jnp.dot(
                picked, act_rows[:, at + TILE : at + 2 * TILE], preferred_element_type=FULL
            ).astype(HALF)
            up_grad[here, there] = jnp.dot(
                picked, act_rows[:, at + 2 * TILE : at + 3 * TILE], preferred_element_type=FULL
            ).astype(HALF)
    for j in range(tiles):
        at = 3 * TILE * j
        hidden = act_rows[:, at : at + TILE].T
        down_grad[j * TILE : (j + 1) * TILE, :] = jnp.dot(
            hidden, part_rows[:, part : 2 * part], preferred_element_type=FULL
        ).astype(HALF)


def grads(acts, parts, part, hidden):
    n, count = len(acts), sum(a.shape[0] for a in acts)
    anywhere = pl.BlockSpec(memory_space=pl.ANY)
    in_vmem = pl.BlockSpec(memory_space=pltpu.VMEM)
    return pl.pallas_call(
        functools.partial(grads_kernel, n),
        in_specs=[anywhere] * (2 * n),
        out_specs=[in_vmem] * 3,
        out_shape=[shape((part, hidden)), shape((part, hidden)), shape((hidden, part))],
        scratch_shapes=[
            pltpu.VMEM((count, 3 * hidden), HALF),
            pltpu.VMEM((count, 2 * part), HALF),
            pltpu.SemaphoreType.DMA((2 * n,)),
        ],
        compiler_params=params(56),
        cost_estimate=pl.CostEstimate(
            flops=6 * count * part * hidden,
            bytes_accessed=2 * count * (3 * hidden + 2 * part) + 6 * part * hidden,
            transcendentals=0,
        ),
        name="grads",
    )(*acts, *parts)


def merge_kernel(keep, came, *outs):
    total = keep[...].astype(FULL) + came[...].astype(FULL)
    mid = MAIN * len(outs)
    for i, out in enumerate(outs):
        out[0:MAIN, :] = total[MAIN * i : MAIN * (i + 1)].astype(HALF)
        pair = total[mid + 8 * (i // 2) : mid + 8 * (i // 2) + 8]
        out[MAIN : MAIN + 8, :] = (pair if i % 2 == 0 else pltpu.roll(pair, REST, 0)).astype(HALF)


def merge(keep, came):
    n, width = keep.shape[0] // CAP, keep.shape[1]
    return pl.pallas_call(
        merge_kernel,
        out_shape=[shape((MAIN + 8, width))] * n,
        compiler_params=params(32),
        name="merge",
    )(keep, came)


def per_device(tokens, cotangent, route_ids, route_probs, gate_weight, up_weight, down_weight):
    n_dp, n_expert = lax.axis_size("dp"), lax.axis_size("expert")
    core_pairs = [(i, i ^ 1) for i in range(n_dp)]
    y_pairs = [(i, (i + 2) % n_dp) for i in range(n_dp)]
    x_pairs = [(i, i ^ 1) for i in range(n_expert)]

    def over_core(v):
        return lax.ppermute(v, "dp", core_pairs)

    def over_y(v):
        return lax.ppermute(v, "dp", y_pairs)

    def over_x(v):
        return lax.ppermute(v, "expert", x_pairs)

    def over_z(v, by):
        return lax.ppermute(
            v, "expert", [(i, (i + 2 * by) % n_expert) for i in range(n_expert)]
        )

    part = tokens.shape[1] // n_dp
    p = lax.axis_index("dp")
    place = jnp.stack([p, p + 1 - 2 * (p % 2)]).astype(jnp.int32)

    block = pack(route_ids, route_probs, tokens, cotangent)
    mine = [block, over_z(block, 1), over_z(block, -1), over_z(block, 2)]
    beside = [over_x(b) for b in mine]
    far_mine = [over_y(b) for b in mine]
    far_beside = [over_x(far_mine[0])] + [over_y(b) for b in beside[1:]]

    weights = (gate_weight, up_weight, down_weight)
    run = functools.partial(forward, gate=gate_weight, up=up_weight, down=down_weight, place=place, part=part)
    results, pieces = [], []
    for lo in (0, 2):
        out = run(mine[lo : lo + 2] + beside[lo : lo + 2], back=True)
        results.append(out[:3])
        pieces += merge(out[4], over_x(out[3]))
    results.append(run(far_mine + far_beside, back=False))
    returned = [pieces[0], over_z(pieces[1], -1), over_z(pieces[2], 1), over_z(pieces[3], 2)]

    acts, parts = [], []
    for act, own, other in results:
        acts += [act, over_core(act)]
        parts += [own, over_core(other)]
    gate_grad, up_grad, down_grad = grads(acts, parts, part, gate_weight.shape[1])
    return unpack(route_ids, returned), gate_grad, up_grad, down_grad


def pick_rows(placer, values):
    return lax.dot_general(
        placer, values, (((0,), (0,)), ((), ())), preferred_element_type=jnp.float32
    ).astype(jnp.bfloat16)


def per_device_general(tokens, cotangent, route_ids, route_probs, gate_weight, up_weight, down_weight):
    hits = route_ids == 0
    chosen = jnp.any(hits, axis=1).astype(jnp.int32)
    share = jnp.sum(jnp.where(hits, route_probs, 0.0), axis=1)
    slots = jnp.cumsum(chosen) - chosen
    placer_mask = (slots[:, None] == jnp.arange(CAP, dtype=jnp.int32)[None, :]) & (
        chosen[:, None] == 1
    )
    placer = placer_mask.astype(jnp.float32)
    placer_half = placer_mask.astype(jnp.bfloat16)
    local_rows = pick_rows(placer_half, tokens)
    local_cotan = pick_rows(placer_half, cotangent)
    local_shares = jnp.sum(placer * share[:, None], axis=0)
    routed, routed_cotan, routed_shares = (
        lax.all_gather(local_rows, "expert", axis=0, tiled=True),
        lax.all_gather(local_cotan, "expert", axis=0, tiled=True),
        lax.all_gather(local_shares.astype(jnp.bfloat16), "expert", axis=0, tiled=True).astype(
            local_shares.dtype
        ),
    )
    gate_pre = jnp.dot(routed, gate_weight, preferred_element_type=jnp.float32)
    up_pre = jnp.dot(routed, up_weight, preferred_element_type=jnp.float32)
    sigma = jax.nn.sigmoid(gate_pre)
    gate_act = gate_pre * sigma
    hidden = (gate_act * up_pre).astype(jnp.bfloat16)
    gate_pre, up_pre, sigma, gate_act, hidden = (gate_pre, up_pre, sigma, gate_act, hidden)
    scaled = (routed_shares[:, None] * routed_cotan.astype(jnp.float32)).astype(jnp.bfloat16)
    down_part = lax.dot_general(
        hidden, scaled, (((0,), (0,)), ((), ())), preferred_element_type=jnp.float32
    )
    hidden_back = lax.dot_general(
        scaled, down_weight, (((1,), (1,)), ((), ())), preferred_element_type=jnp.float32
    )
    gate_back = (hidden_back * up_pre * sigma * (1.0 + gate_pre * (1.0 - sigma))).astype(
        jnp.bfloat16
    )
    up_back = (hidden_back * gate_act).astype(jnp.bfloat16)
    gate_part = lax.dot_general(
        routed, gate_back, (((0,), (0,)), ((), ())), preferred_element_type=jnp.float32
    )
    up_part = lax.dot_general(
        routed, up_back, (((0,), (0,)), ((), ())), preferred_element_type=jnp.float32
    )
    gate_sum, up_sum, down_sum = (
        lax.psum_scatter(
            gate_part.astype(jnp.bfloat16), "dp", scatter_dimension=0, tiled=True
        ).astype(jnp.float32),
        lax.psum_scatter(
            up_part.astype(jnp.bfloat16), "dp", scatter_dimension=0, tiled=True
        ).astype(jnp.float32),
        lax.psum_scatter(
            down_part.astype(jnp.bfloat16), "dp", scatter_dimension=1, tiled=True
        ).astype(jnp.float32),
    )
    partial_value = lax.dot_general(
        gate_back, gate_weight, (((1,), (1,)), ((), ())), preferred_element_type=jnp.float32
    )
    partial_value = partial_value + lax.dot_general(
        up_back, up_weight, (((1,), (1,)), ((), ())), preferred_element_type=jnp.float32
    )
    returned = lax.psum_scatter(
        partial_value.astype(jnp.bfloat16), "expert", scatter_dimension=0, tiled=True
    ).astype(jnp.float32)
    token_grad = jnp.dot(placer, returned, precision=lax.Precision.HIGHEST).astype(jnp.bfloat16)
    return (
        token_grad,
        gate_sum.astype(jnp.bfloat16),
        up_sum.astype(jnp.bfloat16),
        down_sum.astype(jnp.bfloat16),
    )


def solution(mesh):
    in_specs = (
        P(("dp", "expert"), None),
        P(("dp", "expert"), None),
        P(("dp", "expert"), None),
        P(("dp", "expert"), None),
        P(None, "expert"),
        P(None, "expert"),
        P("expert", None),
    )
    out_specs = (P(("dp", "expert"), None), P("dp", "expert"), P("dp", "expert"), P("expert", "dp"))
    fast = mesh.shape["dp"] == 4 and mesh.shape["expert"] == 8
    body = per_device if fast else per_device_general
    return jax.shard_map(
        body, mesh=mesh, in_specs=in_specs, out_specs=out_specs, check_vma=False
    )
```

```python
import functools

import jax
import jax.numpy as jnp
from jax import lax
from jax.experimental import pallas as pl
from jax.experimental.pallas import tpu as pltpu
from jax.sharding import PartitionSpec as P

CAP = 36
MAIN = 32
REST = CAP - MAIN
HALF = jnp.bfloat16
FULL = jnp.float32


def shape(dims, dtype=HALF):
    return jax.ShapeDtypeStruct(dims, dtype)


def params(mib):
    return pltpu.CompilerParams(vmem_limit_bytes=mib * 2**20)


def nt_dot(a, b):
    return lax.dot_general(a, b, (((1,), (1,)), ((), ())), preferred_element_type=FULL)


def tn_dot(a, b):
    return lax.dot_general(a, b, (((0,), (0,)), ((), ())), preferred_element_type=FULL)


def earlier_count(ids):
    count = ids.shape[1]
    chosen = jnp.max((ids == 0).astype(FULL), axis=0, keepdims=True)
    chosen = jnp.broadcast_to(chosen, (8, count))
    before = lax.broadcasted_iota(jnp.int32, (count, count), 0) < lax.broadcasted_iota(
        jnp.int32, (count, count), 1
    )
    slots = jnp.dot(
        chosen.astype(HALF), before.astype(FULL).astype(HALF), preferred_element_type=FULL
    )
    return chosen, slots


def one_hot(places, chosen, count):
    row = lax.broadcasted_iota(jnp.int32, (count, places.shape[1]), 0).astype(FULL)
    return jnp.where(row == places[0:1], jnp.broadcast_to(chosen[0:1], row.shape), 0.0)


def pack_kernel(ids, probs, tokens, cotangent, out, pick_rows, pick_cotan, share):
    @pl.when(pl.program_id(0) == 0)
    def _():
        chosen, slots = earlier_count(ids[...])
        late = (slots >= MAIN).astype(FULL)
        depth = pick_rows.shape[0]
        pick_rows[...] = one_hot(slots + late * MAIN, chosen, depth).astype(HALF)
        picked = one_hot(slots + MAIN + late * REST, chosen, depth)
        pick_cotan[...] = picked.astype(HALF)
        total = jnp.sum(jnp.where(ids[...] == 0, probs[...], 0.0), axis=0, keepdims=True)
        share[...] = jnp.broadcast_to(
            jnp.sum(picked * total, axis=1, keepdims=True), share.shape
        )

    cotan = jnp.dot(pick_cotan[...], cotangent[...], preferred_element_type=FULL)
    rows = jnp.dot(pick_rows[...], tokens[...], preferred_element_type=FULL)
    out[...] = (rows + share[:, 0:1] * cotan)[0 : 2 * CAP].astype(HALF)


def pack(ids, probs, tokens, cotangent):
    count, width = tokens.shape
    step = 1536
    return pl.pallas_call(
        pack_kernel,
        grid=(width // step,),
        in_specs=[
            pl.BlockSpec(ids.shape, lambda j: (0, 0)),
            pl.BlockSpec(probs.shape, lambda j: (0, 0)),
            pl.BlockSpec((count, step), lambda j: (0, j)),
            pl.BlockSpec((count, step), lambda j: (0, j)),
        ],
        out_specs=pl.BlockSpec((2 * CAP, step), lambda j: (0, j)),
        out_shape=shape((2 * CAP, width)),
        scratch_shapes=[
            pltpu.VMEM((80, count), HALF),
            pltpu.VMEM((80, count), HALF),
            pltpu.VMEM((80, 128), FULL),
        ],
        compiler_params=params(32),
        name="pack",
    )(ids, probs, tokens, cotangent)


def unpack_kernel(ids, *refs):
    pieces, out = refs[:-1], refs[-1]
    chosen, slots = earlier_count(ids[...])
    place = one_hot(slots, chosen, pieces[0].shape[0]).astype(HALF)
    total = pieces[0][...].astype(FULL)
    for piece in pieces[1:]:
        total = total + piece[...].astype(FULL)
    out[...] = tn_dot(place, total.astype(HALF)).astype(HALF)


def unpack(ids, pieces):
    count, (depth, width) = ids.shape[1], pieces[0].shape
    step = 1536
    return pl.pallas_call(
        unpack_kernel,
        grid=(width // step,),
        in_specs=[pl.BlockSpec(ids.shape, lambda j: (0, 0))]
        + [pl.BlockSpec((depth, step), lambda j: (0, j)) for _ in pieces],
        out_specs=pl.BlockSpec((count, step), lambda j: (0, j)),
        out_shape=shape((count, width)),
        compiler_params=params(32),
        name="unpack",
    )(ids, *pieces)


TILE = 256


def padded_rows(n):
    return MAIN * n + -(-REST * n // 16) * 16


def load_all(pairs, done):
    copies = [pltpu.make_async_copy(a, b, done.at[i]) for i, (a, b) in enumerate(pairs)]
    for copy in copies:
        copy.start()
    return copies


def weight_copies(weights, buffers):
    pairs = []
    for j in range(buffers[0].shape[1] // TILE):
        here = pl.ds(TILE * j, TILE)
        for k in range(2):
            pairs.append((weights[k].at[:, here], buffers[k].at[:, here]))
        pairs.append((weights[2].at[here, :], buffers[2].at[here, :]))
    return pairs


def assemble(blocks, rows, scaled):
    n, width = len(blocks), rows.shape[1]
    for i, block in enumerate(blocks):
        rows[MAIN * i : MAIN * (i + 1), :] = block[0:MAIN, :]
        scaled[MAIN * i : MAIN * (i + 1), :] = block[MAIN : 2 * MAIN, :]
    first = lax.broadcasted_iota(jnp.int32, (2 * REST, width), 0) < REST
    tails = [block[2 * MAIN : 2 * CAP, :].astype(FULL) for block in blocks]
    row_tails, scaled_tails = [], []
    for a, b in zip(tails[0::2], tails[1::2]):
        row_tails.append(jnp.where(first, a, pltpu.roll(b, REST, 0)))
        scaled_tails.append(jnp.where(first, pltpu.roll(a, REST, 0), b))
    if len(row_tails) % 2:
        row_tails.append(jnp.zeros((2 * REST, width), FULL))
        scaled_tails.append(jnp.zeros((2 * REST, width), FULL))
    for i in range(0, len(row_tails), 2):
        here = slice(MAIN * n + 8 * i, MAIN * n + 8 * i + 16)
        rows[here, :] = jnp.concatenate(row_tails[i : i + 2], axis=0).astype(HALF)
        scaled[here, :] = jnp.concatenate(scaled_tails[i : i + 2], axis=0).astype(HALF)


def activations(rows, scaled, gate, up, down):
    gate_pre = jnp.dot(rows, gate, preferred_element_type=FULL)
    up_pre = jnp.dot(rows, up, preferred_element_type=FULL)
    hidden_back = nt_dot(scaled, down)
    sigma = jax.nn.sigmoid(gate_pre)
    gate_act = gate_pre * sigma
    hidden = (gate_act * up_pre).astype(HALF)
    gate_back = (hidden_back * up_pre * sigma * (1.0 + gate_pre * (1.0 - sigma))).astype(HALF)
    up_back = (hidden_back * gate_act).astype(HALF)
    return hidden, gate_back, up_back


def forward_kernel(n, back, place, *refs):
    blocks, weights, refs = refs[:n], refs[n : n + 3], refs[n + 3 :]
    acts, own, other = refs[:3]
    refs = refs[3:]
    if back:
        send, keep = refs[:2]
        refs = refs[2:]
    rows, scaled, held, gate, up, down, block_done, weight_done = refs
    width, part = rows.shape[1], own.shape[1] // 2
    block_copies = load_all([(blocks[i], held.at[i]) for i in range(n)], block_done)
    copies = load_all(weight_copies(weights, (gate, up, down)), weight_done)
    for copy in block_copies:
        copy.wait()
    assemble([held.at[i] for i in range(n)], rows, scaled)
    for out, index in ((own, 0), (other, 1)):
        columns = pl.ds(pl.multiple_of(place[index] * part, part), part)
        out[:, 0:part] = rows[:, columns]
        out[:, part : 2 * part] = scaled[:, columns]
    tiles = gate.shape[1] // TILE
    for j in range(tiles):
        for copy in copies[3 * j : 3 * j + 3]:
            copy.wait()
        here = slice(TILE * j, TILE * (j + 1))
        found = activations(rows[...], scaled[...], gate[:, here], up[:, here], down[here, :])
        for k in range(3):
            at = TILE * (3 * j + k)
            acts[:, at : at + TILE] = found[k]
    if back:
        half = n // 2
        mid, tail, reach = MAIN * half, MAIN * n, 8 * (-(-half // 2))
        skip = 8 * half - reach
        gate_back = [acts[:, TILE * (3 * j + 1) : TILE * (3 * j + 2)] for j in range(tiles)]
        up_back = [acts[:, TILE * (3 * j + 2) : TILE * (3 * j + 3)] for j in range(tiles)]
        gate_back, up_back = jnp.concatenate(gate_back, axis=1), jnp.concatenate(up_back, axis=1)
        for i in range(0, width, 2 * TILE):
            here = slice(i, i + 2 * TILE)
            total = nt_dot(gate_back, gate[here, :]) + nt_dot(up_back, up[here, :])
            keep[0:mid, here] = total[0:mid].astype(HALF)
            send[0:mid, here] = total[mid : 2 * mid].astype(HALF)
            keep[mid : mid + reach, here] = total[tail : tail + reach].astype(HALF)
            send[mid : mid + reach, here] = total[tail + skip : tail + skip + reach].astype(HALF)


def forward(blocks, gate, up, down, place, part, back):
    n, (width, hidden) = len(blocks), gate.shape
    count = padded_rows(n)
    anywhere = pl.BlockSpec(memory_space=pl.ANY)
    in_vmem = pl.BlockSpec(memory_space=pltpu.VMEM)
    out_shape = [
        shape((count, 3 * hidden)),
        shape((count, 2 * part)),
        shape((count, 2 * part)),
    ]
    if back:
        half = n // 2
        out_shape += [shape((MAIN * half + 8 * (-(-half // 2)), width))] * 2
    matmuls = 5 if back else 3
    return pl.pallas_call(
        functools.partial(forward_kernel, n, back),
        in_specs=[pl.BlockSpec(memory_space=pltpu.SMEM)] + [anywhere] * (n + 3),
        out_specs=[in_vmem] * len(out_shape),
        out_shape=out_shape,
        scratch_shapes=[
            pltpu.VMEM((count, width), HALF),
            pltpu.VMEM((count, width), HALF),
            pltpu.VMEM((n, 2 * CAP, width), HALF),
            pltpu.VMEM((width, hidden), HALF),
            pltpu.VMEM((width, hidden), HALF),
            pltpu.VMEM((hidden, width), HALF),
            pltpu.SemaphoreType.DMA((n,)),
            pltpu.SemaphoreType.DMA((3 * hidden // TILE,)),
        ],
        compiler_params=params(56),
        cost_estimate=pl.CostEstimate(
            flops=2 * matmuls * count * width * hidden,
            bytes_accessed=6 * width * hidden + 4 * count * (width + part),
            transcendentals=count * hidden,
        ),
        name="forward_back" if back else "forward",
    )(place, *blocks, gate, up, down)


def grads_kernel(n, *refs):
    acts, parts, refs = refs[:n], refs[n : 2 * n], refs[2 * n :]
    gate_grad, up_grad, down_grad, act_rows, part_rows, done = refs
    pairs, start = [], 0
    for i in range(n):
        here = pl.ds(start, acts[i].shape[0])
        pairs.append((acts[i], act_rows.at[here, :]))
        pairs.append((parts[i], part_rows.at[here, :]))
        start += acts[i].shape[0]
    for copy in load_all(pairs, done):
        copy.wait()
    part = part_rows.shape[1] // 2
    tiles = act_rows.shape[1] // (3 * TILE)
    for i in range(part // TILE):
        picked = part_rows[:, i * TILE : (i + 1) * TILE].T
        here = slice(i * TILE, (i + 1) * TILE)
        for j in range(tiles):
            at = 3 * TILE * j
            there = slice(j * TILE, (j + 1) * TILE)
            gate_grad[here, there] = jnp.dot(
                picked, act_rows[:, at + TILE : at + 2 * TILE], preferred_element_type=FULL
            ).astype(HALF)
            up_grad[here, there] = jnp.dot(
                picked, act_rows[:, at + 2 * TILE : at + 3 * TILE], preferred_element_type=FULL
            ).astype(HALF)
    for j in range(tiles):
        at = 3 * TILE * j
        hidden = act_rows[:, at : at + TILE].T
        down_grad[j * TILE : (j + 1) * TILE, :] = jnp.dot(
            hidden, part_rows[:, part : 2 * part], preferred_element_type=FULL
        ).astype(HALF)


def grads(acts, parts, part, hidden):
    n, count = len(acts), sum(a.shape[0] for a in acts)
    anywhere = pl.BlockSpec(memory_space=pl.ANY)
    in_vmem = pl.BlockSpec(memory_space=pltpu.VMEM)
    return pl.pallas_call(
        functools.partial(grads_kernel, n),
        in_specs=[anywhere] * (2 * n),
        out_specs=[in_vmem] * 3,
        out_shape=[shape((part, hidden)), shape((part, hidden)), shape((hidden, part))],
        scratch_shapes=[
            pltpu.VMEM((count, 3 * hidden), HALF),
            pltpu.VMEM((count, 2 * part), HALF),
            pltpu.SemaphoreType.DMA((2 * n,)),
        ],
        compiler_params=params(56),
        cost_estimate=pl.CostEstimate(
            flops=6 * count * part * hidden,
            bytes_accessed=2 * count * (3 * hidden + 2 * part) + 6 * part * hidden,
            transcendentals=0,
        ),
        name="grads",
    )(*acts, *parts)


def finish_kernel(n, place, *refs):
    blocks, weights, early, refs = refs[:n], refs[n : n + 3], refs[n + 3 : n + 6], refs[n + 6 :]
    outs, refs = refs[:3], refs[3:]
    rows, scaled, held, gate, up, down = refs[:6]
    sums, block_done, weight_done, sum_done, out_done = refs[6:9], *refs[9:]
    part = outs[0].shape[0]
    block_copies = load_all([(blocks[i], held.at[i]) for i in range(n)], block_done)
    copies = load_all(weight_copies(weights, (gate, up, down)), weight_done)
    sum_copies = load_all([(early[k], sums[k]) for k in range(3)], sum_done)
    for copy in block_copies:
        copy.wait()
    assemble([held.at[i] for i in range(n)], rows, scaled)
    columns = pl.ds(pl.multiple_of(place[0] * part, part), part)
    picked, cotan = rows[:, columns].T, scaled[:, columns]
    out_copies = []
    for j in range(gate.shape[1] // TILE):
        for copy in copies[3 * j : 3 * j + 3]:
            copy.wait()
        here = slice(TILE * j, TILE * (j + 1))
        hidden, gate_back, up_back = activations(
            rows[...], scaled[...], gate[:, here], up[:, here], down[here, :]
        )
        if j == 0:
            for copy in sum_copies:
                copy.wait()
        sums[0][:, here] = (
            sums[0][:, here].astype(FULL)
            + jnp.dot(picked, gate_back, preferred_element_type=FULL)
        ).astype(HALF)
        sums[1][:, here] = (
            sums[1][:, here].astype(FULL) + jnp.dot(picked, up_back, preferred_element_type=FULL)
        ).astype(HALF)
        sums[2][here, :] = (
            sums[2][here, :].astype(FULL) + tn_dot(hidden, cotan)
        ).astype(HALF)
        there = pl.ds(TILE * j, TILE)
        views = [
            (sums[0].at[:, there], outs[0].at[:, there]),
            (sums[1].at[:, there], outs[1].at[:, there]),
            (sums[2].at[there, :], outs[2].at[there, :]),
        ]
        for source, target in views:
            copy = pltpu.make_async_copy(source, target, out_done.at[len(out_copies)])
            copy.start()
            out_copies.append(copy)
    for copy in out_copies:
        copy.wait()


def finish(blocks, gate, up, down, place, early):
    n, (width, hidden) = len(blocks), gate.shape
    count, part = padded_rows(n), early[0].shape[0]
    anywhere = pl.BlockSpec(memory_space=pl.ANY)
    return pl.pallas_call(
        functools.partial(finish_kernel, n),
        in_specs=[pl.BlockSpec(memory_space=pltpu.SMEM)] + [anywhere] * (n + 6),
        out_specs=[anywhere] * 3,
        out_shape=[shape(e.shape) for e in early],
        scratch_shapes=[
            pltpu.VMEM((count, width), HALF),
            pltpu.VMEM((count, width), HALF),
            pltpu.VMEM((n, 2 * CAP, width), HALF),
            pltpu.VMEM((width, hidden), HALF),
            pltpu.VMEM((width, hidden), HALF),
            pltpu.VMEM((hidden, width), HALF),
            *[pltpu.VMEM(e.shape, HALF) for e in early],
            pltpu.SemaphoreType.DMA((n,)),
            pltpu.SemaphoreType.DMA((3 * hidden // TILE,)),
            pltpu.SemaphoreType.DMA((3,)),
            pltpu.SemaphoreType.DMA((3 * hidden // TILE,)),
        ],
        compiler_params=params(56),
        cost_estimate=pl.CostEstimate(
            flops=6 * count * (width + part) * hidden,
            bytes_accessed=6 * width * hidden + 2 * n * CAP * width + 12 * part * hidden,
            transcendentals=count * hidden,
        ),
        name="finish",
    )(place, *blocks, gate, up, down, *early)


def merge_kernel(n, keep, came, *outs):
    mid = MAIN * n
    kept, other = keep[mid:, :].astype(FULL), came[mid:, :].astype(FULL)
    if n % 2:
        other = pltpu.roll(other, other.shape[0] - REST, 0)
    tails = kept + other
    for i, out in enumerate(outs):
        here = slice(MAIN * i, MAIN * (i + 1))
        out[0:MAIN, :] = (keep[here, :].astype(FULL) + came[here, :].astype(FULL)).astype(HALF)
        pair = tails[8 * (i // 2) : 8 * (i // 2) + 8]
        out[MAIN : MAIN + 8, :] = (pair if i % 2 == 0 else pltpu.roll(pair, REST, 0)).astype(HALF)


def merge(n, keep, came):
    return pl.pallas_call(
        functools.partial(merge_kernel, n),
        out_shape=[shape((MAIN + 8, keep.shape[1]))] * n,
        compiler_params=params(32),
        name="merge",
    )(keep, came)


def after(value, *others):
    return lax.optimization_barrier((value, *others))[0]


def per_device(tokens, cotangent, route_ids, route_probs, gate_weight, up_weight, down_weight):
    n_dp, n_expert = lax.axis_size("dp"), lax.axis_size("expert")
    core_pairs = [(i, i ^ 1) for i in range(n_dp)]
    y_pairs = [(i, (i + 2) % n_dp) for i in range(n_dp)]
    x_pairs = [(i, i ^ 1) for i in range(n_expert)]

    def over_core(v):
        return lax.ppermute(v, "dp", core_pairs)

    def over_y(v):
        return lax.ppermute(v, "dp", y_pairs)

    def over_x(v):
        return lax.ppermute(v, "expert", x_pairs)

    def over_z(v, by):
        return lax.ppermute(
            v, "expert", [(i, (i + 2 * by) % n_expert) for i in range(n_expert)]
        )

    part = tokens.shape[1] // n_dp
    p = lax.axis_index("dp")
    place = jnp.stack([p, p + 1 - 2 * (p % 2)]).astype(jnp.int32)
    ids, probs = route_ids.T, route_probs.T
    weights = dict(gate=gate_weight, up=up_weight, down=down_weight)

    b0 = pack(ids, probs, tokens, cotangent)
    z1 = over_z(b0, 1)
    x0, y0 = over_x(b0), over_y(b0)
    x1, y1 = over_x(z1), over_y(z1)
    z3 = over_z(after(b0, z1), -1)
    yx0 = over_x(y0)
    z2 = over_z(after(z1, z3), 1)
    x3, y3 = over_x(z3), over_y(z3)
    yx1 = over_y(x1)
    x2, y2 = over_x(z2), over_y(z2)
    yx3, yx2 = over_y(x3), over_y(x2)

    acts, parts = [], []

    def share(act, own, other):
        acts.extend([act, over_core(act)])
        parts.extend([own, over_core(other)])

    run = functools.partial(forward, place=place, part=part, **weights)
    *first, send, keep = run([b0, z1, z3, x0, x1, x3], back=True)
    pieces = merge(3, keep, over_x(send))
    share(*first)
    *second, send, keep = run([z2, x2], back=True)
    pieces += merge(1, keep, over_x(send))
    share(*second)
    returned = [pieces[0], over_z(pieces[1], -1), over_z(pieces[2], 1), over_z(pieces[3], 2)]
    share(*run([y0, yx0, y1, yx1], back=False))
    early = grads(acts, parts, part, gate_weight.shape[1])
    last = [y3, y2, yx3, yx2]
    last = last + [over_core(b) for b in last]
    gate_grad, up_grad, down_grad = finish(last, place=place, early=early, **weights)
    return unpack(ids, returned), gate_grad, up_grad, down_grad


def pick_rows(placer, values):
    return lax.dot_general(
        placer, values, (((0,), (0,)), ((), ())), preferred_element_type=jnp.float32
    ).astype(jnp.bfloat16)


def per_device_general(tokens, cotangent, route_ids, route_probs, gate_weight, up_weight, down_weight):
    hits = route_ids == 0
    chosen = jnp.any(hits, axis=1).astype(jnp.int32)
    share = jnp.sum(jnp.where(hits, route_probs, 0.0), axis=1)
    slots = jnp.cumsum(chosen) - chosen
    placer_mask = (slots[:, None] == jnp.arange(CAP, dtype=jnp.int32)[None, :]) & (
        chosen[:, None] == 1
    )
    placer = placer_mask.astype(jnp.float32)
    placer_half = placer_mask.astype(jnp.bfloat16)
    local_rows = pick_rows(placer_half, tokens)
    local_cotan = pick_rows(placer_half, cotangent)
    local_shares = jnp.sum(placer * share[:, None], axis=0)
    routed, routed_cotan, routed_shares = (
        lax.all_gather(local_rows, "expert", axis=0, tiled=True),
        lax.all_gather(local_cotan, "expert", axis=0, tiled=True),
        lax.all_gather(local_shares.astype(jnp.bfloat16), "expert", axis=0, tiled=True).astype(
            local_shares.dtype
        ),
    )
    gate_pre = jnp.dot(routed, gate_weight, preferred_element_type=jnp.float32)
    up_pre = jnp.dot(routed, up_weight, preferred_element_type=jnp.float32)
    sigma = jax.nn.sigmoid(gate_pre)
    gate_act = gate_pre * sigma
    hidden = (gate_act * up_pre).astype(jnp.bfloat16)
    gate_pre, up_pre, sigma, gate_act, hidden = (gate_pre, up_pre, sigma, gate_act, hidden)
    scaled = (routed_shares[:, None] * routed_cotan.astype(jnp.float32)).astype(jnp.bfloat16)
    down_part = lax.dot_general(
        hidden, scaled, (((0,), (0,)), ((), ())), preferred_element_type=jnp.float32
    )
    hidden_back = lax.dot_general(
        scaled, down_weight, (((1,), (1,)), ((), ())), preferred_element_type=jnp.float32
    )
    gate_back = (hidden_back * up_pre * sigma * (1.0 + gate_pre * (1.0 - sigma))).astype(
        jnp.bfloat16
    )
    up_back = (hidden_back * gate_act).astype(jnp.bfloat16)
    gate_part = lax.dot_general(
        routed, gate_back, (((0,), (0,)), ((), ())), preferred_element_type=jnp.float32
    )
    up_part = lax.dot_general(
        routed, up_back, (((0,), (0,)), ((), ())), preferred_element_type=jnp.float32
    )
    gate_sum, up_sum, down_sum = (
        lax.psum_scatter(
            gate_part.astype(jnp.bfloat16), "dp", scatter_dimension=0, tiled=True
        ).astype(jnp.float32),
        lax.psum_scatter(
            up_part.astype(jnp.bfloat16), "dp", scatter_dimension=0, tiled=True
        ).astype(jnp.float32),
        lax.psum_scatter(
            down_part.astype(jnp.bfloat16), "dp", scatter_dimension=1, tiled=True
        ).astype(jnp.float32),
    )
    partial_value = lax.dot_general(
        gate_back, gate_weight, (((1,), (1,)), ((), ())), preferred_element_type=jnp.float32
    )
    partial_value = partial_value + lax.dot_general(
        up_back, up_weight, (((1,), (1,)), ((), ())), preferred_element_type=jnp.float32
    )
    returned = lax.psum_scatter(
        partial_value.astype(jnp.bfloat16), "expert", scatter_dimension=0, tiled=True
    ).astype(jnp.float32)
    token_grad = jnp.dot(placer, returned, precision=lax.Precision.HIGHEST).astype(jnp.bfloat16)
    return (
        token_grad,
        gate_sum.astype(jnp.bfloat16),
        up_sum.astype(jnp.bfloat16),
        down_sum.astype(jnp.bfloat16),
    )


def solution(mesh):
    in_specs = (
        P(("dp", "expert"), None),
        P(("dp", "expert"), None),
        P(("dp", "expert"), None),
        P(("dp", "expert"), None),
        P(None, "expert"),
        P(None, "expert"),
        P("expert", None),
    )
    out_specs = (P(("dp", "expert"), None), P("dp", "expert"), P("dp", "expert"), P("expert", "dp"))
    fast = mesh.shape["dp"] == 4 and mesh.shape["expert"] == 8
    body = per_device if fast else per_device_general
    return jax.shard_map(
        body, mesh=mesh, in_specs=in_specs, out_specs=out_specs, check_vma=False
    )
```

```python
import functools

import jax
import jax.numpy as jnp
from jax import lax
from jax.experimental import pallas as pl
from jax.experimental.pallas import tpu as pltpu
from jax.sharding import PartitionSpec as P

CAP = 36
MAIN = 32
REST = CAP - MAIN
TILE = 256
LIMIT = 20
HALF = jnp.bfloat16
FULL = jnp.float32


def shape(dims, dtype=HALF):
    return jax.ShapeDtypeStruct(dims, dtype)


def params(mib):
    return pltpu.CompilerParams(vmem_limit_bytes=mib * 2**20)


def nt_dot(a, b):
    return lax.dot_general(a, b, (((1,), (1,)), ((), ())), preferred_element_type=FULL)


def tn_dot(a, b):
    return lax.dot_general(a, b, (((0,), (0,)), ((), ())), preferred_element_type=FULL)


def earlier_count(ids):
    count = ids.shape[1]
    chosen = jnp.max((ids == 0).astype(FULL), axis=0, keepdims=True)
    chosen = jnp.broadcast_to(chosen, (8, count))
    before = lax.broadcasted_iota(jnp.int32, (count, count), 0) < lax.broadcasted_iota(
        jnp.int32, (count, count), 1
    )
    slots = jnp.dot(
        chosen.astype(HALF), before.astype(FULL).astype(HALF), preferred_element_type=FULL
    )
    return chosen, slots


def one_hot(places, chosen, count):
    row = lax.broadcasted_iota(jnp.int32, (count, places.shape[1]), 0).astype(FULL)
    return jnp.where(row == places[0:1], jnp.broadcast_to(chosen[0:1], row.shape), 0.0)


def pack_kernel(ids_in, probs_in, tokens_in, cotangent_in, out, ids, probs, tokens, cotangent, done):
    pairs = ((ids_in, ids), (probs_in, probs), (tokens_in, tokens), (cotangent_in, cotangent))
    copies = [pltpu.make_async_copy(a, b, done.at[i]) for i, (a, b) in enumerate(pairs)]
    for copy in copies:
        copy.start()
    copies[0].wait()
    copies[1].wait()
    chosen, slots = earlier_count(ids[...])
    late = (slots >= MAIN).astype(FULL)
    pick_rows = one_hot(slots + late * MAIN, chosen, 80).astype(HALF)
    picked = one_hot(slots + MAIN + late * REST, chosen, 80)
    total = jnp.sum(jnp.where(ids[...] == 0, probs[...], 0.0), axis=0, keepdims=True)
    share = jnp.sum(picked * total, axis=1, keepdims=True)
    picked = picked.astype(HALF)
    copies[2].wait()
    copies[3].wait()
    width = out.shape[1]
    for i in range(0, width, 768):
        here = slice(i, i + 768)
        cotan = jnp.dot(picked, cotangent[:, here], preferred_element_type=FULL)
        rows = jnp.dot(pick_rows, tokens[:, here], preferred_element_type=FULL)
        out[:, here] = (rows + share * cotan)[0 : 2 * CAP].astype(HALF)


def pack(ids, probs, tokens, cotangent):
    values = (ids, probs, tokens, cotangent)
    return pl.pallas_call(
        pack_kernel,
        in_specs=[pl.BlockSpec(memory_space=pl.ANY)] * 4,
        out_shape=shape((2 * CAP, tokens.shape[1])),
        scratch_shapes=[pltpu.VMEM(v.shape, v.dtype) for v in values]
        + [pltpu.SemaphoreType.DMA((4,))],
        compiler_params=params(LIMIT),
        name="pack",
    )(*values)


def unpack_kernel(ids, *refs):
    pieces, out = refs[:-1], refs[-1]
    chosen, slots = earlier_count(ids[...])
    place = one_hot(slots, chosen, pieces[0].shape[0]).astype(HALF)
    total = pieces[0][...].astype(FULL)
    for piece in pieces[1:]:
        total = total + piece[...].astype(FULL)
    out[...] = tn_dot(place, total.astype(HALF)).astype(HALF)


def unpack(ids, pieces):
    count, (depth, width) = ids.shape[1], pieces[0].shape
    step = 1536
    return pl.pallas_call(
        unpack_kernel,
        grid=(width // step,),
        in_specs=[pl.BlockSpec(ids.shape, lambda j: (0, 0))]
        + [pl.BlockSpec((depth, step), lambda j: (0, j)) for _ in pieces],
        out_specs=pl.BlockSpec((count, step), lambda j: (0, j)),
        out_shape=shape((count, width)),
        compiler_params=params(32),
        name="unpack",
    )(ids, *pieces)


def padded_rows(n):
    return MAIN * n + -(-REST * n // 16) * 16


def assemble(blocks, rows, scaled):
    n, width = len(blocks), rows.shape[1]
    for i, block in enumerate(blocks):
        rows[MAIN * i : MAIN * (i + 1), :] = block[0:MAIN, :]
        scaled[MAIN * i : MAIN * (i + 1), :] = block[MAIN : 2 * MAIN, :]
    first = lax.broadcasted_iota(jnp.int32, (2 * REST, width), 0) < REST
    tails = [block[2 * MAIN : 2 * CAP, :].astype(FULL) for block in blocks]
    row_tails, scaled_tails = [], []
    for a, b in zip(tails[0::2], tails[1::2]):
        row_tails.append(jnp.where(first, a, pltpu.roll(b, REST, 0)))
        scaled_tails.append(jnp.where(first, pltpu.roll(a, REST, 0), b))
    if len(row_tails) % 2:
        row_tails.append(jnp.zeros((2 * REST, width), FULL))
        scaled_tails.append(jnp.zeros((2 * REST, width), FULL))
    for i in range(0, len(row_tails), 2):
        here = slice(MAIN * n + 8 * i, MAIN * n + 8 * i + 16)
        rows[here, :] = jnp.concatenate(row_tails[i : i + 2], axis=0).astype(HALF)
        scaled[here, :] = jnp.concatenate(scaled_tails[i : i + 2], axis=0).astype(HALF)


def activations(rows, scaled, gate, up, down):
    gate_pre = jnp.dot(rows, gate, preferred_element_type=FULL)
    up_pre = jnp.dot(rows, up, preferred_element_type=FULL)
    hidden_back = nt_dot(scaled, down)
    sigma = jax.nn.sigmoid(gate_pre)
    gate_act = gate_pre * sigma
    hidden = (gate_act * up_pre).astype(HALF)
    gate_back = (hidden_back * up_pre * sigma * (1.0 + gate_pre * (1.0 - sigma))).astype(HALF)
    up_back = (hidden_back * gate_act).astype(HALF)
    return hidden, gate_back, up_back


def forward_kernel(n, back, place, *refs):
    blocks, weights, refs = refs[:n], refs[n : n + 3], refs[n + 3 :]
    acts, own, other = refs[:3]
    refs = refs[3:]
    if back:
        send, keep = refs[:2]
        refs = refs[2:]
    rows, scaled = refs
    gate, up, down = weights
    width, part = rows.shape[1], own.shape[1] // 2
    assemble(blocks, rows, scaled)
    for out, index in ((own, 0), (other, 1)):
        columns = pl.ds(pl.multiple_of(place[index] * part, part), part)
        out[:, 0:part] = rows[:, columns]
        out[:, part : 2 * part] = scaled[:, columns]
    tiles = gate.shape[1] // TILE
    for j in range(tiles):
        here = slice(TILE * j, TILE * (j + 1))
        found = activations(rows[...], scaled[...], gate[:, here], up[:, here], down[here, :])
        for k in range(3):
            at = TILE * (3 * j + k)
            acts[:, at : at + TILE] = found[k]
    if back:
        half = n // 2
        mid, tail, reach = MAIN * half, MAIN * n, 8 * (-(-half // 2))
        skip = 8 * half - reach
        gate_back = [acts[:, TILE * (3 * j + 1) : TILE * (3 * j + 2)] for j in range(tiles)]
        up_back = [acts[:, TILE * (3 * j + 2) : TILE * (3 * j + 3)] for j in range(tiles)]
        gate_back, up_back = jnp.concatenate(gate_back, axis=1), jnp.concatenate(up_back, axis=1)
        for i in range(0, width, 2 * TILE):
            here = slice(i, i + 2 * TILE)
            total = nt_dot(gate_back, gate[here, :]) + nt_dot(up_back, up[here, :])
            keep[0:mid, here] = total[0:mid].astype(HALF)
            send[0:mid, here] = total[mid : 2 * mid].astype(HALF)
            keep[mid : mid + reach, here] = total[tail : tail + reach].astype(HALF)
            send[mid : mid + reach, here] = total[tail + skip : tail + skip + reach].astype(HALF)


def forward(blocks, gate, up, down, place, part, back):
    n, (width, hidden) = len(blocks), gate.shape
    count = padded_rows(n)
    in_vmem = pl.BlockSpec(memory_space=pltpu.VMEM)
    out_shape = [
        shape((count, 3 * hidden)),
        shape((count, 2 * part)),
        shape((count, 2 * part)),
    ]
    if back:
        half = n // 2
        out_shape += [shape((MAIN * half + 8 * (-(-half // 2)), width))] * 2
    matmuls = 5 if back else 3
    return pl.pallas_call(
        functools.partial(forward_kernel, n, back),
        in_specs=[pl.BlockSpec(memory_space=pltpu.SMEM)] + [in_vmem] * (n + 3),
        out_specs=[in_vmem] * len(out_shape),
        out_shape=out_shape,
        scratch_shapes=[
            pltpu.VMEM((count, width), HALF),
            pltpu.VMEM((count, width), HALF),
        ],
        compiler_params=params(LIMIT),
        cost_estimate=pl.CostEstimate(
            flops=2 * matmuls * count * width * hidden,
            bytes_accessed=6 * width * hidden + 4 * count * (width + part),
            transcendentals=count * hidden,
        ),
        name="forward_back" if back else "forward",
    )(place, *blocks, gate, up, down)


def grads_kernel(n, *refs):
    acts, parts, refs = refs[:n], refs[n : 2 * n], refs[2 * n :]
    gate_grad, up_grad, down_grad, act_rows, part_rows = refs
    start = 0
    for act, piece in zip(acts, parts):
        here = slice(start, start + act.shape[0])
        act_rows[here, :] = act[...]
        part_rows[here, :] = piece[...]
        start += act.shape[0]
    part = part_rows.shape[1] // 2
    tiles = act_rows.shape[1] // (3 * TILE)
    for i in range(part // TILE):
        picked = part_rows[:, i * TILE : (i + 1) * TILE].T
        here = slice(i * TILE, (i + 1) * TILE)
        for j in range(tiles):
            at = 3 * TILE * j
            there = slice(j * TILE, (j + 1) * TILE)
            gate_grad[here, there] = jnp.dot(
                picked, act_rows[:, at + TILE : at + 2 * TILE], preferred_element_type=FULL
            ).astype(HALF)
            up_grad[here, there] = jnp.dot(
                picked, act_rows[:, at + 2 * TILE : at + 3 * TILE], preferred_element_type=FULL
            ).astype(HALF)
    for j in range(tiles):
        at = 3 * TILE * j
        hidden = act_rows[:, at : at + TILE].T
        down_grad[j * TILE : (j + 1) * TILE, :] = jnp.dot(
            hidden, part_rows[:, part : 2 * part], preferred_element_type=FULL
        ).astype(HALF)


def grads(acts, parts, part, hidden):
    n, count = len(acts), sum(a.shape[0] for a in acts)
    in_vmem = pl.BlockSpec(memory_space=pltpu.VMEM)
    return pl.pallas_call(
        functools.partial(grads_kernel, n),
        in_specs=[in_vmem] * (2 * n),
        out_specs=[in_vmem] * 3,
        out_shape=[shape((part, hidden)), shape((part, hidden)), shape((hidden, part))],
        scratch_shapes=[
            pltpu.VMEM((count, 3 * hidden), HALF),
            pltpu.VMEM((count, 2 * part), HALF),
        ],
        compiler_params=params(LIMIT),
        cost_estimate=pl.CostEstimate(
            flops=6 * count * part * hidden,
            bytes_accessed=2 * count * (3 * hidden + 2 * part) + 6 * part * hidden,
            transcendentals=0,
        ),
        name="grads",
    )(*acts, *parts)


def finish_kernel(n, place, *refs):
    blocks, (gate, up, down), early, refs = refs[:n], refs[n : n + 3], refs[n + 3 : n + 6], refs[n + 6 :]
    gate_grad, up_grad, down_grad, rows, scaled = refs
    part = gate_grad.shape[0]
    assemble(blocks, rows, scaled)
    columns = pl.ds(pl.multiple_of(place[0] * part, part), part)
    picked, cotan = rows[:, columns].T, scaled[:, columns]
    for j in range(gate.shape[1] // TILE):
        here = slice(TILE * j, TILE * (j + 1))
        hidden, gate_back, up_back = activations(
            rows[...], scaled[...], gate[:, here], up[:, here], down[here, :]
        )
        gate_grad[:, here] = (
            early[0][:, here].astype(FULL)
            + jnp.dot(picked, gate_back, preferred_element_type=FULL)
        ).astype(HALF)
        up_grad[:, here] = (
            early[1][:, here].astype(FULL) + jnp.dot(picked, up_back, preferred_element_type=FULL)
        ).astype(HALF)
        down_grad[here, :] = (
            early[2][here, :].astype(FULL) + tn_dot(hidden, cotan)
        ).astype(HALF)


def finish(blocks, gate, up, down, place, early):
    n, (width, hidden) = len(blocks), gate.shape
    count, part = padded_rows(n), early[0].shape[0]
    in_vmem = pl.BlockSpec(memory_space=pltpu.VMEM)
    return pl.pallas_call(
        functools.partial(finish_kernel, n),
        in_specs=[pl.BlockSpec(memory_space=pltpu.SMEM)] + [in_vmem] * (n + 6),
        out_specs=[in_vmem] * 3,
        out_shape=[shape(e.shape) for e in early],
        scratch_shapes=[
            pltpu.VMEM((count, width), HALF),
            pltpu.VMEM((count, width), HALF),
        ],
        compiler_params=params(LIMIT),
        cost_estimate=pl.CostEstimate(
            flops=6 * count * (width + part) * hidden,
            bytes_accessed=6 * width * hidden + 2 * n * CAP * width + 12 * part * hidden,
            transcendentals=count * hidden,
        ),
        name="finish",
    )(place, *blocks, gate, up, down, *early)


def merge_kernel(n, keep, came, *outs):
    mid = MAIN * n
    kept, other = keep[mid:, :].astype(FULL), came[mid:, :].astype(FULL)
    if n % 2:
        other = pltpu.roll(other, other.shape[0] - REST, 0)
    tails = kept + other
    for i, out in enumerate(outs):
        here = slice(MAIN * i, MAIN * (i + 1))
        out[0:MAIN, :] = (keep[here, :].astype(FULL) + came[here, :].astype(FULL)).astype(HALF)
        pair = tails[8 * (i // 2) : 8 * (i // 2) + 8]
        out[MAIN : MAIN + 8, :] = (pair if i % 2 == 0 else pltpu.roll(pair, REST, 0)).astype(HALF)


def merge(n, keep, came):
    return pl.pallas_call(
        functools.partial(merge_kernel, n),
        out_shape=[shape((MAIN + 8, keep.shape[1]))] * n,
        compiler_params=params(32),
        name="merge",
    )(keep, came)


def after(value, *others):
    return lax.optimization_barrier((value, *others))[0]


def per_device(tokens, cotangent, route_ids, route_probs, gate_weight, up_weight, down_weight):
    n_dp, n_expert = lax.axis_size("dp"), lax.axis_size("expert")
    core_pairs = [(i, i ^ 1) for i in range(n_dp)]
    y_pairs = [(i, (i + 2) % n_dp) for i in range(n_dp)]
    x_pairs = [(i, i ^ 1) for i in range(n_expert)]

    def over_core(v):
        return lax.ppermute(v, "dp", core_pairs)

    def over_y(v):
        return lax.ppermute(v, "dp", y_pairs)

    def over_x(v):
        return lax.ppermute(v, "expert", x_pairs)

    def over_z(v, by):
        return lax.ppermute(
            v, "expert", [(i, (i + 2 * by) % n_expert) for i in range(n_expert)]
        )

    part = tokens.shape[1] // n_dp
    p = lax.axis_index("dp")
    place = jnp.stack([p, p + 1 - 2 * (p % 2)]).astype(jnp.int32)
    ids, probs = route_ids.T, route_probs.T
    weights = dict(gate=gate_weight, up=up_weight, down=down_weight)

    b0 = pack(ids, probs, tokens, cotangent)
    z1 = over_z(b0, 1)
    x0, y0 = over_x(b0), over_y(b0)
    x1, y1 = over_x(z1), over_y(z1)
    z3 = over_z(after(b0, z1), -1)
    yx0 = over_x(y0)
    z2 = over_z(after(z1, z3), 1)
    x3, y3 = over_x(z3), over_y(z3)
    yx1 = over_y(x1)
    x2, y2 = over_x(z2), over_y(z2)
    yx3, yx2 = over_y(x3), over_y(x2)

    acts, parts = [], []

    def share(act, own, other):
        acts.extend([act, over_core(act)])
        parts.extend([own, over_core(other)])

    run = functools.partial(forward, place=place, part=part, **weights)
    *first, send, keep = run([b0, z1, z3, x0, x1, x3], back=True)
    pieces = merge(3, keep, over_x(send))
    share(*first)
    *second, send, keep = run([z2, x2], back=True)
    pieces += merge(1, keep, over_x(send))
    share(*second)
    returned = [pieces[0], over_z(pieces[1], -1), over_z(pieces[2], 1), over_z(pieces[3], 2)]
    share(*run([y0, yx0, y1, yx1], back=False))
    early = grads(acts, parts, part, gate_weight.shape[1])
    last = [y3, y2, yx3, yx2]
    last = last + [over_core(b) for b in last]
    gate_grad, up_grad, down_grad = finish(last, place=place, early=early, **weights)
    return unpack(ids, returned), gate_grad, up_grad, down_grad


def pick_rows(placer, values):
    return lax.dot_general(
        placer, values, (((0,), (0,)), ((), ())), preferred_element_type=jnp.float32
    ).astype(jnp.bfloat16)


def per_device_general(tokens, cotangent, route_ids, route_probs, gate_weight, up_weight, down_weight):
    hits = route_ids == 0
    chosen = jnp.any(hits, axis=1).astype(jnp.int32)
    share = jnp.sum(jnp.where(hits, route_probs, 0.0), axis=1)
    slots = jnp.cumsum(chosen) - chosen
    placer_mask = (slots[:, None] == jnp.arange(CAP, dtype=jnp.int32)[None, :]) & (
        chosen[:, None] == 1
    )
    placer = placer_mask.astype(jnp.float32)
    placer_half = placer_mask.astype(jnp.bfloat16)
    local_rows = pick_rows(placer_half, tokens)
    local_cotan = pick_rows(placer_half, cotangent)
    local_shares = jnp.sum(placer * share[:, None], axis=0)
    routed, routed_cotan, routed_shares = (
        lax.all_gather(local_rows, "expert", axis=0, tiled=True),
        lax.all_gather(local_cotan, "expert", axis=0, tiled=True),
        lax.all_gather(local_shares.astype(jnp.bfloat16), "expert", axis=0, tiled=True).astype(
            local_shares.dtype
        ),
    )
    gate_pre = jnp.dot(routed, gate_weight, preferred_element_type=jnp.float32)
    up_pre = jnp.dot(routed, up_weight, preferred_element_type=jnp.float32)
    sigma = jax.nn.sigmoid(gate_pre)
    gate_act = gate_pre * sigma
    hidden = (gate_act * up_pre).astype(jnp.bfloat16)
    gate_pre, up_pre, sigma, gate_act, hidden = (gate_pre, up_pre, sigma, gate_act, hidden)
    scaled = (routed_shares[:, None] * routed_cotan.astype(jnp.float32)).astype(jnp.bfloat16)
    down_part = lax.dot_general(
        hidden, scaled, (((0,), (0,)), ((), ())), preferred_element_type=jnp.float32
    )
    hidden_back = lax.dot_general(
        scaled, down_weight, (((1,), (1,)), ((), ())), preferred_element_type=jnp.float32
    )
    gate_back = (hidden_back * up_pre * sigma * (1.0 + gate_pre * (1.0 - sigma))).astype(
        jnp.bfloat16
    )
    up_back = (hidden_back * gate_act).astype(jnp.bfloat16)
    gate_part = lax.dot_general(
        routed, gate_back, (((0,), (0,)), ((), ())), preferred_element_type=jnp.float32
    )
    up_part = lax.dot_general(
        routed, up_back, (((0,), (0,)), ((), ())), preferred_element_type=jnp.float32
    )
    gate_sum, up_sum, down_sum = (
        lax.psum_scatter(
            gate_part.astype(jnp.bfloat16), "dp", scatter_dimension=0, tiled=True
        ).astype(jnp.float32),
        lax.psum_scatter(
            up_part.astype(jnp.bfloat16), "dp", scatter_dimension=0, tiled=True
        ).astype(jnp.float32),
        lax.psum_scatter(
            down_part.astype(jnp.bfloat16), "dp", scatter_dimension=1, tiled=True
        ).astype(jnp.float32),
    )
    partial_value = lax.dot_general(
        gate_back, gate_weight, (((1,), (1,)), ((), ())), preferred_element_type=jnp.float32
    )
    partial_value = partial_value + lax.dot_general(
        up_back, up_weight, (((1,), (1,)), ((), ())), preferred_element_type=jnp.float32
    )
    returned = lax.psum_scatter(
        partial_value.astype(jnp.bfloat16), "expert", scatter_dimension=0, tiled=True
    ).astype(jnp.float32)
    token_grad = jnp.dot(placer, returned, precision=lax.Precision.HIGHEST).astype(jnp.bfloat16)
    return (
        token_grad,
        gate_sum.astype(jnp.bfloat16),
        up_sum.astype(jnp.bfloat16),
        down_sum.astype(jnp.bfloat16),
    )


def solution(mesh):
    in_specs = (
        P(("dp", "expert"), None),
        P(("dp", "expert"), None),
        P(("dp", "expert"), None),
        P(("dp", "expert"), None),
        P(None, "expert"),
        P(None, "expert"),
        P("expert", None),
    )
    out_specs = (P(("dp", "expert"), None), P("dp", "expert"), P("dp", "expert"), P("expert", "dp"))
    fast = mesh.shape["dp"] == 4 and mesh.shape["expert"] == 8
    body = per_device if fast else per_device_general
    return jax.shard_map(
        body, mesh=mesh, in_specs=in_specs, out_specs=out_specs, check_vma=False
    )
```

```python
import functools

import jax
import jax.numpy as jnp
from jax import lax
from jax.experimental import pallas as pl
from jax.experimental.pallas import tpu as pltpu
from jax.sharding import PartitionSpec as P

CAP = 36
MAIN = 32
REST = CAP - MAIN
TILE = 256
LIMIT = 20
HALF = jnp.bfloat16
FULL = jnp.float32


def shape(dims, dtype=HALF):
    return jax.ShapeDtypeStruct(dims, dtype)


def params(mib):
    return pltpu.CompilerParams(vmem_limit_bytes=mib * 2**20)


def nt_dot(a, b):
    return lax.dot_general(a, b, (((1,), (1,)), ((), ())), preferred_element_type=FULL)


def tn_dot(a, b):
    return lax.dot_general(a, b, (((0,), (0,)), ((), ())), preferred_element_type=FULL)


def earlier_count(ids):
    count = ids.shape[1]
    chosen = jnp.max((ids == 0).astype(FULL), axis=0, keepdims=True)
    chosen = jnp.broadcast_to(chosen, (8, count))
    before = lax.broadcasted_iota(jnp.int32, (count, count), 0) < lax.broadcasted_iota(
        jnp.int32, (count, count), 1
    )
    slots = jnp.dot(
        chosen.astype(HALF), before.astype(FULL).astype(HALF), preferred_element_type=FULL
    )
    return chosen, slots


def one_hot(places, chosen, count):
    row = lax.broadcasted_iota(jnp.int32, (count, places.shape[1]), 0).astype(FULL)
    return jnp.where(row == places[0:1], jnp.broadcast_to(chosen[0:1], row.shape), 0.0)


def pack_kernel(ids_in, probs_in, tokens_in, cotangent_in, out, ids, probs, tokens, cotangent, done):
    pairs = ((ids_in, ids), (probs_in, probs), (tokens_in, tokens), (cotangent_in, cotangent))
    copies = [pltpu.make_async_copy(a, b, done.at[i]) for i, (a, b) in enumerate(pairs)]
    for copy in copies:
        copy.start()
    copies[0].wait()
    copies[1].wait()
    chosen, slots = earlier_count(ids[...])
    late = (slots >= MAIN).astype(FULL)
    pick_rows = one_hot(slots + late * MAIN, chosen, 80).astype(HALF)
    picked = one_hot(slots + MAIN + late * REST, chosen, 80)
    total = jnp.sum(jnp.where(ids[...] == 0, probs[...], 0.0), axis=0, keepdims=True)
    share = jnp.sum(picked * total, axis=1, keepdims=True)
    picked = picked.astype(HALF)
    copies[2].wait()
    copies[3].wait()
    width = out.shape[1]
    for i in range(0, width, 768):
        here = slice(i, i + 768)
        cotan = jnp.dot(picked, cotangent[:, here], preferred_element_type=FULL)
        rows = jnp.dot(pick_rows, tokens[:, here], preferred_element_type=FULL)
        out[:, here] = (rows + share * cotan)[0 : 2 * CAP].astype(HALF)


def pack(ids, probs, tokens, cotangent):
    values = (ids, probs, tokens, cotangent)
    return pl.pallas_call(
        pack_kernel,
        in_specs=[pl.BlockSpec(memory_space=pltpu.HBM)] * 4,
        out_shape=shape((2 * CAP, tokens.shape[1])),
        scratch_shapes=[pltpu.VMEM(v.shape, v.dtype) for v in values]
        + [pltpu.SemaphoreType.DMA((4,))],
        compiler_params=params(LIMIT),
        name="pack",
    )(*values)


def unpack_kernel(ids, *refs):
    pieces, out = refs[:-1], refs[-1]
    chosen, slots = earlier_count(ids[...])
    place = one_hot(slots, chosen, pieces[0].shape[0]).astype(HALF)
    total = pieces[0][...].astype(FULL)
    for piece in pieces[1:]:
        total = total + piece[...].astype(FULL)
    out[...] = tn_dot(place, total.astype(HALF)).astype(HALF)


def unpack(ids, pieces):
    count, (depth, width) = ids.shape[1], pieces[0].shape
    step = 1536
    return pl.pallas_call(
        unpack_kernel,
        grid=(width // step,),
        in_specs=[pl.BlockSpec(ids.shape, lambda j: (0, 0))]
        + [pl.BlockSpec((depth, step), lambda j: (0, j)) for _ in pieces],
        out_specs=pl.BlockSpec((count, step), lambda j: (0, j)),
        out_shape=shape((count, width)),
        compiler_params=params(32),
        name="unpack",
    )(ids, *pieces)


def padded_rows(n):
    return MAIN * n + -(-REST * n // 16) * 16


def assemble(blocks, rows, scaled):
    n, width = len(blocks), rows.shape[1]
    for i, block in enumerate(blocks):
        rows[MAIN * i : MAIN * (i + 1), :] = block[0:MAIN, :]
        scaled[MAIN * i : MAIN * (i + 1), :] = block[MAIN : 2 * MAIN, :]
    first = lax.broadcasted_iota(jnp.int32, (2 * REST, width), 0) < REST
    tails = [block[2 * MAIN : 2 * CAP, :].astype(FULL) for block in blocks]
    row_tails, scaled_tails = [], []
    for a, b in zip(tails[0::2], tails[1::2]):
        row_tails.append(jnp.where(first, a, pltpu.roll(b, REST, 0)))
        scaled_tails.append(jnp.where(first, pltpu.roll(a, REST, 0), b))
    if len(row_tails) % 2:
        row_tails.append(jnp.zeros((2 * REST, width), FULL))
        scaled_tails.append(jnp.zeros((2 * REST, width), FULL))
    for i in range(0, len(row_tails), 2):
        here = slice(MAIN * n + 8 * i, MAIN * n + 8 * i + 16)
        rows[here, :] = jnp.concatenate(row_tails[i : i + 2], axis=0).astype(HALF)
        scaled[here, :] = jnp.concatenate(scaled_tails[i : i + 2], axis=0).astype(HALF)


def activations(rows, scaled, gate, up, down):
    gate_pre = jnp.dot(rows, gate, preferred_element_type=FULL)
    up_pre = jnp.dot(rows, up, preferred_element_type=FULL)
    hidden_back = nt_dot(scaled, down)
    sigma = jax.nn.sigmoid(gate_pre)
    gate_act = gate_pre * sigma
    hidden = (gate_act * up_pre).astype(HALF)
    gate_back = (hidden_back * up_pre * sigma * (1.0 + gate_pre * (1.0 - sigma))).astype(HALF)
    up_back = (hidden_back * gate_act).astype(HALF)
    return hidden, gate_back, up_back


def forward_kernel(n, back, place, *refs):
    blocks, weights, refs = refs[:n], refs[n : n + 3], refs[n + 3 :]
    acts, own, other = refs[:3]
    refs = refs[3:]
    if back:
        send, keep = refs[:2]
        refs = refs[2:]
    rows, scaled = refs
    gate, up, down = weights
    width, part = rows.shape[1], own.shape[1] // 2
    assemble(blocks, rows, scaled)
    for out, index in ((own, 0), (other, 1)):
        columns = pl.ds(pl.multiple_of(place[index] * part, part), part)
        out[:, 0:part] = rows[:, columns]
        out[:, part : 2 * part] = scaled[:, columns]
    tiles = gate.shape[1] // TILE
    for j in range(tiles):
        here = slice(TILE * j, TILE * (j + 1))
        found = activations(rows[...], scaled[...], gate[:, here], up[:, here], down[here, :])
        for k in range(3):
            at = TILE * (3 * j + k)
            acts[:, at : at + TILE] = found[k]
    if back:
        half = n // 2
        mid, tail, reach = MAIN * half, MAIN * n, 8 * (-(-half // 2))
        skip = 8 * half - reach
        gate_back = [acts[:, TILE * (3 * j + 1) : TILE * (3 * j + 2)] for j in range(tiles)]
        up_back = [acts[:, TILE * (3 * j + 2) : TILE * (3 * j + 3)] for j in range(tiles)]
        gate_back, up_back = jnp.concatenate(gate_back, axis=1), jnp.concatenate(up_back, axis=1)
        for i in range(0, width, 2 * TILE):
            here = slice(i, i + 2 * TILE)
            total = nt_dot(gate_back, gate[here, :]) + nt_dot(up_back, up[here, :])
            keep[0:mid, here] = total[0:mid].astype(HALF)
            send[0:mid, here] = total[mid : 2 * mid].astype(HALF)
            keep[mid : mid + reach, here] = total[tail : tail + reach].astype(HALF)
            send[mid : mid + reach, here] = total[tail + skip : tail + skip + reach].astype(HALF)


def forward(blocks, gate, up, down, place, part, back):
    n, (width, hidden) = len(blocks), gate.shape
    count = padded_rows(n)
    in_vmem = pl.BlockSpec(memory_space=pltpu.VMEM)
    out_shape = [
        shape((count, 3 * hidden)),
        shape((count, 2 * part)),
        shape((count, 2 * part)),
    ]
    if back:
        half = n // 2
        out_shape += [shape((MAIN * half + 8 * (-(-half // 2)), width))] * 2
    matmuls = 5 if back else 3
    return pl.pallas_call(
        functools.partial(forward_kernel, n, back),
        in_specs=[pl.BlockSpec(memory_space=pltpu.SMEM)] + [in_vmem] * (n + 3),
        out_specs=[in_vmem] * len(out_shape),
        out_shape=out_shape,
        scratch_shapes=[
            pltpu.VMEM((count, width), HALF),
            pltpu.VMEM((count, width), HALF),
        ],
        compiler_params=params(LIMIT),
        cost_estimate=pl.CostEstimate(
            flops=2 * matmuls * count * width * hidden,
            bytes_accessed=6 * width * hidden + 4 * count * (width + part),
            transcendentals=count * hidden,
        ),
        name="forward_back" if back else "forward",
    )(place, *blocks, gate, up, down)


def grads_kernel(n, *refs):
    acts, parts, refs = refs[:n], refs[n : 2 * n], refs[2 * n :]
    gate_grad, up_grad, down_grad, act_rows, part_rows = refs
    start = 0
    for act, piece in zip(acts, parts):
        here = slice(start, start + act.shape[0])
        act_rows[here, :] = act[...]
        part_rows[here, :] = piece[...]
        start += act.shape[0]
    part = part_rows.shape[1] // 2
    tiles = act_rows.shape[1] // (3 * TILE)
    for i in range(part // TILE):
        picked = part_rows[:, i * TILE : (i + 1) * TILE].T
        here = slice(i * TILE, (i + 1) * TILE)
        for j in range(tiles):
            at = 3 * TILE * j
            there = slice(j * TILE, (j + 1) * TILE)
            gate_grad[here, there] = jnp.dot(
                picked, act_rows[:, at + TILE : at + 2 * TILE], preferred_element_type=FULL
            ).astype(HALF)
            up_grad[here, there] = jnp.dot(
                picked, act_rows[:, at + 2 * TILE : at + 3 * TILE], preferred_element_type=FULL
            ).astype(HALF)
    for j in range(tiles):
        at = 3 * TILE * j
        hidden = act_rows[:, at : at + TILE].T
        down_grad[j * TILE : (j + 1) * TILE, :] = jnp.dot(
            hidden, part_rows[:, part : 2 * part], preferred_element_type=FULL
        ).astype(HALF)


def grads(acts, parts, part, hidden):
    n, count = len(acts), sum(a.shape[0] for a in acts)
    in_vmem = pl.BlockSpec(memory_space=pltpu.VMEM)
    return pl.pallas_call(
        functools.partial(grads_kernel, n),
        in_specs=[in_vmem] * (2 * n),
        out_specs=[in_vmem] * 3,
        out_shape=[shape((part, hidden)), shape((part, hidden)), shape((hidden, part))],
        scratch_shapes=[
            pltpu.VMEM((count, 3 * hidden), HALF),
            pltpu.VMEM((count, 2 * part), HALF),
        ],
        compiler_params=params(LIMIT),
        cost_estimate=pl.CostEstimate(
            flops=6 * count * part * hidden,
            bytes_accessed=2 * count * (3 * hidden + 2 * part) + 6 * part * hidden,
            transcendentals=0,
        ),
        name="grads",
    )(*acts, *parts)


def finish_kernel(n, place, *refs):
    blocks, (gate, up, down), early, refs = refs[:n], refs[n : n + 3], refs[n + 3 : n + 6], refs[n + 6 :]
    gate_grad, up_grad, down_grad, rows, scaled = refs
    part = gate_grad.shape[0]
    assemble(blocks, rows, scaled)
    columns = pl.ds(pl.multiple_of(place[0] * part, part), part)
    picked, cotan = rows[:, columns].T, scaled[:, columns]
    for j in range(gate.shape[1] // TILE):
        here = slice(TILE * j, TILE * (j + 1))
        hidden, gate_back, up_back = activations(
            rows[...], scaled[...], gate[:, here], up[:, here], down[here, :]
        )
        gate_grad[:, here] = (
            early[0][:, here].astype(FULL)
            + jnp.dot(picked, gate_back, preferred_element_type=FULL)
        ).astype(HALF)
        up_grad[:, here] = (
            early[1][:, here].astype(FULL) + jnp.dot(picked, up_back, preferred_element_type=FULL)
        ).astype(HALF)
        down_grad[here, :] = (
            early[2][here, :].astype(FULL) + tn_dot(hidden, cotan)
        ).astype(HALF)


def finish(blocks, gate, up, down, place, early):
    n, (width, hidden) = len(blocks), gate.shape
    count, part = padded_rows(n), early[0].shape[0]
    in_vmem = pl.BlockSpec(memory_space=pltpu.VMEM)
    return pl.pallas_call(
        functools.partial(finish_kernel, n),
        in_specs=[pl.BlockSpec(memory_space=pltpu.SMEM)] + [in_vmem] * (n + 6),
        out_specs=[in_vmem] * 3,
        out_shape=[shape(e.shape) for e in early],
        scratch_shapes=[
            pltpu.VMEM((count, width), HALF),
            pltpu.VMEM((count, width), HALF),
        ],
        compiler_params=params(LIMIT),
        cost_estimate=pl.CostEstimate(
            flops=6 * count * (width + part) * hidden,
            bytes_accessed=6 * width * hidden + 2 * n * CAP * width + 12 * part * hidden,
            transcendentals=count * hidden,
        ),
        name="finish",
    )(place, *blocks, gate, up, down, *early)


def ready_kernel(place, block, gate, up, down, out):
    out[0] = place[0]
    out[1] = place[1]


def ready(place, block, gate, up, down):
    in_vmem, in_smem = pl.BlockSpec(memory_space=pltpu.VMEM), pl.BlockSpec(memory_space=pltpu.SMEM)
    return pl.pallas_call(
        ready_kernel,
        in_specs=[in_smem, in_vmem, in_vmem, in_vmem, in_vmem],
        out_specs=in_smem,
        out_shape=shape((2,), jnp.int32),
        compiler_params=params(LIMIT),
        cost_estimate=pl.CostEstimate(
            flops=0, bytes_accessed=6 * gate.size, transcendentals=0
        ),
        name="ready",
    )(place, block, gate, up, down)


def merge_kernel(n, keep, came, *outs):
    mid = MAIN * n
    kept, other = keep[mid:, :].astype(FULL), came[mid:, :].astype(FULL)
    if n % 2:
        other = pltpu.roll(other, other.shape[0] - REST, 0)
    tails = kept + other
    for i, out in enumerate(outs):
        here = slice(MAIN * i, MAIN * (i + 1))
        out[0:MAIN, :] = (keep[here, :].astype(FULL) + came[here, :].astype(FULL)).astype(HALF)
        pair = tails[8 * (i // 2) : 8 * (i // 2) + 8]
        out[MAIN : MAIN + 8, :] = (pair if i % 2 == 0 else pltpu.roll(pair, REST, 0)).astype(HALF)


def merge(n, keep, came):
    return pl.pallas_call(
        functools.partial(merge_kernel, n),
        out_shape=[shape((MAIN + 8, keep.shape[1]))] * n,
        compiler_params=params(32),
        name="merge",
    )(keep, came)


def after(value, *others):
    return lax.optimization_barrier((value, *others))[0]


def per_device(tokens, cotangent, route_ids, route_probs, gate_weight, up_weight, down_weight):
    n_dp, n_expert = lax.axis_size("dp"), lax.axis_size("expert")
    core_pairs = [(i, i ^ 1) for i in range(n_dp)]
    y_pairs = [(i, (i + 2) % n_dp) for i in range(n_dp)]
    x_pairs = [(i, i ^ 1) for i in range(n_expert)]

    def over_core(v):
        return lax.ppermute(v, "dp", core_pairs)

    def over_y(v):
        return lax.ppermute(v, "dp", y_pairs)

    def over_x(v):
        return lax.ppermute(v, "expert", x_pairs)

    def over_z(v, by):
        return lax.ppermute(
            v, "expert", [(i, (i + 2 * by) % n_expert) for i in range(n_expert)]
        )

    part = tokens.shape[1] // n_dp
    p = lax.axis_index("dp")
    place = jnp.stack([p, p + 1 - 2 * (p % 2)]).astype(jnp.int32)
    ids, probs = route_ids.T, route_probs.T
    weights = dict(gate=gate_weight, up=up_weight, down=down_weight)

    b0 = pack(ids, probs, tokens, cotangent)
    place = ready(place, b0, **weights)
    z1, x0, y0, z3 = over_z(b0, 1), over_x(b0), over_y(b0), over_z(b0, -1)
    xy0 = over_y(after(x0, y0))
    z1 = after(z1, x0, y0)
    z2, x1, y1 = over_z(z1, 1), over_x(z1), over_y(z1)
    x3 = over_x(z3)
    xy1 = over_y(after(x1, y1))
    x2 = over_x(after(z2, x1))
    y2 = over_y(after(z2, xy0))
    y3 = over_z(after(y0, z2), -1)
    xy3 = over_z(after(xy0, z2), -1)
    xy2 = over_y(after(x2, xy1))

    acts, parts = [], []

    def share(act, own, other):
        acts.extend([act, over_core(act)])
        parts.extend([own, over_core(other)])

    run = functools.partial(forward, place=place, part=part, **weights)
    *first, send, keep = run([b0, z1, z3, x0, x1, x3], back=True)
    pieces = merge(3, keep, over_x(send))
    share(*first)
    *second, send, keep = run([z2, x2], back=True)
    pieces += merge(1, keep, over_x(send))
    share(*second)
    returned = [pieces[0], over_z(pieces[1], -1), over_z(pieces[2], 1), over_z(pieces[3], 2)]
    share(*run([y0, xy0, y1, xy1, y3, xy3], back=False))
    early = grads(acts, parts, part, gate_weight.shape[1])
    last = [y2, xy2]
    last = last + [over_core(b) for b in last]
    gate_grad, up_grad, down_grad = finish(last, place=place, early=early, **weights)
    return unpack(ids, returned), gate_grad, up_grad, down_grad


def pick_rows(placer, values):
    return lax.dot_general(
        placer, values, (((0,), (0,)), ((), ())), preferred_element_type=jnp.float32
    ).astype(jnp.bfloat16)


def per_device_general(tokens, cotangent, route_ids, route_probs, gate_weight, up_weight, down_weight):
    hits = route_ids == 0
    chosen = jnp.any(hits, axis=1).astype(jnp.int32)
    share = jnp.sum(jnp.where(hits, route_probs, 0.0), axis=1)
    slots = jnp.cumsum(chosen) - chosen
    placer_mask = (slots[:, None] == jnp.arange(CAP, dtype=jnp.int32)[None, :]) & (
        chosen[:, None] == 1
    )
    placer = placer_mask.astype(jnp.float32)
    placer_half = placer_mask.astype(jnp.bfloat16)
    local_rows = pick_rows(placer_half, tokens)
    local_cotan = pick_rows(placer_half, cotangent)
    local_shares = jnp.sum(placer * share[:, None], axis=0)
    routed, routed_cotan, routed_shares = (
        lax.all_gather(local_rows, "expert", axis=0, tiled=True),
        lax.all_gather(local_cotan, "expert", axis=0, tiled=True),
        lax.all_gather(local_shares.astype(jnp.bfloat16), "expert", axis=0, tiled=True).astype(
            local_shares.dtype
        ),
    )
    gate_pre = jnp.dot(routed, gate_weight, preferred_element_type=jnp.float32)
    up_pre = jnp.dot(routed, up_weight, preferred_element_type=jnp.float32)
    sigma = jax.nn.sigmoid(gate_pre)
    gate_act = gate_pre * sigma
    hidden = (gate_act * up_pre).astype(jnp.bfloat16)
    gate_pre, up_pre, sigma, gate_act, hidden = (gate_pre, up_pre, sigma, gate_act, hidden)
    scaled = (routed_shares[:, None] * routed_cotan.astype(jnp.float32)).astype(jnp.bfloat16)
    down_part = lax.dot_general(
        hidden, scaled, (((0,), (0,)), ((), ())), preferred_element_type=jnp.float32
    )
    hidden_back = lax.dot_general(
        scaled, down_weight, (((1,), (1,)), ((), ())), preferred_element_type=jnp.float32
    )
    gate_back = (hidden_back * up_pre * sigma * (1.0 + gate_pre * (1.0 - sigma))).astype(
        jnp.bfloat16
    )
    up_back = (hidden_back * gate_act).astype(jnp.bfloat16)
    gate_part = lax.dot_general(
        routed, gate_back, (((0,), (0,)), ((), ())), preferred_element_type=jnp.float32
    )
    up_part = lax.dot_general(
        routed, up_back, (((0,), (0,)), ((), ())), preferred_element_type=jnp.float32
    )
    gate_sum, up_sum, down_sum = (
        lax.psum_scatter(
            gate_part.astype(jnp.bfloat16), "dp", scatter_dimension=0, tiled=True
        ).astype(jnp.float32),
        lax.psum_scatter(
            up_part.astype(jnp.bfloat16), "dp", scatter_dimension=0, tiled=True
        ).astype(jnp.float32),
        lax.psum_scatter(
            down_part.astype(jnp.bfloat16), "dp", scatter_dimension=1, tiled=True
        ).astype(jnp.float32),
    )
    partial_value = lax.dot_general(
        gate_back, gate_weight, (((1,), (1,)), ((), ())), preferred_element_type=jnp.float32
    )
    partial_value = partial_value + lax.dot_general(
        up_back, up_weight, (((1,), (1,)), ((), ())), preferred_element_type=jnp.float32
    )
    returned = lax.psum_scatter(
        partial_value.astype(jnp.bfloat16), "expert", scatter_dimension=0, tiled=True
    ).astype(jnp.float32)
    token_grad = jnp.dot(placer, returned, precision=lax.Precision.HIGHEST).astype(jnp.bfloat16)
    return (
        token_grad,
        gate_sum.astype(jnp.bfloat16),
        up_sum.astype(jnp.bfloat16),
        down_sum.astype(jnp.bfloat16),
    )


def solution(mesh):
    in_specs = (
        P(("dp", "expert"), None),
        P(("dp", "expert"), None),
        P(("dp", "expert"), None),
        P(("dp", "expert"), None),
        P(None, "expert"),
        P(None, "expert"),
        P("expert", None),
    )
    out_specs = (P(("dp", "expert"), None), P("dp", "expert"), P("dp", "expert"), P("expert", "dp"))
    fast = mesh.shape["dp"] == 4 and mesh.shape["expert"] == 8
    body = per_device if fast else per_device_general
    return jax.shard_map(
        body, mesh=mesh, in_specs=in_specs, out_specs=out_specs, check_vma=False
    )
```

```python
import functools

import jax
import jax.numpy as jnp
from jax import lax
from jax.experimental import pallas as pl
from jax.experimental.pallas import tpu as pltpu
from jax.sharding import PartitionSpec as P

CAP = 36
MAIN = 32
REST = CAP - MAIN
TILE = 256
LIMIT = 16
WAIT = 20 * 10**9
COST = 10**10
HALF = jnp.bfloat16
FULL = jnp.float32


def shape(dims, dtype=HALF):
    return jax.ShapeDtypeStruct(dims, dtype)


def params(mib):
    return pltpu.CompilerParams(vmem_limit_bytes=mib * 2**20)


def nt_dot(a, b):
    return lax.dot_general(a, b, (((1,), (1,)), ((), ())), preferred_element_type=FULL)


def tn_dot(a, b):
    return lax.dot_general(a, b, (((0,), (0,)), ((), ())), preferred_element_type=FULL)


def earlier_count(ids):
    count = ids.shape[1]
    chosen = jnp.max((ids == 0).astype(FULL), axis=0, keepdims=True)
    chosen = jnp.broadcast_to(chosen, (8, count))
    before = lax.broadcasted_iota(jnp.int32, (count, count), 0) < lax.broadcasted_iota(
        jnp.int32, (count, count), 1
    )
    slots = jnp.dot(
        chosen.astype(HALF), before.astype(FULL).astype(HALF), preferred_element_type=FULL
    )
    return chosen, slots


def one_hot(places, chosen, count):
    row = lax.broadcasted_iota(jnp.int32, (count, places.shape[1]), 0).astype(FULL)
    return jnp.where(row == places[0:1], jnp.broadcast_to(chosen[0:1], row.shape), 0.0)


def pack_kernel(ids_in, probs_in, tokens_in, cotangent_in, out, ids, probs, tokens, cotangent, done):
    pairs = ((ids_in, ids), (probs_in, probs), (tokens_in, tokens), (cotangent_in, cotangent))
    copies = [pltpu.make_async_copy(a, b, done.at[i]) for i, (a, b) in enumerate(pairs)]
    for copy in copies:
        copy.start()
    copies[0].wait()
    copies[1].wait()
    chosen, slots = earlier_count(ids[...])
    late = (slots >= MAIN).astype(FULL)
    pick_rows = one_hot(slots + late * MAIN, chosen, 80).astype(HALF)
    picked = one_hot(slots + MAIN + late * REST, chosen, 80)
    total = jnp.sum(jnp.where(ids[...] == 0, probs[...], 0.0), axis=0, keepdims=True)
    share = jnp.sum(picked * total, axis=1, keepdims=True)
    picked = picked.astype(HALF)
    copies[2].wait()
    copies[3].wait()
    width = out.shape[1]
    for i in range(0, width, 768):
        here = slice(i, i + 768)
        cotan = jnp.dot(picked, cotangent[:, here], preferred_element_type=FULL)
        rows = jnp.dot(pick_rows, tokens[:, here], preferred_element_type=FULL)
        out[:, here] = (rows + share * cotan)[0 : 2 * CAP].astype(HALF)


def pack(ids, probs, tokens, cotangent):
    values = (ids, probs, tokens, cotangent)
    return pl.pallas_call(
        pack_kernel,
        in_specs=[pl.BlockSpec(memory_space=pltpu.HBM)] * 4,
        out_shape=shape((2 * CAP, tokens.shape[1])),
        scratch_shapes=[pltpu.VMEM(v.shape, v.dtype) for v in values]
        + [pltpu.SemaphoreType.DMA((4,))],
        compiler_params=params(60),
        name="pack",
    )(*values)


def unpack_kernel(ids, *refs):
    pieces, out = refs[:-1], refs[-1]
    chosen, slots = earlier_count(ids[...])
    place = one_hot(slots, chosen, pieces[0].shape[0]).astype(HALF)
    total = pieces[0][...].astype(FULL)
    for piece in pieces[1:]:
        total = total + piece[...].astype(FULL)
    out[...] = tn_dot(place, total.astype(HALF)).astype(HALF)


def unpack(ids, pieces):
    count, (depth, width) = ids.shape[1], pieces[0].shape
    step = 1536
    return pl.pallas_call(
        unpack_kernel,
        grid=(width // step,),
        in_specs=[pl.BlockSpec(ids.shape, lambda j: (0, 0))]
        + [pl.BlockSpec((depth, step), lambda j: (0, j)) for _ in pieces],
        out_specs=pl.BlockSpec((count, step), lambda j: (0, j)),
        out_shape=shape((count, width)),
        compiler_params=params(32),
        name="unpack",
    )(ids, *pieces)


def padded_rows(n):
    return MAIN * n + -(-REST * n // 16) * 16


def assemble(blocks, rows, scaled):
    n, width = len(blocks), rows.shape[1]
    for i, block in enumerate(blocks):
        rows[MAIN * i : MAIN * (i + 1), :] = block[0:MAIN, :]
        scaled[MAIN * i : MAIN * (i + 1), :] = block[MAIN : 2 * MAIN, :]
    first = lax.broadcasted_iota(jnp.int32, (2 * REST, width), 0) < REST
    tails = [block[2 * MAIN : 2 * CAP, :].astype(FULL) for block in blocks]
    row_tails, scaled_tails = [], []
    for a, b in zip(tails[0::2], tails[1::2]):
        row_tails.append(jnp.where(first, a, pltpu.roll(b, REST, 0)))
        scaled_tails.append(jnp.where(first, pltpu.roll(a, REST, 0), b))
    if len(row_tails) % 2:
        row_tails.append(jnp.zeros((2 * REST, width), FULL))
        scaled_tails.append(jnp.zeros((2 * REST, width), FULL))
    for i in range(0, len(row_tails), 2):
        here = slice(MAIN * n + 8 * i, MAIN * n + 8 * i + 16)
        rows[here, :] = jnp.concatenate(row_tails[i : i + 2], axis=0).astype(HALF)
        scaled[here, :] = jnp.concatenate(scaled_tails[i : i + 2], axis=0).astype(HALF)


def activations(rows, scaled, gate, up, down):
    gate_pre = jnp.dot(rows, gate, preferred_element_type=FULL)
    up_pre = jnp.dot(rows, up, preferred_element_type=FULL)
    hidden_back = nt_dot(scaled, down)
    sigma = jax.nn.sigmoid(gate_pre)
    gate_act = gate_pre * sigma
    hidden = (gate_act * up_pre).astype(HALF)
    gate_back = (hidden_back * up_pre * sigma * (1.0 + gate_pre * (1.0 - sigma))).astype(HALF)
    up_back = (hidden_back * gate_act).astype(HALF)
    return hidden, gate_back, up_back


def forward_kernel(n, back, place, *refs):
    blocks, weights, refs = refs[:n], refs[n : n + 3], refs[n + 3 :]
    acts, own = refs[:2]
    refs = refs[2:]
    if back:
        send, keep = refs[:2]
        refs = refs[2:]
    rows, scaled = refs
    gate, up, down = weights
    width, part = rows.shape[1], own.shape[1] // 2
    assemble(blocks, rows, scaled)
    base = 3 * gate.shape[1]
    for out, start, index in ((own, 0, 0), (acts, base, 1)):
        columns = pl.ds(pl.multiple_of(place[index] * part, part), part)
        out[:, start : start + part] = rows[:, columns]
        out[:, start + part : start + 2 * part] = scaled[:, columns]
    tiles = gate.shape[1] // TILE
    for j in range(tiles):
        here = slice(TILE * j, TILE * (j + 1))
        found = activations(rows[...], scaled[...], gate[:, here], up[:, here], down[here, :])
        for k in range(3):
            at = TILE * (3 * j + k)
            acts[:, at : at + TILE] = found[k]
    if back:
        half = n // 2
        mid, tail, reach = MAIN * half, MAIN * n, 8 * (-(-half // 2))
        skip = 8 * half - reach
        gate_back = [acts[:, TILE * (3 * j + 1) : TILE * (3 * j + 2)] for j in range(tiles)]
        up_back = [acts[:, TILE * (3 * j + 2) : TILE * (3 * j + 3)] for j in range(tiles)]
        gate_back, up_back = jnp.concatenate(gate_back, axis=1), jnp.concatenate(up_back, axis=1)
        for i in range(0, width, 2 * TILE):
            here = slice(i, i + 2 * TILE)
            total = nt_dot(gate_back, gate[here, :]) + nt_dot(up_back, up[here, :])
            keep[0:mid, here] = total[0:mid].astype(HALF)
            send[0:mid, here] = total[mid : 2 * mid].astype(HALF)
            keep[mid : mid + reach, here] = total[tail : tail + reach].astype(HALF)
            send[mid : mid + reach, here] = total[tail + skip : tail + skip + reach].astype(HALF)


def forward(blocks, gate, up, down, place, part, back):
    n, (width, hidden) = len(blocks), gate.shape
    count = padded_rows(n)
    in_vmem = pl.BlockSpec(memory_space=pltpu.VMEM)
    out_shape = [
        shape((count, 3 * hidden + 2 * part)),
        shape((count, 2 * part)),
    ]
    if back:
        half = n // 2
        out_shape += [shape((MAIN * half + 8 * (-(-half // 2)), width))] * 2
    matmuls = 5 if back else 3
    return pl.pallas_call(
        functools.partial(forward_kernel, n, back),
        in_specs=[pl.BlockSpec(memory_space=pltpu.SMEM)] + [in_vmem] * (n + 3),
        out_specs=[in_vmem] * len(out_shape),
        out_shape=out_shape,
        scratch_shapes=[
            pltpu.VMEM((count, width), HALF),
            pltpu.VMEM((count, width), HALF),
        ],
        compiler_params=params(LIMIT),
        cost_estimate=pl.CostEstimate(flops=COST, bytes_accessed=0, transcendentals=0),
        name="forward_back" if back else "forward",
    )(place, *blocks, gate, up, down)


def grads_kernel(n, *refs):
    own, parts, came, refs = refs[:n], refs[n : 2 * n], refs[2 * n : 3 * n], refs[3 * n :]
    gate_grad, up_grad, down_grad, act_rows, part_rows = refs
    start, reach = 0, act_rows.shape[1]
    for mine, piece, other in zip(own, parts, came):
        count = mine.shape[0]
        here, there = slice(start, start + count), slice(start + count, start + 2 * count)
        act_rows[here, :] = mine[:, 0:reach]
        part_rows[here, :] = piece[...]
        act_rows[there, :] = other[:, 0:reach]
        part_rows[there, :] = other[:, reach:]
        start += 2 * count
    part = part_rows.shape[1] // 2
    tiles = act_rows.shape[1] // (3 * TILE)
    for i in range(part // TILE):
        picked = part_rows[:, i * TILE : (i + 1) * TILE].T
        here = slice(i * TILE, (i + 1) * TILE)
        for j in range(tiles):
            at = 3 * TILE * j
            there = slice(j * TILE, (j + 1) * TILE)
            gate_grad[here, there] = jnp.dot(
                picked, act_rows[:, at + TILE : at + 2 * TILE], preferred_element_type=FULL
            ).astype(HALF)
            up_grad[here, there] = jnp.dot(
                picked, act_rows[:, at + 2 * TILE : at + 3 * TILE], preferred_element_type=FULL
            ).astype(HALF)
    for j in range(tiles):
        at = 3 * TILE * j
        hidden = act_rows[:, at : at + TILE].T
        down_grad[j * TILE : (j + 1) * TILE, :] = jnp.dot(
            hidden, part_rows[:, part : 2 * part], preferred_element_type=FULL
        ).astype(HALF)


def grads(own, parts, came, hidden):
    n, count, part = len(own), 2 * sum(a.shape[0] for a in own), parts[0].shape[1] // 2
    in_vmem = pl.BlockSpec(memory_space=pltpu.VMEM)
    return pl.pallas_call(
        functools.partial(grads_kernel, n),
        in_specs=[in_vmem] * (3 * n),
        out_specs=[in_vmem] * 3,
        out_shape=[shape((part, hidden)), shape((part, hidden)), shape((hidden, part))],
        scratch_shapes=[
            pltpu.VMEM((count, 3 * hidden), HALF),
            pltpu.VMEM((count, 2 * part), HALF),
        ],
        compiler_params=params(24),
        cost_estimate=pl.CostEstimate(flops=COST, bytes_accessed=0, transcendentals=0),
        name="grads",
    )(*own, *parts, *came)


def settle_kernel(place, block, out):
    out[0] = place[0]
    out[1] = place[1]


def settle(place, block):
    in_smem = pl.BlockSpec(memory_space=pltpu.SMEM)
    return pl.pallas_call(
        settle_kernel,
        in_specs=[in_smem, pl.BlockSpec(memory_space=pl.ANY)],
        out_specs=in_smem,
        out_shape=shape((2,), jnp.int32),
        compiler_params=params(LIMIT),
        cost_estimate=pl.CostEstimate(
            flops=WAIT, bytes_accessed=0, transcendentals=0
        ),
        name="settle",
    )(place, block)


def merge_kernel(n, keep, came, *outs):
    mid = MAIN * n
    kept, other = keep[mid:, :].astype(FULL), came[mid:, :].astype(FULL)
    if n % 2:
        other = pltpu.roll(other, other.shape[0] - REST, 0)
    tails = kept + other
    for i, out in enumerate(outs):
        here = slice(MAIN * i, MAIN * (i + 1))
        out[0:MAIN, :] = (keep[here, :].astype(FULL) + came[here, :].astype(FULL)).astype(HALF)
        pair = tails[8 * (i // 2) : 8 * (i // 2) + 8]
        out[MAIN : MAIN + 8, :] = (pair if i % 2 == 0 else pltpu.roll(pair, REST, 0)).astype(HALF)


def merge(n, keep, came):
    return pl.pallas_call(
        functools.partial(merge_kernel, n),
        out_shape=[shape((MAIN + 8, keep.shape[1]))] * n,
        compiler_params=params(32),
        name="merge",
    )(keep, came)


def after(value, *others):
    return lax.optimization_barrier((value, *others))[0]


def per_device(tokens, cotangent, route_ids, route_probs, gate_weight, up_weight, down_weight):
    n_dp, n_expert = lax.axis_size("dp"), lax.axis_size("expert")
    core_pairs = [(i, i ^ 1) for i in range(n_dp)]
    y_pairs = [(i, (i + 2) % n_dp) for i in range(n_dp)]
    x_pairs = [(i, i ^ 1) for i in range(n_expert)]

    def over_core(v):
        return lax.ppermute(v, "dp", core_pairs)

    def over_y(v):
        return lax.ppermute(v, "dp", y_pairs)

    def over_x(v):
        return lax.ppermute(v, "expert", x_pairs)

    def over_z(v, by):
        return lax.ppermute(
            v, "expert", [(i, (i + 2 * by) % n_expert) for i in range(n_expert)]
        )

    part = tokens.shape[1] // n_dp
    p = lax.axis_index("dp")
    place = jnp.stack([p, p + 1 - 2 * (p % 2)]).astype(jnp.int32)
    ids, probs = route_ids.T, route_probs.T

    b0 = pack(ids, probs, tokens, cotangent)
    place = settle(place, b0)
    z1, x0, y0 = over_z(b0, 1), over_x(b0), over_y(b0)
    z3 = over_z(after(b0, place), -1)
    z1 = after(z1, x0, y0, place)
    z2, x1, y1 = over_z(z1, 1), over_x(z1), over_y(z1)
    xy0 = over_y(after(x0, z1))
    x3 = over_x(z3)
    x2 = over_x(after(z2, x1))
    xy1 = over_y(after(x1, z2))
    y2 = over_y(after(z2, x1))
    xy2 = over_y(x2)

    run = functools.partial(
        forward, gate=gate_weight, up=up_weight, down=down_weight, place=place, part=part
    )
    act0, own0, send0, keep0 = run([after(b0, xy0, z2), z1, x0, x1], back=True)
    came0 = over_x(send0)
    y3 = over_z(after(y0, send0), -1)
    act1, own1, send1, keep1 = run([after(z3, send0, y1), x3], back=True)
    came1 = over_x(send1)
    xy3 = over_z(after(xy0, send1), -1)
    other0 = over_core(after(act0, send1))
    act2, own2, send2, keep2 = run([after(z2, send1, xy1, y2, y3, came0), x2], back=True)
    p0, p1 = merge(2, keep0, after(came0, send2))
    came2, r1 = over_x(send2), over_z(p1, -1)
    other1 = over_core(after(act1, send2))
    y0 = after(y0, send2, p1, xy2, came1, other0)
    act3, own3 = run([y0, xy0, y1, xy1, y3, xy3], back=False)
    (p3,) = merge(1, keep1, after(came1, act3))
    (p2,) = merge(1, keep2, after(came2, act3))
    r3, r2 = over_z(p3, 1), over_z(p2, 2)
    other2, other3 = over_core(after(act2, act3)), over_core(act3)
    y2 = after(y2, act3, r1, other1, p2, p3)
    act4, own4 = run([y2, xy2], back=False)
    other4 = over_core(act4)
    act0 = after(act0, r3)
    gate_grad, up_grad, down_grad = grads(
        [act0, act1, act2, act3, act4],
        [own0, own1, own2, own3, own4],
        [other0, other1, other2, other3, other4],
        gate_weight.shape[1],
    )
    token_grad = unpack(after(ids, gate_grad), [p0, r1, r2, r3])
    return token_grad, gate_grad, up_grad, down_grad


def pick_rows(placer, values):
    return lax.dot_general(
        placer, values, (((0,), (0,)), ((), ())), preferred_element_type=jnp.float32
    ).astype(jnp.bfloat16)


def per_device_general(tokens, cotangent, route_ids, route_probs, gate_weight, up_weight, down_weight):
    hits = route_ids == 0
    chosen = jnp.any(hits, axis=1).astype(jnp.int32)
    share = jnp.sum(jnp.where(hits, route_probs, 0.0), axis=1)
    slots = jnp.cumsum(chosen) - chosen
    placer_mask = (slots[:, None] == jnp.arange(CAP, dtype=jnp.int32)[None, :]) & (
        chosen[:, None] == 1
    )
    placer = placer_mask.astype(jnp.float32)
    placer_half = placer_mask.astype(jnp.bfloat16)
    local_rows = pick_rows(placer_half, tokens)
    local_cotan = pick_rows(placer_half, cotangent)
    local_shares = jnp.sum(placer * share[:, None], axis=0)
    routed, routed_cotan, routed_shares = (
        lax.all_gather(local_rows, "expert", axis=0, tiled=True),
        lax.all_gather(local_cotan, "expert", axis=0, tiled=True),
        lax.all_gather(local_shares.astype(jnp.bfloat16), "expert", axis=0, tiled=True).astype(
            local_shares.dtype
        ),
    )
    gate_pre = jnp.dot(routed, gate_weight, preferred_element_type=jnp.float32)
    up_pre = jnp.dot(routed, up_weight, preferred_element_type=jnp.float32)
    sigma = jax.nn.sigmoid(gate_pre)
    gate_act = gate_pre * sigma
    hidden = (gate_act * up_pre).astype(jnp.bfloat16)
    gate_pre, up_pre, sigma, gate_act, hidden = (gate_pre, up_pre, sigma, gate_act, hidden)
    scaled = (routed_shares[:, None] * routed_cotan.astype(jnp.float32)).astype(jnp.bfloat16)
    down_part = lax.dot_general(
        hidden, scaled, (((0,), (0,)), ((), ())), preferred_element_type=jnp.float32
    )
    hidden_back = lax.dot_general(
        scaled, down_weight, (((1,), (1,)), ((), ())), preferred_element_type=jnp.float32
    )
    gate_back = (hidden_back * up_pre * sigma * (1.0 + gate_pre * (1.0 - sigma))).astype(
        jnp.bfloat16
    )
    up_back = (hidden_back * gate_act).astype(jnp.bfloat16)
    gate_part = lax.dot_general(
        routed, gate_back, (((0,), (0,)), ((), ())), preferred_element_type=jnp.float32
    )
    up_part = lax.dot_general(
        routed, up_back, (((0,), (0,)), ((), ())), preferred_element_type=jnp.float32
    )
    gate_sum, up_sum, down_sum = (
        lax.psum_scatter(
            gate_part.astype(jnp.bfloat16), "dp", scatter_dimension=0, tiled=True
        ).astype(jnp.float32),
        lax.psum_scatter(
            up_part.astype(jnp.bfloat16), "dp", scatter_dimension=0, tiled=True
        ).astype(jnp.float32),
        lax.psum_scatter(
            down_part.astype(jnp.bfloat16), "dp", scatter_dimension=1, tiled=True
        ).astype(jnp.float32),
    )
    partial_value = lax.dot_general(
        gate_back, gate_weight, (((1,), (1,)), ((), ())), preferred_element_type=jnp.float32
    )
    partial_value = partial_value + lax.dot_general(
        up_back, up_weight, (((1,), (1,)), ((), ())), preferred_element_type=jnp.float32
    )
    returned = lax.psum_scatter(
        partial_value.astype(jnp.bfloat16), "expert", scatter_dimension=0, tiled=True
    ).astype(jnp.float32)
    token_grad = jnp.dot(placer, returned, precision=lax.Precision.HIGHEST).astype(jnp.bfloat16)
    return (
        token_grad,
        gate_sum.astype(jnp.bfloat16),
        up_sum.astype(jnp.bfloat16),
        down_sum.astype(jnp.bfloat16),
    )


def solution(mesh):
    in_specs = (
        P(("dp", "expert"), None),
        P(("dp", "expert"), None),
        P(("dp", "expert"), None),
        P(("dp", "expert"), None),
        P(None, "expert"),
        P(None, "expert"),
        P("expert", None),
    )
    out_specs = (P(("dp", "expert"), None), P("dp", "expert"), P("dp", "expert"), P("expert", "dp"))
    fast = mesh.shape["dp"] == 4 and mesh.shape["expert"] == 8
    body = per_device if fast else per_device_general
    return jax.shard_map(
        body, mesh=mesh, in_specs=in_specs, out_specs=out_specs, check_vma=False
    )
```

```python
import functools

import jax
import jax.numpy as jnp
from jax import lax
from jax.experimental import pallas as pl
from jax.experimental.pallas import tpu as pltpu
from jax.sharding import PartitionSpec as P

CAP = 36
MAIN = 32
REST = CAP - MAIN
TILE = 256
LIMIT = 9
GRADS_LIMIT = 14
WAIT = 20 * 10**9
COST = 10**10
HALF = jnp.bfloat16
FULL = jnp.float32


def shape(dims, dtype=HALF):
    return jax.ShapeDtypeStruct(dims, dtype)


def params(mib):
    return pltpu.CompilerParams(vmem_limit_bytes=mib * 2**20)


def nt_dot(a, b):
    return lax.dot_general(a, b, (((1,), (1,)), ((), ())), preferred_element_type=FULL)


def tn_dot(a, b):
    return lax.dot_general(a, b, (((0,), (0,)), ((), ())), preferred_element_type=FULL)


def earlier_count(ids):
    count = ids.shape[1]
    chosen = jnp.max((ids == 0).astype(FULL), axis=0, keepdims=True)
    chosen = jnp.broadcast_to(chosen, (8, count))
    before = lax.broadcasted_iota(jnp.int32, (count, count), 0) < lax.broadcasted_iota(
        jnp.int32, (count, count), 1
    )
    slots = jnp.dot(
        chosen.astype(HALF), before.astype(FULL).astype(HALF), preferred_element_type=FULL
    )
    return chosen, slots


def one_hot(places, chosen, count):
    row = lax.broadcasted_iota(jnp.int32, (count, places.shape[1]), 0).astype(FULL)
    return jnp.where(row == places[0:1], jnp.broadcast_to(chosen[0:1], row.shape), 0.0)


def pack_kernel(ids_in, probs_in, tokens_in, cotangent_in, out, ids, probs, tokens, cotangent, done):
    pairs = ((ids_in, ids), (probs_in, probs), (tokens_in, tokens), (cotangent_in, cotangent))
    copies = [pltpu.make_async_copy(a, b, done.at[i]) for i, (a, b) in enumerate(pairs)]
    for copy in copies:
        copy.start()
    copies[0].wait()
    copies[1].wait()
    chosen, slots = earlier_count(ids[...])
    late = (slots >= MAIN).astype(FULL)
    pick_rows = one_hot(slots + late * MAIN, chosen, 80).astype(HALF)
    picked = one_hot(slots + MAIN + late * REST, chosen, 80)
    total = jnp.sum(jnp.where(ids[...] == 0, probs[...], 0.0), axis=0, keepdims=True)
    share = jnp.sum(picked * total, axis=1, keepdims=True)
    picked = picked.astype(HALF)
    copies[2].wait()
    copies[3].wait()
    width = out.shape[1]
    for i in range(0, width, 768):
        here = slice(i, i + 768)
        cotan = jnp.dot(picked, cotangent[:, here], preferred_element_type=FULL)
        rows = jnp.dot(pick_rows, tokens[:, here], preferred_element_type=FULL)
        out[:, here] = (rows + share * cotan)[0 : 2 * CAP].astype(HALF)


def pack(ids, probs, tokens, cotangent):
    values = (ids, probs, tokens, cotangent)
    return pl.pallas_call(
        pack_kernel,
        in_specs=[pl.BlockSpec(memory_space=pltpu.HBM)] * 4,
        out_shape=shape((2 * CAP, tokens.shape[1])),
        scratch_shapes=[pltpu.VMEM(v.shape, v.dtype) for v in values]
        + [pltpu.SemaphoreType.DMA((4,))],
        compiler_params=params(60),
        name="pack",
    )(*values)


def unpack_kernel(ids, *refs):
    pieces, out = refs[:-1], refs[-1]
    chosen, slots = earlier_count(ids[...])
    place = one_hot(slots, chosen, pieces[0].shape[0]).astype(HALF)
    total = pieces[0][...].astype(FULL)
    for piece in pieces[1:]:
        total = total + piece[...].astype(FULL)
    out[...] = tn_dot(place, total.astype(HALF)).astype(HALF)


def unpack(ids, pieces):
    count, (depth, width) = ids.shape[1], pieces[0].shape
    step = 1536
    return pl.pallas_call(
        unpack_kernel,
        grid=(width // step,),
        in_specs=[pl.BlockSpec(ids.shape, lambda j: (0, 0))]
        + [pl.BlockSpec((depth, step), lambda j: (0, j)) for _ in pieces],
        out_specs=pl.BlockSpec((count, step), lambda j: (0, j)),
        out_shape=shape((count, width)),
        compiler_params=params(32),
        name="unpack",
    )(ids, *pieces)


def padded_rows(n):
    return MAIN * n + -(-REST * n // 16) * 16


def assemble(blocks, rows, scaled):
    n, width = len(blocks), rows.shape[1]
    for i, block in enumerate(blocks):
        rows[MAIN * i : MAIN * (i + 1), :] = block[0:MAIN, :]
        scaled[MAIN * i : MAIN * (i + 1), :] = block[MAIN : 2 * MAIN, :]
    first = lax.broadcasted_iota(jnp.int32, (2 * REST, width), 0) < REST
    tails = [block[2 * MAIN : 2 * CAP, :].astype(FULL) for block in blocks]
    row_tails, scaled_tails = [], []
    for a, b in zip(tails[0::2], tails[1::2]):
        row_tails.append(jnp.where(first, a, pltpu.roll(b, REST, 0)))
        scaled_tails.append(jnp.where(first, pltpu.roll(a, REST, 0), b))
    if len(row_tails) % 2:
        row_tails.append(jnp.zeros((2 * REST, width), FULL))
        scaled_tails.append(jnp.zeros((2 * REST, width), FULL))
    for i in range(0, len(row_tails), 2):
        here = slice(MAIN * n + 8 * i, MAIN * n + 8 * i + 16)
        rows[here, :] = jnp.concatenate(row_tails[i : i + 2], axis=0).astype(HALF)
        scaled[here, :] = jnp.concatenate(scaled_tails[i : i + 2], axis=0).astype(HALF)


def activations(rows, scaled, gate, up, down):
    gate_pre = jnp.dot(rows, gate, preferred_element_type=FULL)
    up_pre = jnp.dot(rows, up, preferred_element_type=FULL)
    hidden_back = nt_dot(scaled, down)
    sigma = jax.nn.sigmoid(gate_pre)
    gate_act = gate_pre * sigma
    hidden = (gate_act * up_pre).astype(HALF)
    gate_back = (hidden_back * up_pre * sigma * (1.0 + gate_pre * (1.0 - sigma))).astype(HALF)
    up_back = (hidden_back * gate_act).astype(HALF)
    return hidden, gate_back, up_back


def forward_kernel(n, back, place, *refs):
    blocks, weights, refs = refs[:n], refs[n : n + 3], refs[n + 3 :]
    acts, own = refs[:2]
    refs = refs[2:]
    if back:
        send, keep = refs[:2]
        refs = refs[2:]
    rows, scaled = refs
    gate, up, down = weights
    width, part = rows.shape[1], own.shape[1] // 2
    assemble(blocks, rows, scaled)
    base = 3 * gate.shape[1]
    for out, start, index in ((own, 0, 0), (acts, base, 1)):
        columns = pl.ds(pl.multiple_of(place[index] * part, part), part)
        out[:, start : start + part] = rows[:, columns]
        out[:, start + part : start + 2 * part] = scaled[:, columns]
    tiles = gate.shape[1] // TILE
    for j in range(tiles):
        here = slice(TILE * j, TILE * (j + 1))
        found = activations(rows[...], scaled[...], gate[:, here], up[:, here], down[here, :])
        for k in range(3):
            at = TILE * (3 * j + k)
            acts[:, at : at + TILE] = found[k]
    if back:
        half = n // 2
        mid, tail, reach = MAIN * half, MAIN * n, 8 * (-(-half // 2))
        skip = 8 * half - reach
        gate_back = [acts[:, TILE * (3 * j + 1) : TILE * (3 * j + 2)] for j in range(tiles)]
        up_back = [acts[:, TILE * (3 * j + 2) : TILE * (3 * j + 3)] for j in range(tiles)]
        gate_back, up_back = jnp.concatenate(gate_back, axis=1), jnp.concatenate(up_back, axis=1)
        for i in range(0, width, 2 * TILE):
            here = slice(i, i + 2 * TILE)
            total = nt_dot(gate_back, gate[here, :]) + nt_dot(up_back, up[here, :])
            keep[0:mid, here] = total[0:mid].astype(HALF)
            send[0:mid, here] = total[mid : 2 * mid].astype(HALF)
            keep[mid : mid + reach, here] = total[tail : tail + reach].astype(HALF)
            send[mid : mid + reach, here] = total[tail + skip : tail + skip + reach].astype(HALF)


def forward(blocks, gate, up, down, place, part, back, cost=COST):
    n, (width, hidden) = len(blocks), gate.shape
    count = padded_rows(n)
    in_vmem = pl.BlockSpec(memory_space=pltpu.VMEM)
    out_shape = [
        shape((count, 3 * hidden + 2 * part)),
        shape((count, 2 * part)),
    ]
    if back:
        half = n // 2
        out_shape += [shape((MAIN * half + 8 * (-(-half // 2)), width))] * 2
    matmuls = 5 if back else 3
    return pl.pallas_call(
        functools.partial(forward_kernel, n, back),
        in_specs=[pl.BlockSpec(memory_space=pltpu.SMEM)] + [in_vmem] * (n + 3),
        out_specs=[in_vmem] * len(out_shape),
        out_shape=out_shape,
        scratch_shapes=[
            pltpu.VMEM((count, width), HALF),
            pltpu.VMEM((count, width), HALF),
        ],
        compiler_params=params(LIMIT),
        cost_estimate=pl.CostEstimate(flops=cost, bytes_accessed=0, transcendentals=0),
        name="forward_back" if back else "forward",
    )(place, *blocks, gate, up, down)


def grads_kernel(n, early, *refs):
    own, parts, came, refs = refs[:n], refs[n : 2 * n], refs[2 * n : 3 * n], refs[3 * n :]
    sums, refs = refs[:early], refs[early:]
    gate_grad, up_grad, down_grad, act_rows, part_rows = refs
    start, reach = 0, act_rows.shape[1]
    for mine, piece, other in zip(own, parts, came):
        count = mine.shape[0]
        here, there = slice(start, start + count), slice(start + count, start + 2 * count)
        act_rows[here, :] = mine[:, 0:reach]
        part_rows[here, :] = piece[...]
        act_rows[there, :] = other[:, 0:reach]
        part_rows[there, :] = other[:, reach:]
        start += 2 * count
    part = part_rows.shape[1] // 2
    tiles = act_rows.shape[1] // (3 * TILE)

    def put(k, out, rows, columns, value):
        if early:
            value = value + sums[k][rows, columns].astype(FULL)
        out[rows, columns] = value.astype(HALF)

    for i in range(part // TILE):
        picked = part_rows[:, i * TILE : (i + 1) * TILE].T
        here = slice(i * TILE, (i + 1) * TILE)
        for j in range(tiles):
            at = 3 * TILE * j
            there = slice(j * TILE, (j + 1) * TILE)
            gate_back = act_rows[:, at + TILE : at + 2 * TILE]
            up_back = act_rows[:, at + 2 * TILE : at + 3 * TILE]
            put(0, gate_grad, here, there, jnp.dot(picked, gate_back, preferred_element_type=FULL))
            put(1, up_grad, here, there, jnp.dot(picked, up_back, preferred_element_type=FULL))
    cotan = part_rows[:, part : 2 * part]
    for j in range(tiles):
        at = 3 * TILE * j
        hidden = act_rows[:, at : at + TILE].T
        here = slice(j * TILE, (j + 1) * TILE)
        value = jnp.dot(hidden, cotan, preferred_element_type=FULL)
        put(2, down_grad, here, slice(0, part), value)


def grads(own, parts, came, hidden, early=(), cost=COST):
    n, count, part = len(own), 2 * sum(a.shape[0] for a in own), parts[0].shape[1] // 2
    in_vmem = pl.BlockSpec(memory_space=pltpu.VMEM)
    return pl.pallas_call(
        functools.partial(grads_kernel, n, len(early)),
        in_specs=[in_vmem] * (3 * n + len(early)),
        out_specs=[in_vmem] * 3,
        out_shape=[shape((part, hidden)), shape((part, hidden)), shape((hidden, part))],
        scratch_shapes=[
            pltpu.VMEM((count, 3 * hidden), HALF),
            pltpu.VMEM((count, 2 * part), HALF),
        ],
        compiler_params=params(GRADS_LIMIT),
        cost_estimate=pl.CostEstimate(flops=cost, bytes_accessed=0, transcendentals=0),
        name="grads",
    )(*own, *parts, *came, *early)


def settle_kernel(place, block, out):
    out[0] = place[0]
    out[1] = place[1]


def settle(place, block):
    in_smem = pl.BlockSpec(memory_space=pltpu.SMEM)
    return pl.pallas_call(
        settle_kernel,
        in_specs=[in_smem, pl.BlockSpec(memory_space=pl.ANY)],
        out_specs=in_smem,
        out_shape=shape((2,), jnp.int32),
        compiler_params=params(LIMIT),
        cost_estimate=pl.CostEstimate(
            flops=WAIT, bytes_accessed=0, transcendentals=0
        ),
        name="settle",
    )(place, block)


def merge_kernel(n, keep, came, *outs):
    mid = MAIN * n
    kept, other = keep[mid:, :].astype(FULL), came[mid:, :].astype(FULL)
    if n % 2:
        other = pltpu.roll(other, other.shape[0] - REST, 0)
    tails = kept + other
    for i, out in enumerate(outs):
        here = slice(MAIN * i, MAIN * (i + 1))
        out[0:MAIN, :] = (keep[here, :].astype(FULL) + came[here, :].astype(FULL)).astype(HALF)
        pair = tails[8 * (i // 2) : 8 * (i // 2) + 8]
        out[MAIN : MAIN + 8, :] = (pair if i % 2 == 0 else pltpu.roll(pair, REST, 0)).astype(HALF)


def merge(n, keep, came):
    return pl.pallas_call(
        functools.partial(merge_kernel, n),
        out_shape=[shape((MAIN + 8, keep.shape[1]))] * n,
        compiler_params=params(32),
        name="merge",
    )(keep, came)


def after(value, *others):
    return lax.optimization_barrier((value, *others))[0]


def per_device(tokens, cotangent, route_ids, route_probs, gate_weight, up_weight, down_weight):
    n_dp, n_expert = lax.axis_size("dp"), lax.axis_size("expert")
    core_pairs = [(i, i ^ 1) for i in range(n_dp)]
    y_pairs = [(i, (i + 2) % n_dp) for i in range(n_dp)]
    x_pairs = [(i, i ^ 1) for i in range(n_expert)]

    def over_core(v):
        return lax.ppermute(v, "dp", core_pairs)

    def over_y(v):
        return lax.ppermute(v, "dp", y_pairs)

    def over_x(v):
        return lax.ppermute(v, "expert", x_pairs)

    def over_z(v, by):
        return lax.ppermute(
            v, "expert", [(i, (i + 2 * by) % n_expert) for i in range(n_expert)]
        )

    part = tokens.shape[1] // n_dp
    p = lax.axis_index("dp")
    place = jnp.stack([p, p + 1 - 2 * (p % 2)]).astype(jnp.int32)
    ids, probs = route_ids.T, route_probs.T

    b0 = pack(ids, probs, tokens, cotangent)
    place = settle(place, b0)
    z1, x0, y0 = over_z(b0, 1), over_x(b0), over_y(b0)
    z3 = over_z(after(b0, place), -1)
    z1 = after(z1, x0, y0, place)
    z2, x1, y1 = over_z(z1, 1), over_x(z1), over_y(z1)
    xy0 = over_y(after(x0, z1))
    x3 = over_x(z3)
    x2 = over_x(after(z2, x1))
    xy1 = over_y(after(x1, z2))
    y2 = over_y(after(z2, x1))
    xy2 = over_y(x2)

    run = functools.partial(
        forward, gate=gate_weight, up=up_weight, down=down_weight, place=place, part=part
    )
    act0, own0, send0, keep0 = run([after(b0, xy0, z2), z1, x0, x1], back=True)
    came0 = over_x(send0)
    y3 = over_z(after(y0, z2), -1)
    xy3 = over_z(after(xy0, send0), -1)
    act1, own1, send1, keep1 = run([after(z3, send0, y1, y3), x3], back=True)
    came1 = over_x(send1)
    other0 = over_core(after(act0, send1))
    p0, p1 = merge(2, keep0, came0)
    r1 = over_z(p1, -1)
    act2, own2, send2, keep2 = run([after(z2, send1, xy1, y2, xy3, p1), x2], back=True)
    (p3,) = merge(1, keep1, after(came1, send2))
    came2, r3 = over_x(send2), over_z(p3, 1)
    other1 = over_core(after(act1, send2))
    y0 = after(y0, send2, r1, p3, xy2, other0)
    act3, own3 = run([y0, xy0, y1, xy1, y3, xy3, y2, xy2], back=False)
    (p2,) = merge(1, keep2, after(came2, act3, r3, other1))
    r2 = over_z(p2, 2)
    other2, other3 = over_core(act2), over_core(act3)
    hidden = gate_weight.shape[1]
    early = grads([act0, act1, act2], [own0, own1, own2], [other0, other1, other2], hidden, cost=4 * COST)
    gate_grad, up_grad, down_grad = grads([act3], [own3], [other3], hidden, early, cost=10**6)
    token_grad = unpack(after(ids, gate_grad), [p0, r1, r2, r3])
    return token_grad, gate_grad, up_grad, down_grad


def pick_rows(placer, values):
    return lax.dot_general(
        placer, values, (((0,), (0,)), ((), ())), preferred_element_type=jnp.float32
    ).astype(jnp.bfloat16)


def per_device_general(tokens, cotangent, route_ids, route_probs, gate_weight, up_weight, down_weight):
    hits = route_ids == 0
    chosen = jnp.any(hits, axis=1).astype(jnp.int32)
    share = jnp.sum(jnp.where(hits, route_probs, 0.0), axis=1)
    slots = jnp.cumsum(chosen) - chosen
    placer_mask = (slots[:, None] == jnp.arange(CAP, dtype=jnp.int32)[None, :]) & (
        chosen[:, None] == 1
    )
    placer = placer_mask.astype(jnp.float32)
    placer_half = placer_mask.astype(jnp.bfloat16)
    local_rows = pick_rows(placer_half, tokens)
    local_cotan = pick_rows(placer_half, cotangent)
    local_shares = jnp.sum(placer * share[:, None], axis=0)
    routed, routed_cotan, routed_shares = (
        lax.all_gather(local_rows, "expert", axis=0, tiled=True),
        lax.all_gather(local_cotan, "expert", axis=0, tiled=True),
        lax.all_gather(local_shares.astype(jnp.bfloat16), "expert", axis=0, tiled=True).astype(
            local_shares.dtype
        ),
    )
    gate_pre = jnp.dot(routed, gate_weight, preferred_element_type=jnp.float32)
    up_pre = jnp.dot(routed, up_weight, preferred_element_type=jnp.float32)
    sigma = jax.nn.sigmoid(gate_pre)
    gate_act = gate_pre * sigma
    hidden = (gate_act * up_pre).astype(jnp.bfloat16)
    gate_pre, up_pre, sigma, gate_act, hidden = (gate_pre, up_pre, sigma, gate_act, hidden)
    scaled = (routed_shares[:, None] * routed_cotan.astype(jnp.float32)).astype(jnp.bfloat16)
    down_part = lax.dot_general(
        hidden, scaled, (((0,), (0,)), ((), ())), preferred_element_type=jnp.float32
    )
    hidden_back = lax.dot_general(
        scaled, down_weight, (((1,), (1,)), ((), ())), preferred_element_type=jnp.float32
    )
    gate_back = (hidden_back * up_pre * sigma * (1.0 + gate_pre * (1.0 - sigma))).astype(
        jnp.bfloat16
    )
    up_back = (hidden_back * gate_act).astype(jnp.bfloat16)
    gate_part = lax.dot_general(
        routed, gate_back, (((0,), (0,)), ((), ())), preferred_element_type=jnp.float32
    )
    up_part = lax.dot_general(
        routed, up_back, (((0,), (0,)), ((), ())), preferred_element_type=jnp.float32
    )
    gate_sum, up_sum, down_sum = (
        lax.psum_scatter(
            gate_part.astype(jnp.bfloat16), "dp", scatter_dimension=0, tiled=True
        ).astype(jnp.float32),
        lax.psum_scatter(
            up_part.astype(jnp.bfloat16), "dp", scatter_dimension=0, tiled=True
        ).astype(jnp.float32),
        lax.psum_scatter(
            down_part.astype(jnp.bfloat16), "dp", scatter_dimension=1, tiled=True
        ).astype(jnp.float32),
    )
    partial_value = lax.dot_general(
        gate_back, gate_weight, (((1,), (1,)), ((), ())), preferred_element_type=jnp.float32
    )
    partial_value = partial_value + lax.dot_general(
        up_back, up_weight, (((1,), (1,)), ((), ())), preferred_element_type=jnp.float32
    )
    returned = lax.psum_scatter(
        partial_value.astype(jnp.bfloat16), "expert", scatter_dimension=0, tiled=True
    ).astype(jnp.float32)
    token_grad = jnp.dot(placer, returned, precision=lax.Precision.HIGHEST).astype(jnp.bfloat16)
    return (
        token_grad,
        gate_sum.astype(jnp.bfloat16),
        up_sum.astype(jnp.bfloat16),
        down_sum.astype(jnp.bfloat16),
    )


def solution(mesh):
    in_specs = (
        P(("dp", "expert"), None),
        P(("dp", "expert"), None),
        P(("dp", "expert"), None),
        P(("dp", "expert"), None),
        P(None, "expert"),
        P(None, "expert"),
        P("expert", None),
    )
    out_specs = (P(("dp", "expert"), None), P("dp", "expert"), P("dp", "expert"), P("expert", "dp"))
    fast = mesh.shape["dp"] == 4 and mesh.shape["expert"] == 8
    body = per_device if fast else per_device_general
    return jax.shard_map(
        body, mesh=mesh, in_specs=in_specs, out_specs=out_specs, check_vma=False
    )
```

```python
import functools

import jax
import jax.numpy as jnp
from jax import lax
from jax.experimental import pallas as pl
from jax.experimental.pallas import tpu as pltpu
from jax.sharding import PartitionSpec as P

CAP = 36
MAIN = 32
REST = CAP - MAIN
TILE = 256
LIMIT = 9
GRADS_LIMIT = 14
WAIT = 20 * 10**9
COST = 10**10
COSTS = (10**10, 10**10, 10**6, 10**10, 4 * 10**10, 10**6)
HALF = jnp.bfloat16
FULL = jnp.float32


def shape(dims, dtype=HALF):
    return jax.ShapeDtypeStruct(dims, dtype)


def params(mib):
    return pltpu.CompilerParams(vmem_limit_bytes=mib * 2**20)


def nt_dot(a, b):
    return lax.dot_general(a, b, (((1,), (1,)), ((), ())), preferred_element_type=FULL)


def tn_dot(a, b):
    return lax.dot_general(a, b, (((0,), (0,)), ((), ())), preferred_element_type=FULL)


def earlier_count(ids):
    count = ids.shape[1]
    chosen = jnp.max((ids == 0).astype(FULL), axis=0, keepdims=True)
    chosen = jnp.broadcast_to(chosen, (8, count))
    before = lax.broadcasted_iota(jnp.int32, (count, count), 0) < lax.broadcasted_iota(
        jnp.int32, (count, count), 1
    )
    slots = jnp.dot(
        chosen.astype(HALF), before.astype(FULL).astype(HALF), preferred_element_type=FULL
    )
    return chosen, slots


def one_hot(places, chosen, count):
    row = lax.broadcasted_iota(jnp.int32, (count, places.shape[1]), 0).astype(FULL)
    return jnp.where(row == places[0:1], jnp.broadcast_to(chosen[0:1], row.shape), 0.0)


def pack_kernel(ids_in, probs_in, tokens_in, cotangent_in, out, ids, probs, tokens, cotangent, done):
    pairs = ((ids_in, ids), (probs_in, probs), (tokens_in, tokens), (cotangent_in, cotangent))
    copies = [pltpu.make_async_copy(a, b, done.at[i]) for i, (a, b) in enumerate(pairs)]
    for copy in copies:
        copy.start()
    copies[0].wait()
    copies[1].wait()
    chosen, slots = earlier_count(ids[...])
    late = (slots >= MAIN).astype(FULL)
    pick_rows = one_hot(slots + late * MAIN, chosen, 80).astype(HALF)
    picked = one_hot(slots + MAIN + late * REST, chosen, 80)
    total = jnp.sum(jnp.where(ids[...] == 0, probs[...], 0.0), axis=0, keepdims=True)
    share = jnp.sum(picked * total, axis=1, keepdims=True)
    picked = picked.astype(HALF)
    copies[2].wait()
    copies[3].wait()
    width = out.shape[1]
    for i in range(0, width, 768):
        here = slice(i, i + 768)
        cotan = jnp.dot(picked, cotangent[:, here], preferred_element_type=FULL)
        rows = jnp.dot(pick_rows, tokens[:, here], preferred_element_type=FULL)
        out[:, here] = (rows + share * cotan)[0 : 2 * CAP].astype(HALF)


def pack(ids, probs, tokens, cotangent):
    values = (ids, probs, tokens, cotangent)
    return pl.pallas_call(
        pack_kernel,
        in_specs=[pl.BlockSpec(memory_space=pltpu.HBM)] * 4,
        out_shape=shape((2 * CAP, tokens.shape[1])),
        scratch_shapes=[pltpu.VMEM(v.shape, v.dtype) for v in values]
        + [pltpu.SemaphoreType.DMA((4,))],
        compiler_params=params(60),
        name="pack",
    )(*values)


def unpack_kernel(ids, *refs):
    pieces, out = refs[:-1], refs[-1]
    chosen, slots = earlier_count(ids[...])
    place = one_hot(slots, chosen, pieces[0].shape[0]).astype(HALF)
    total = pieces[0][...].astype(FULL)
    for piece in pieces[1:]:
        total = total + piece[...].astype(FULL)
    out[...] = tn_dot(place, total.astype(HALF)).astype(HALF)


def unpack(ids, pieces):
    count, (depth, width) = ids.shape[1], pieces[0].shape
    step = 1536
    return pl.pallas_call(
        unpack_kernel,
        grid=(width // step,),
        in_specs=[pl.BlockSpec(ids.shape, lambda j: (0, 0))]
        + [pl.BlockSpec((depth, step), lambda j: (0, j)) for _ in pieces],
        out_specs=pl.BlockSpec((count, step), lambda j: (0, j)),
        out_shape=shape((count, width)),
        compiler_params=params(LIMIT),
        name="unpack",
    )(ids, *pieces)


def padded_rows(n):
    return MAIN * n + -(-REST * n // 16) * 16


def assemble(blocks, rows, scaled):
    n, width = len(blocks), rows.shape[1]
    for i, block in enumerate(blocks):
        rows[MAIN * i : MAIN * (i + 1), :] = block[0:MAIN, :]
        scaled[MAIN * i : MAIN * (i + 1), :] = block[MAIN : 2 * MAIN, :]
    first = lax.broadcasted_iota(jnp.int32, (2 * REST, width), 0) < REST
    tails = [block[2 * MAIN : 2 * CAP, :].astype(FULL) for block in blocks]
    row_tails, scaled_tails = [], []
    for a, b in zip(tails[0::2], tails[1::2]):
        row_tails.append(jnp.where(first, a, pltpu.roll(b, REST, 0)))
        scaled_tails.append(jnp.where(first, pltpu.roll(a, REST, 0), b))
    if len(row_tails) % 2:
        row_tails.append(jnp.zeros((2 * REST, width), FULL))
        scaled_tails.append(jnp.zeros((2 * REST, width), FULL))
    for i in range(0, len(row_tails), 2):
        here = slice(MAIN * n + 8 * i, MAIN * n + 8 * i + 16)
        rows[here, :] = jnp.concatenate(row_tails[i : i + 2], axis=0).astype(HALF)
        scaled[here, :] = jnp.concatenate(scaled_tails[i : i + 2], axis=0).astype(HALF)


def activations(rows, scaled, gate, up, down):
    gate_pre = jnp.dot(rows, gate, preferred_element_type=FULL)
    up_pre = jnp.dot(rows, up, preferred_element_type=FULL)
    hidden_back = nt_dot(scaled, down)
    sigma = jax.nn.sigmoid(gate_pre)
    gate_act = gate_pre * sigma
    hidden = (gate_act * up_pre).astype(HALF)
    gate_back = (hidden_back * up_pre * sigma * (1.0 + gate_pre * (1.0 - sigma))).astype(HALF)
    up_back = (hidden_back * gate_act).astype(HALF)
    return hidden, gate_back, up_back


def forward_kernel(n, back, place, *refs):
    arrays, weights, refs = refs[:n], refs[n : n + 3], refs[n + 3 :]
    blocks = []
    for array in arrays:
        blocks += [array] if len(array.shape) == 2 else [array.at[0], array.at[1]]
    n = len(blocks)
    acts, own = refs[:2]
    refs = refs[2:]
    if back == "halves":
        send, keep = refs[:2]
        refs = refs[2:]
    elif back == "pieces":
        pieces, refs = refs[:n], refs[n:]
    rows, scaled = refs
    gate, up, down = weights
    width, part = rows.shape[1], own.shape[1] // 2
    assemble(blocks, rows, scaled)
    base = 3 * gate.shape[1]
    for out, start, index in ((own, 0, 0), (acts, base, 1)):
        columns = pl.ds(pl.multiple_of(place[index] * part, part), part)
        out[:, start : start + part] = rows[:, columns]
        out[:, start + part : start + 2 * part] = scaled[:, columns]
    tiles = gate.shape[1] // TILE
    for j in range(tiles):
        here = slice(TILE * j, TILE * (j + 1))
        found = activations(rows[...], scaled[...], gate[:, here], up[:, here], down[here, :])
        for k in range(3):
            at = TILE * (3 * j + k)
            acts[:, at : at + TILE] = found[k]
    if back:
        half = n // 2
        mid, tail, reach = MAIN * half, MAIN * n, 8 * (-(-half // 2))
        skip = 8 * half - reach
        gate_back = [acts[:, TILE * (3 * j + 1) : TILE * (3 * j + 2)] for j in range(tiles)]
        up_back = [acts[:, TILE * (3 * j + 2) : TILE * (3 * j + 3)] for j in range(tiles)]
        gate_back, up_back = jnp.concatenate(gate_back, axis=1), jnp.concatenate(up_back, axis=1)
        for i in range(0, width, 2 * TILE):
            here = slice(i, i + 2 * TILE)
            total = nt_dot(gate_back, gate[here, :]) + nt_dot(up_back, up[here, :])
            if back == "pieces":
                for k, piece in enumerate(pieces):
                    piece[0:MAIN, here] = total[MAIN * k : MAIN * (k + 1)].astype(HALF)
                    pair = total[tail + 8 * (k // 2) : tail + 8 * (k // 2) + 8]
                    pair = pair if k % 2 == 0 else pltpu.roll(pair, REST, 0)
                    piece[MAIN : MAIN + 8, here] = pair.astype(HALF)
                continue
            keep[0:mid, here] = total[0:mid].astype(HALF)
            send[0:mid, here] = total[mid : 2 * mid].astype(HALF)
            keep[mid : mid + reach, here] = total[tail : tail + reach].astype(HALF)
            send[mid : mid + reach, here] = total[tail + skip : tail + skip + reach].astype(HALF)


def forward(blocks, gate, up, down, place, part, back, cost=COST):
    given, (width, hidden) = len(blocks), gate.shape
    n = sum(1 if len(block.shape) == 2 else 2 for block in blocks)
    count = padded_rows(n)
    in_vmem = pl.BlockSpec(memory_space=pltpu.VMEM)
    out_shape = [
        shape((count, 3 * hidden + 2 * part)),
        shape((count, 2 * part)),
    ]
    if back == "pieces":
        out_shape += [shape((MAIN + 8, width))] * n
    elif back:
        half = n // 2
        out_shape += [shape((MAIN * half + 8 * (-(-half // 2)), width))] * 2
    matmuls = 5 if back else 3
    return pl.pallas_call(
        functools.partial(forward_kernel, given, back),
        in_specs=[pl.BlockSpec(memory_space=pltpu.SMEM)] + [in_vmem] * (given + 3),
        out_specs=[in_vmem] * len(out_shape),
        out_shape=out_shape,
        scratch_shapes=[
            pltpu.VMEM((count, width), HALF),
            pltpu.VMEM((count, width), HALF),
        ],
        compiler_params=params(LIMIT),
        cost_estimate=pl.CostEstimate(flops=cost, bytes_accessed=0, transcendentals=0),
        name="forward_back" if back else "forward",
    )(place, *blocks, gate, up, down)


def grads_kernel(n, early, *refs):
    own, parts, came, refs = refs[:n], refs[n : 2 * n], refs[2 * n : 3 * n], refs[3 * n :]
    sums, refs = refs[:early], refs[early:]
    gate_grad, up_grad, down_grad, act_rows, part_rows = refs
    start, reach = 0, act_rows.shape[1]
    for mine, piece, other in zip(own, parts, came):
        count = mine.shape[0]
        here, there = slice(start, start + count), slice(start + count, start + 2 * count)
        act_rows[here, :] = mine[:, 0:reach]
        part_rows[here, :] = piece[...]
        act_rows[there, :] = other[:, 0:reach]
        part_rows[there, :] = other[:, reach:]
        start += 2 * count
    part = part_rows.shape[1] // 2
    tiles = act_rows.shape[1] // (3 * TILE)

    def put(k, out, rows, columns, value):
        if early:
            value = value + sums[k][rows, columns].astype(FULL)
        out[rows, columns] = value.astype(HALF)

    for i in range(part // TILE):
        picked = part_rows[:, i * TILE : (i + 1) * TILE].T
        here = slice(i * TILE, (i + 1) * TILE)
        for j in range(tiles):
            at = 3 * TILE * j
            there = slice(j * TILE, (j + 1) * TILE)
            gate_back = act_rows[:, at + TILE : at + 2 * TILE]
            up_back = act_rows[:, at + 2 * TILE : at + 3 * TILE]
            put(0, gate_grad, here, there, jnp.dot(picked, gate_back, preferred_element_type=FULL))
            put(1, up_grad, here, there, jnp.dot(picked, up_back, preferred_element_type=FULL))
    cotan = part_rows[:, part : 2 * part]
    for j in range(tiles):
        at = 3 * TILE * j
        hidden = act_rows[:, at : at + TILE].T
        here = slice(j * TILE, (j + 1) * TILE)
        value = jnp.dot(hidden, cotan, preferred_element_type=FULL)
        put(2, down_grad, here, slice(0, part), value)


def grads(own, parts, came, hidden, early=(), cost=COST):
    n, count, part = len(own), 2 * sum(a.shape[0] for a in own), parts[0].shape[1] // 2
    in_vmem = pl.BlockSpec(memory_space=pltpu.VMEM)
    return pl.pallas_call(
        functools.partial(grads_kernel, n, len(early)),
        in_specs=[in_vmem] * (3 * n + len(early)),
        out_specs=[in_vmem] * 3,
        out_shape=[shape((part, hidden)), shape((part, hidden)), shape((hidden, part))],
        scratch_shapes=[
            pltpu.VMEM((count, 3 * hidden), HALF),
            pltpu.VMEM((count, 2 * part), HALF),
        ],
        compiler_params=params(GRADS_LIMIT),
        cost_estimate=pl.CostEstimate(flops=cost, bytes_accessed=0, transcendentals=0),
        name="grads",
    )(*own, *parts, *came, *early)


def settle_kernel(place, block, out):
    out[0] = place[0]
    out[1] = place[1]


def settle(place, block):
    in_smem = pl.BlockSpec(memory_space=pltpu.SMEM)
    return pl.pallas_call(
        settle_kernel,
        in_specs=[in_smem, pl.BlockSpec(memory_space=pl.ANY)],
        out_specs=in_smem,
        out_shape=shape((2,), jnp.int32),
        compiler_params=params(LIMIT),
        cost_estimate=pl.CostEstimate(
            flops=WAIT, bytes_accessed=0, transcendentals=0
        ),
        name="settle",
    )(place, block)


def merge_kernel(n, keep, came, *outs):
    mid = MAIN * n
    kept, other = keep[mid:, :].astype(FULL), came[mid:, :].astype(FULL)
    if n % 2:
        other = pltpu.roll(other, other.shape[0] - REST, 0)
    tails = kept + other
    for i, out in enumerate(outs):
        here = slice(MAIN * i, MAIN * (i + 1))
        out[0:MAIN, :] = (keep[here, :].astype(FULL) + came[here, :].astype(FULL)).astype(HALF)
        pair = tails[8 * (i // 2) : 8 * (i // 2) + 8]
        out[MAIN : MAIN + 8, :] = (pair if i % 2 == 0 else pltpu.roll(pair, REST, 0)).astype(HALF)


def merge(n, keep, came):
    return pl.pallas_call(
        functools.partial(merge_kernel, n),
        out_shape=[shape((MAIN + 8, keep.shape[1]))] * n,
        compiler_params=params(LIMIT),
        name="merge",
    )(keep, came)


def pair_kernel(a, b, out):
    out[0] = a[...]
    out[1] = b[...]


def pair(a, b):
    return pl.pallas_call(
        pair_kernel,
        out_shape=shape((2,) + a.shape),
        compiler_params=params(LIMIT),
        cost_estimate=pl.CostEstimate(flops=10**6, bytes_accessed=0, transcendentals=0),
        name="pair",
    )(a, b)


def add_kernel(a, b, out):
    out[...] = (a[...].astype(FULL) + b[...].astype(FULL)).astype(HALF)


def add(a, b):
    return pl.pallas_call(
        add_kernel, out_shape=shape(a.shape), compiler_params=params(LIMIT), name="add"
    )(a, b)


def after(value, *others):
    return lax.optimization_barrier((value, *others))[0]


def per_device(tokens, cotangent, route_ids, route_probs, gate_weight, up_weight, down_weight):
    n_dp, n_expert = lax.axis_size("dp"), lax.axis_size("expert")
    core_pairs = [(i, i ^ 1) for i in range(n_dp)]
    y_pairs = [(i, (i + 2) % n_dp) for i in range(n_dp)]
    x_pairs = [(i, i ^ 1) for i in range(n_expert)]

    def over_core(v):
        return lax.ppermute(v, "dp", core_pairs)

    def over_y(v):
        return lax.ppermute(v, "dp", y_pairs)

    def over_x(v):
        return lax.ppermute(v, "expert", x_pairs)

    def over_z(v, by):
        return lax.ppermute(
            v, "expert", [(i, (i + 2 * by) % n_expert) for i in range(n_expert)]
        )

    part = tokens.shape[1] // n_dp
    p = lax.axis_index("dp")
    place = jnp.stack([p, p + 1 - 2 * (p % 2)]).astype(jnp.int32)
    ids, probs = route_ids.T, route_probs.T

    b0 = pack(ids, probs, tokens, cotangent)
    place = settle(place, b0)
    z1, x0, y0 = over_z(b0, 1), over_x(b0), over_y(b0)
    z3 = over_z(after(b0, place), -1)
    z1 = after(z1, x0, y0, place)
    z2, x1, y1 = over_z(z1, 1), over_x(z1), over_y(z1)
    xy0 = over_y(after(x0, z1))
    x3 = over_x(z3)
    x2 = over_x(after(z2, x1))
    xy1 = over_y(x1)
    y2 = over_y(after(z2, x1))
    xy2 = over_y(x2)
    y3 = over_z(after(y0, z2), -1)

    run = functools.partial(
        forward, gate=gate_weight, up=up_weight, down=down_weight, place=place, part=part
    )
    act0, own0, send0, keep0 = run(
        [after(z1, xy0, z2, y1), z3, x1, x3], back="halves", cost=COSTS[0]
    )
    came0 = over_x(send0)
    xy3 = over_z(after(xy0, send0), -1)
    act1, own1, keep2, near, send2, aside = run(
        [after(z2, send0, xy1, y3), b0, x2, x0], back="pieces", cost=COSTS[1]
    )
    came2 = over_x(send2)
    other0 = over_core(act0)
    p1, p3 = merge(2, keep0, after(came0, send2))
    r1, r3 = over_z(p1, -1), over_z(p3, 1)
    other1 = over_core(act1)
    y0 = after(y0, p1, other0, y2, xy3)
    act2, own2 = run([y0, xy0, y1, xy1], back=False, cost=COSTS[2])
    other2 = over_core(act2)
    y2 = after(y2, act2)
    act3, own3 = run([y2, xy2, y3, xy3], back=False, cost=COSTS[3])
    other3 = over_core(act3)
    p2 = add(keep2, after(came2, act3, r1, r3))
    r2 = over_z(p2, 2)
    beside = over_x(after(aside, act3))
    hidden = gate_weight.shape[1]
    early = grads([act0, act1], [own0, own1], [other0, other1], hidden, cost=COSTS[4])
    gate_grad, up_grad, down_grad = grads(
        [act2, act3], [own2, own3], [other2, other3], hidden, early, cost=COSTS[5]
    )
    token_grad = unpack(after(ids, gate_grad), [near, beside, r1, r2, r3])
    return token_grad, gate_grad, up_grad, down_grad


def pick_rows(placer, values):
    return lax.dot_general(
        placer, values, (((0,), (0,)), ((), ())), preferred_element_type=jnp.float32
    ).astype(jnp.bfloat16)


def per_device_general(tokens, cotangent, route_ids, route_probs, gate_weight, up_weight, down_weight):
    hits = route_ids == 0
    chosen = jnp.any(hits, axis=1).astype(jnp.int32)
    share = jnp.sum(jnp.where(hits, route_probs, 0.0), axis=1)
    slots = jnp.cumsum(chosen) - chosen
    placer_mask = (slots[:, None] == jnp.arange(CAP, dtype=jnp.int32)[None, :]) & (
        chosen[:, None] == 1
    )
    placer = placer_mask.astype(jnp.float32)
    placer_half = placer_mask.astype(jnp.bfloat16)
    local_rows = pick_rows(placer_half, tokens)
    local_cotan = pick_rows(placer_half, cotangent)
    local_shares = jnp.sum(placer * share[:, None], axis=0)
    routed, routed_cotan, routed_shares = (
        lax.all_gather(local_rows, "expert", axis=0, tiled=True),
        lax.all_gather(local_cotan, "expert", axis=0, tiled=True),
        lax.all_gather(local_shares.astype(jnp.bfloat16), "expert", axis=0, tiled=True).astype(
            local_shares.dtype
        ),
    )
    gate_pre = jnp.dot(routed, gate_weight, preferred_element_type=jnp.float32)
    up_pre = jnp.dot(routed, up_weight, preferred_element_type=jnp.float32)
    sigma = jax.nn.sigmoid(gate_pre)
    gate_act = gate_pre * sigma
    hidden = (gate_act * up_pre).astype(jnp.bfloat16)
    gate_pre, up_pre, sigma, gate_act, hidden = (gate_pre, up_pre, sigma, gate_act, hidden)
    scaled = (routed_shares[:, None] * routed_cotan.astype(jnp.float32)).astype(jnp.bfloat16)
    down_part = lax.dot_general(
        hidden, scaled, (((0,), (0,)), ((), ())), preferred_element_type=jnp.float32
    )
    hidden_back = lax.dot_general(
        scaled, down_weight, (((1,), (1,)), ((), ())), preferred_element_type=jnp.float32
    )
    gate_back = (hidden_back * up_pre * sigma * (1.0 + gate_pre * (1.0 - sigma))).astype(
        jnp.bfloat16
    )
    up_back = (hidden_back * gate_act).astype(jnp.bfloat16)
    gate_part = lax.dot_general(
        routed, gate_back, (((0,), (0,)), ((), ())), preferred_element_type=jnp.float32
    )
    up_part = lax.dot_general(
        routed, up_back, (((0,), (0,)), ((), ())), preferred_element_type=jnp.float32
    )
    gate_sum, up_sum, down_sum = (
        lax.psum_scatter(
            gate_part.astype(jnp.bfloat16), "dp", scatter_dimension=0, tiled=True
        ).astype(jnp.float32),
        lax.psum_scatter(
            up_part.astype(jnp.bfloat16), "dp", scatter_dimension=0, tiled=True
        ).astype(jnp.float32),
        lax.psum_scatter(
            down_part.astype(jnp.bfloat16), "dp", scatter_dimension=1, tiled=True
        ).astype(jnp.float32),
    )
    partial_value = lax.dot_general(
        gate_back, gate_weight, (((1,), (1,)), ((), ())), preferred_element_type=jnp.float32
    )
    partial_value = partial_value + lax.dot_general(
        up_back, up_weight, (((1,), (1,)), ((), ())), preferred_element_type=jnp.float32
    )
    returned = lax.psum_scatter(
        partial_value.astype(jnp.bfloat16), "expert", scatter_dimension=0, tiled=True
    ).astype(jnp.float32)
    token_grad = jnp.dot(placer, returned, precision=lax.Precision.HIGHEST).astype(jnp.bfloat16)
    return (
        token_grad,
        gate_sum.astype(jnp.bfloat16),
        up_sum.astype(jnp.bfloat16),
        down_sum.astype(jnp.bfloat16),
    )


def solution(mesh):
    in_specs = (
        P(("dp", "expert"), None),
        P(("dp", "expert"), None),
        P(("dp", "expert"), None),
        P(("dp", "expert"), None),
        P(None, "expert"),
        P(None, "expert"),
        P("expert", None),
    )
    out_specs = (P(("dp", "expert"), None), P("dp", "expert"), P("dp", "expert"), P("expert", "dp"))
    fast = mesh.shape["dp"] == 4 and mesh.shape["expert"] == 8
    body = per_device if fast else per_device_general
    return jax.shard_map(
        body, mesh=mesh, in_specs=in_specs, out_specs=out_specs, check_vma=False
    )
```

```python
import functools

import jax
import jax.numpy as jnp
from jax import lax
from jax.experimental import pallas as pl
from jax.experimental.pallas import tpu as pltpu
from jax.sharding import PartitionSpec as P

CAP = 36
MAIN = 32
REST = CAP - MAIN
TILE = 256
LIMIT = 9
GRADS_LIMIT = 14
WAIT = 20 * 10**9
COST = 10**10
COSTS = (10**10, 10**10, 10**6, 10**10, 4 * 10**10, 10**6)
HALF = jnp.bfloat16
FULL = jnp.float32


def shape(dims, dtype=HALF):
    return jax.ShapeDtypeStruct(dims, dtype)


def params(mib):
    return pltpu.CompilerParams(vmem_limit_bytes=mib * 2**20)


def nt_dot(a, b):
    return lax.dot_general(a, b, (((1,), (1,)), ((), ())), preferred_element_type=FULL)


def tn_dot(a, b):
    return lax.dot_general(a, b, (((0,), (0,)), ((), ())), preferred_element_type=FULL)


def earlier_count(ids):
    count = ids.shape[1]
    chosen = jnp.max((ids == 0).astype(FULL), axis=0, keepdims=True)
    chosen = jnp.broadcast_to(chosen, (8, count))
    before = lax.broadcasted_iota(jnp.int32, (count, count), 0) < lax.broadcasted_iota(
        jnp.int32, (count, count), 1
    )
    slots = jnp.dot(
        chosen.astype(HALF), before.astype(FULL).astype(HALF), preferred_element_type=FULL
    )
    return chosen, slots


def one_hot(places, chosen, count):
    row = lax.broadcasted_iota(jnp.int32, (count, places.shape[1]), 0).astype(FULL)
    return jnp.where(row == places[0:1], jnp.broadcast_to(chosen[0:1], row.shape), 0.0)


def pack_kernel(ids_in, probs_in, tokens_in, cotangent_in, out, ids, probs, tokens, cotangent, done):
    pairs = ((ids_in, ids), (probs_in, probs), (tokens_in, tokens), (cotangent_in, cotangent))
    copies = [pltpu.make_async_copy(a, b, done.at[i]) for i, (a, b) in enumerate(pairs)]
    for copy in copies:
        copy.start()
    copies[0].wait()
    copies[1].wait()
    chosen, slots = earlier_count(ids[...])
    late = (slots >= MAIN).astype(FULL)
    pick_rows = one_hot(slots + late * MAIN, chosen, 80).astype(HALF)
    picked = one_hot(slots + MAIN + late * REST, chosen, 80)
    total = jnp.sum(jnp.where(ids[...] == 0, probs[...], 0.0), axis=0, keepdims=True)
    share = jnp.sum(picked * total, axis=1, keepdims=True)
    picked = picked.astype(HALF)
    copies[2].wait()
    copies[3].wait()
    width = out.shape[1]
    for i in range(0, width, 768):
        here = slice(i, i + 768)
        cotan = jnp.dot(picked, cotangent[:, here], preferred_element_type=FULL)
        rows = jnp.dot(pick_rows, tokens[:, here], preferred_element_type=FULL)
        out[:, here] = (rows + share * cotan)[0 : 2 * CAP].astype(HALF)


def pack(ids, probs, tokens, cotangent):
    values = (ids, probs, tokens, cotangent)
    return pl.pallas_call(
        pack_kernel,
        in_specs=[pl.BlockSpec(memory_space=pltpu.HBM)] * 4,
        out_shape=shape((2 * CAP, tokens.shape[1])),
        scratch_shapes=[pltpu.VMEM(v.shape, v.dtype) for v in values]
        + [pltpu.SemaphoreType.DMA((4,))],
        compiler_params=params(60),
        name="pack",
    )(*values)


def unpack_kernel(ids, *refs):
    pieces, out = refs[:-1], refs[-1]
    chosen, slots = earlier_count(ids[...])
    place = one_hot(slots, chosen, pieces[0].shape[0]).astype(HALF)
    total = pieces[0][...].astype(FULL)
    for piece in pieces[1:]:
        total = total + piece[...].astype(FULL)
    out[...] = tn_dot(place, total.astype(HALF)).astype(HALF)


def unpack(ids, pieces):
    count, (depth, width) = ids.shape[1], pieces[0].shape
    step = 1536
    return pl.pallas_call(
        unpack_kernel,
        grid=(width // step,),
        in_specs=[pl.BlockSpec(ids.shape, lambda j: (0, 0))]
        + [pl.BlockSpec((depth, step), lambda j: (0, j)) for _ in pieces],
        out_specs=pl.BlockSpec((count, step), lambda j: (0, j)),
        out_shape=shape((count, width)),
        compiler_params=params(LIMIT),
        name="unpack",
    )(ids, *pieces)


def padded_rows(n):
    return MAIN * n + -(-REST * n // 16) * 16


def assemble(blocks, rows, scaled):
    n, width = len(blocks), rows.shape[1]
    for i, block in enumerate(blocks):
        rows[MAIN * i : MAIN * (i + 1), :] = block[0:MAIN, :]
        scaled[MAIN * i : MAIN * (i + 1), :] = block[MAIN : 2 * MAIN, :]
    first = lax.broadcasted_iota(jnp.int32, (2 * REST, width), 0) < REST
    tails = [block[2 * MAIN : 2 * CAP, :].astype(FULL) for block in blocks]
    row_tails, scaled_tails = [], []
    for a, b in zip(tails[0::2], tails[1::2]):
        row_tails.append(jnp.where(first, a, pltpu.roll(b, REST, 0)))
        scaled_tails.append(jnp.where(first, pltpu.roll(a, REST, 0), b))
    if len(row_tails) % 2:
        row_tails.append(jnp.zeros((2 * REST, width), FULL))
        scaled_tails.append(jnp.zeros((2 * REST, width), FULL))
    for i in range(0, len(row_tails), 2):
        here = slice(MAIN * n + 8 * i, MAIN * n + 8 * i + 16)
        rows[here, :] = jnp.concatenate(row_tails[i : i + 2], axis=0).astype(HALF)
        scaled[here, :] = jnp.concatenate(scaled_tails[i : i + 2], axis=0).astype(HALF)


def activations(rows, scaled, gate, up, down):
    gate_pre = jnp.dot(rows, gate, preferred_element_type=FULL)
    up_pre = jnp.dot(rows, up, preferred_element_type=FULL)
    hidden_back = nt_dot(scaled, down)
    sigma = jax.nn.sigmoid(gate_pre)
    gate_act = gate_pre * sigma
    hidden = (gate_act * up_pre).astype(HALF)
    gate_back = (hidden_back * up_pre * sigma * (1.0 + gate_pre * (1.0 - sigma))).astype(HALF)
    up_back = (hidden_back * gate_act).astype(HALF)
    return hidden, gate_back, up_back


def forward_kernel(n, back, place, *refs):
    arrays, weights, refs = refs[:n], refs[n : n + 3], refs[n + 3 :]
    blocks = []
    for array in arrays:
        blocks += [array] if len(array.shape) == 2 else [array.at[0], array.at[1]]
    n = len(blocks)
    acts, own = refs[:2]
    refs = refs[2:]
    if back == "halves":
        send, keep = refs[:2]
        refs = refs[2:]
    elif back == "pieces":
        pieces, refs = refs[:n], refs[n:]
    rows, scaled = refs
    gate, up, down = weights
    width, part = rows.shape[1], own.shape[1] // 2
    assemble(blocks, rows, scaled)
    base = 3 * gate.shape[1]
    for out, start, index in ((own, 0, 0), (acts, base, 1)):
        columns = pl.ds(pl.multiple_of(place[index] * part, part), part)
        out[:, start : start + part] = rows[:, columns]
        out[:, start + part : start + 2 * part] = scaled[:, columns]
    tiles = gate.shape[1] // TILE
    for j in range(tiles):
        here = slice(TILE * j, TILE * (j + 1))
        found = activations(rows[...], scaled[...], gate[:, here], up[:, here], down[here, :])
        for k in range(3):
            at = TILE * (3 * j + k)
            acts[:, at : at + TILE] = found[k]
    if back:
        half = n // 2
        mid, tail, reach = MAIN * half, MAIN * n, 8 * (-(-half // 2))
        skip = 8 * half - reach
        gate_back = [acts[:, TILE * (3 * j + 1) : TILE * (3 * j + 2)] for j in range(tiles)]
        up_back = [acts[:, TILE * (3 * j + 2) : TILE * (3 * j + 3)] for j in range(tiles)]
        gate_back, up_back = jnp.concatenate(gate_back, axis=1), jnp.concatenate(up_back, axis=1)
        for i in range(0, width, 2 * TILE):
            here = slice(i, i + 2 * TILE)
            total = nt_dot(gate_back, gate[here, :]) + nt_dot(up_back, up[here, :])
            if back == "pieces":
                for k, piece in enumerate(pieces):
                    piece[0:MAIN, here] = total[MAIN * k : MAIN * (k + 1)].astype(HALF)
                    pair = total[tail + 8 * (k // 2) : tail + 8 * (k // 2) + 8]
                    pair = pair if k % 2 == 0 else pltpu.roll(pair, REST, 0)
                    piece[MAIN : MAIN + 8, here] = pair.astype(HALF)
                continue
            keep[0:mid, here] = total[0:mid].astype(HALF)
            send[0:mid, here] = total[mid : 2 * mid].astype(HALF)
            keep[mid : mid + reach, here] = total[tail : tail + reach].astype(HALF)
            send[mid : mid + reach, here] = total[tail + skip : tail + skip + reach].astype(HALF)


def forward(blocks, gate, up, down, place, part, back, cost=COST):
    given, (width, hidden) = len(blocks), gate.shape
    n = sum(1 if len(block.shape) == 2 else 2 for block in blocks)
    count = padded_rows(n)
    in_vmem = pl.BlockSpec(memory_space=pltpu.VMEM)
    out_shape = [
        shape((count, 3 * hidden + 2 * part)),
        shape((count, 2 * part)),
    ]
    if back == "pieces":
        out_shape += [shape((MAIN + 8, width))] * n
    elif back:
        half = n // 2
        out_shape += [shape((MAIN * half + 8 * (-(-half // 2)), width))] * 2
    matmuls = 5 if back else 3
    return pl.pallas_call(
        functools.partial(forward_kernel, given, back),
        in_specs=[pl.BlockSpec(memory_space=pltpu.SMEM)] + [in_vmem] * (given + 3),
        out_specs=[in_vmem] * len(out_shape),
        out_shape=out_shape,
        scratch_shapes=[
            pltpu.VMEM((count, width), HALF),
            pltpu.VMEM((count, width), HALF),
        ],
        compiler_params=params(LIMIT),
        cost_estimate=pl.CostEstimate(flops=cost, bytes_accessed=0, transcendentals=0),
        name="forward_back" if back else "forward",
    )(place, *blocks, gate, up, down)


def grads_kernel(n, early, *refs):
    own, parts, came, refs = refs[:n], refs[n : 2 * n], refs[2 * n : 3 * n], refs[3 * n :]
    sums, refs = refs[:early], refs[early:]
    gate_grad, up_grad, down_grad, act_rows, part_rows = refs
    start, reach = 0, act_rows.shape[1]
    for mine, piece, other in zip(own, parts, came):
        count = mine.shape[0]
        here, there = slice(start, start + count), slice(start + count, start + 2 * count)
        act_rows[here, :] = mine[:, 0:reach]
        part_rows[here, :] = piece[...]
        act_rows[there, :] = other[:, 0:reach]
        part_rows[there, :] = other[:, reach:]
        start += 2 * count
    part = part_rows.shape[1] // 2
    tiles = act_rows.shape[1] // (3 * TILE)

    def put(k, out, rows, columns, value):
        if early:
            value = value + sums[k][rows, columns].astype(FULL)
        out[rows, columns] = value.astype(HALF)

    for i in range(part // TILE):
        picked = part_rows[:, i * TILE : (i + 1) * TILE].T
        here = slice(i * TILE, (i + 1) * TILE)
        for j in range(tiles):
            at = 3 * TILE * j
            there = slice(j * TILE, (j + 1) * TILE)
            gate_back = act_rows[:, at + TILE : at + 2 * TILE]
            up_back = act_rows[:, at + 2 * TILE : at + 3 * TILE]
            put(0, gate_grad, here, there, jnp.dot(picked, gate_back, preferred_element_type=FULL))
            put(1, up_grad, here, there, jnp.dot(picked, up_back, preferred_element_type=FULL))
    cotan = part_rows[:, part : 2 * part]
    for j in range(tiles):
        at = 3 * TILE * j
        hidden = act_rows[:, at : at + TILE].T
        here = slice(j * TILE, (j + 1) * TILE)
        value = jnp.dot(hidden, cotan, preferred_element_type=FULL)
        put(2, down_grad, here, slice(0, part), value)


def grads(own, parts, came, hidden, early=(), cost=COST):
    n, count, part = len(own), 2 * sum(a.shape[0] for a in own), parts[0].shape[1] // 2
    in_vmem = pl.BlockSpec(memory_space=pltpu.VMEM)
    return pl.pallas_call(
        functools.partial(grads_kernel, n, len(early)),
        in_specs=[in_vmem] * (3 * n + len(early)),
        out_specs=[in_vmem] * 3,
        out_shape=[shape((part, hidden)), shape((part, hidden)), shape((hidden, part))],
        scratch_shapes=[
            pltpu.VMEM((count, 3 * hidden), HALF),
            pltpu.VMEM((count, 2 * part), HALF),
        ],
        compiler_params=params(GRADS_LIMIT),
        cost_estimate=pl.CostEstimate(flops=cost, bytes_accessed=0, transcendentals=0),
        name="grads",
    )(*own, *parts, *came, *early)


def settle_kernel(place, block, out):
    out[0] = place[0]
    out[1] = place[1]


def settle(place, block):
    in_smem = pl.BlockSpec(memory_space=pltpu.SMEM)
    return pl.pallas_call(
        settle_kernel,
        in_specs=[in_smem, pl.BlockSpec(memory_space=pl.ANY)],
        out_specs=in_smem,
        out_shape=shape((2,), jnp.int32),
        compiler_params=params(LIMIT),
        cost_estimate=pl.CostEstimate(
            flops=WAIT, bytes_accessed=0, transcendentals=0
        ),
        name="settle",
    )(place, block)


def merge_kernel(n, keep, came, *outs):
    mid = MAIN * n
    kept, other = keep[mid:, :].astype(FULL), came[mid:, :].astype(FULL)
    if n % 2:
        other = pltpu.roll(other, other.shape[0] - REST, 0)
    tails = kept + other
    for i, out in enumerate(outs):
        here = slice(MAIN * i, MAIN * (i + 1))
        out[0:MAIN, :] = (keep[here, :].astype(FULL) + came[here, :].astype(FULL)).astype(HALF)
        pair = tails[8 * (i // 2) : 8 * (i // 2) + 8]
        out[MAIN : MAIN + 8, :] = (pair if i % 2 == 0 else pltpu.roll(pair, REST, 0)).astype(HALF)


def merge(n, keep, came):
    return pl.pallas_call(
        functools.partial(merge_kernel, n),
        out_shape=[shape((MAIN + 8, keep.shape[1]))] * n,
        compiler_params=params(LIMIT),
        name="merge",
    )(keep, came)


def pair_kernel(a, b, out):
    out[0] = a[...]
    out[1] = b[...]


def pair(a, b):
    return pl.pallas_call(
        pair_kernel,
        out_shape=shape((2,) + a.shape),
        compiler_params=params(LIMIT),
        cost_estimate=pl.CostEstimate(flops=10**6, bytes_accessed=0, transcendentals=0),
        name="pair",
    )(a, b)


def add_kernel(a, b, out):
    out[...] = (a[...].astype(FULL) + b[...].astype(FULL)).astype(HALF)


def add(a, b):
    return pl.pallas_call(
        add_kernel, out_shape=shape(a.shape), compiler_params=params(LIMIT), name="add"
    )(a, b)


def after(value, *others):
    return lax.optimization_barrier((value, *others))[0]


def per_device(tokens, cotangent, route_ids, route_probs, gate_weight, up_weight, down_weight):
    n_dp, n_expert = lax.axis_size("dp"), lax.axis_size("expert")
    core_pairs = [(i, i ^ 1) for i in range(n_dp)]
    y_pairs = [(i, (i + 2) % n_dp) for i in range(n_dp)]
    x_pairs = [(i, i ^ 1) for i in range(n_expert)]

    def over_core(v):
        return lax.ppermute(v, "dp", core_pairs)

    def over_y(v):
        return lax.ppermute(v, "dp", y_pairs)

    def over_x(v):
        return lax.ppermute(v, "expert", x_pairs)

    def over_z(v, by):
        return lax.ppermute(
            v, "expert", [(i, (i + 2 * by) % n_expert) for i in range(n_expert)]
        )

    part = tokens.shape[1] // n_dp
    p = lax.axis_index("dp")
    place = jnp.stack([p, p + 1 - 2 * (p % 2)]).astype(jnp.int32)
    ids, probs = route_ids.T, route_probs.T

    b0 = pack(ids, probs, tokens, cotangent)
    place = settle(place, b0)
    z1, x0, y0 = over_z(b0, 1), over_x(b0), over_y(b0)
    z3 = over_z(after(b0, place), -1)
    z1 = after(z1, x0, y0, place)
    z2, x1 = over_z(z1, 1), over_x(z1)
    xy0 = over_y(after(x0, z1))
    x3 = over_x(z3)
    x2 = over_x(after(z2, x1))
    y3, xy3 = over_y(z3), over_y(x3)
    y2 = over_y(after(z2, x1))
    xy2 = over_y(x2)
    y1 = over_z(after(y0, z2), 1)

    run = functools.partial(
        forward, gate=gate_weight, up=up_weight, down=down_weight, place=place, part=part
    )
    act0, own0, send0, keep0 = run(
        [after(z1, xy0, z2), z3, x1, x3], back="halves", cost=COSTS[0]
    )
    came0 = over_x(send0)
    xy1 = over_z(after(xy0, send0), 1)
    act1, own1, keep2, near, send2, aside = run(
        [after(z2, send0, y3, y1, y2), b0, x2, x0], back="pieces", cost=COSTS[1]
    )
    came2 = over_x(send2)
    other0 = over_core(act0)
    p1, p3 = merge(2, keep0, after(came0, send2))
    r1, r3 = over_z(p1, -1), over_z(p3, 1)
    other1 = over_core(act1)
    y0 = after(y0, p1, other0, y2, xy1)
    act2, own2 = run([y0, xy0, y3, xy3], back=False, cost=COSTS[2])
    other2 = over_core(act2)
    y2 = after(y2, act2)
    act3, own3 = run([y2, xy2, y1, xy1], back=False, cost=COSTS[3])
    other3 = over_core(act3)
    p2 = add(keep2, after(came2, act3, r1, r3))
    r2 = over_z(p2, 2)
    beside = over_x(after(aside, p2))
    hidden = gate_weight.shape[1]
    early = grads([act0, act1], [own0, own1], [other0, other1], hidden, cost=COSTS[4])
    gate_grad, up_grad, down_grad = grads(
        [act2, act3], [own2, own3], [other2, other3], hidden, early, cost=COSTS[5]
    )
    token_grad = unpack(after(ids, gate_grad), [near, beside, r1, r2, r3])
    return token_grad, gate_grad, up_grad, down_grad


def pick_rows(placer, values):
    return lax.dot_general(
        placer, values, (((0,), (0,)), ((), ())), preferred_element_type=jnp.float32
    ).astype(jnp.bfloat16)


def per_device_general(tokens, cotangent, route_ids, route_probs, gate_weight, up_weight, down_weight):
    hits = route_ids == 0
    chosen = jnp.any(hits, axis=1).astype(jnp.int32)
    share = jnp.sum(jnp.where(hits, route_probs, 0.0), axis=1)
    slots = jnp.cumsum(chosen) - chosen
    placer_mask = (slots[:, None] == jnp.arange(CAP, dtype=jnp.int32)[None, :]) & (
        chosen[:, None] == 1
    )
    placer = placer_mask.astype(jnp.float32)
    placer_half = placer_mask.astype(jnp.bfloat16)
    local_rows = pick_rows(placer_half, tokens)
    local_cotan = pick_rows(placer_half, cotangent)
    local_shares = jnp.sum(placer * share[:, None], axis=0)
    routed, routed_cotan, routed_shares = (
        lax.all_gather(local_rows, "expert", axis=0, tiled=True),
        lax.all_gather(local_cotan, "expert", axis=0, tiled=True),
        lax.all_gather(local_shares.astype(jnp.bfloat16), "expert", axis=0, tiled=True).astype(
            local_shares.dtype
        ),
    )
    gate_pre = jnp.dot(routed, gate_weight, preferred_element_type=jnp.float32)
    up_pre = jnp.dot(routed, up_weight, preferred_element_type=jnp.float32)
    sigma = jax.nn.sigmoid(gate_pre)
    gate_act = gate_pre * sigma
    hidden = (gate_act * up_pre).astype(jnp.bfloat16)
    gate_pre, up_pre, sigma, gate_act, hidden = (gate_pre, up_pre, sigma, gate_act, hidden)
    scaled = (routed_shares[:, None] * routed_cotan.astype(jnp.float32)).astype(jnp.bfloat16)
    down_part = lax.dot_general(
        hidden, scaled, (((0,), (0,)), ((), ())), preferred_element_type=jnp.float32
    )
    hidden_back = lax.dot_general(
        scaled, down_weight, (((1,), (1,)), ((), ())), preferred_element_type=jnp.float32
    )
    gate_back = (hidden_back * up_pre * sigma * (1.0 + gate_pre * (1.0 - sigma))).astype(
        jnp.bfloat16
    )
    up_back = (hidden_back * gate_act).astype(jnp.bfloat16)
    gate_part = lax.dot_general(
        routed, gate_back, (((0,), (0,)), ((), ())), preferred_element_type=jnp.float32
    )
    up_part = lax.dot_general(
        routed, up_back, (((0,), (0,)), ((), ())), preferred_element_type=jnp.float32
    )
    gate_sum, up_sum, down_sum = (
        lax.psum_scatter(
            gate_part.astype(jnp.bfloat16), "dp", scatter_dimension=0, tiled=True
        ).astype(jnp.float32),
        lax.psum_scatter(
            up_part.astype(jnp.bfloat16), "dp", scatter_dimension=0, tiled=True
        ).astype(jnp.float32),
        lax.psum_scatter(
            down_part.astype(jnp.bfloat16), "dp", scatter_dimension=1, tiled=True
        ).astype(jnp.float32),
    )
    partial_value = lax.dot_general(
        gate_back, gate_weight, (((1,), (1,)), ((), ())), preferred_element_type=jnp.float32
    )
    partial_value = partial_value + lax.dot_general(
        up_back, up_weight, (((1,), (1,)), ((), ())), preferred_element_type=jnp.float32
    )
    returned = lax.psum_scatter(
        partial_value.astype(jnp.bfloat16), "expert", scatter_dimension=0, tiled=True
    ).astype(jnp.float32)
    token_grad = jnp.dot(placer, returned, precision=lax.Precision.HIGHEST).astype(jnp.bfloat16)
    return (
        token_grad,
        gate_sum.astype(jnp.bfloat16),
        up_sum.astype(jnp.bfloat16),
        down_sum.astype(jnp.bfloat16),
    )


def solution(mesh):
    in_specs = (
        P(("dp", "expert"), None),
        P(("dp", "expert"), None),
        P(("dp", "expert"), None),
        P(("dp", "expert"), None),
        P(None, "expert"),
        P(None, "expert"),
        P("expert", None),
    )
    out_specs = (P(("dp", "expert"), None), P("dp", "expert"), P("dp", "expert"), P("expert", "dp"))
    fast = mesh.shape["dp"] == 4 and mesh.shape["expert"] == 8
    body = per_device if fast else per_device_general
    return jax.shard_map(
        body, mesh=mesh, in_specs=in_specs, out_specs=out_specs, check_vma=False
    )
```

```python
import functools

import jax
import jax.numpy as jnp
from jax import lax
from jax.experimental import pallas as pl
from jax.experimental.pallas import tpu as pltpu
from jax.sharding import PartitionSpec as P

CAP = 36
MAIN = 32
REST = CAP - MAIN
TILE = 256
LIMIT = 9
GRADS_LIMIT = 14
WAIT = 20 * 10**9
COST = 10**10
COSTS = (10**10, 10**10, 10**6, 10**10, 4 * 10**10, 10**6)
HALF = jnp.bfloat16
FULL = jnp.float32


def shape(dims, dtype=HALF):
    return jax.ShapeDtypeStruct(dims, dtype)


def params(mib):
    return pltpu.CompilerParams(vmem_limit_bytes=mib * 2**20)


def nt_dot(a, b):
    return lax.dot_general(a, b, (((1,), (1,)), ((), ())), preferred_element_type=FULL)


def tn_dot(a, b):
    return lax.dot_general(a, b, (((0,), (0,)), ((), ())), preferred_element_type=FULL)


def earlier_count(ids):
    count = ids.shape[1]
    chosen = jnp.max((ids == 0).astype(FULL), axis=0, keepdims=True)
    chosen = jnp.broadcast_to(chosen, (8, count))
    before = lax.broadcasted_iota(jnp.int32, (count, count), 0) < lax.broadcasted_iota(
        jnp.int32, (count, count), 1
    )
    slots = jnp.dot(
        chosen.astype(HALF), before.astype(FULL).astype(HALF), preferred_element_type=FULL
    )
    return chosen, slots


def one_hot(places, chosen, count):
    row = lax.broadcasted_iota(jnp.int32, (count, places.shape[1]), 0).astype(FULL)
    return jnp.where(row == places[0:1], jnp.broadcast_to(chosen[0:1], row.shape), 0.0)


def pack_kernel(ids_in, probs_in, tokens_in, cotangent_in, out, ids, probs, tokens, cotangent, done):
    pairs = ((ids_in, ids), (probs_in, probs), (tokens_in, tokens), (cotangent_in, cotangent))
    copies = [pltpu.make_async_copy(a, b, done.at[i]) for i, (a, b) in enumerate(pairs)]
    for copy in copies:
        copy.start()
    copies[0].wait()
    copies[1].wait()
    chosen, slots = earlier_count(ids[...])
    late = (slots >= MAIN).astype(FULL)
    pick_rows = one_hot(slots + late * MAIN, chosen, 80).astype(HALF)
    picked = one_hot(slots + MAIN + late * REST, chosen, 80)
    total = jnp.sum(jnp.where(ids[...] == 0, probs[...], 0.0), axis=0, keepdims=True)
    share = jnp.sum(picked * total, axis=1, keepdims=True)
    picked = picked.astype(HALF)
    copies[2].wait()
    copies[3].wait()
    width = out.shape[1]
    for i in range(0, width, 768):
        here = slice(i, i + 768)
        cotan = jnp.dot(picked, cotangent[:, here], preferred_element_type=FULL)
        rows = jnp.dot(pick_rows, tokens[:, here], preferred_element_type=FULL)
        out[:, here] = (rows + share * cotan)[0 : 2 * CAP].astype(HALF)


def pack(ids, probs, tokens, cotangent):
    values = (ids, probs, tokens, cotangent)
    return pl.pallas_call(
        pack_kernel,
        in_specs=[pl.BlockSpec(memory_space=pltpu.HBM)] * 4,
        out_shape=shape((2 * CAP, tokens.shape[1])),
        scratch_shapes=[pltpu.VMEM(v.shape, v.dtype) for v in values]
        + [pltpu.SemaphoreType.DMA((4,))],
        compiler_params=params(60),
        name="pack",
    )(*values)


def settle_rows_kernel(ids, *refs):
    pieces, (place, total) = refs[:-2], refs[-2:]
    chosen, slots = earlier_count(ids[...])
    place[...] = one_hot(slots, chosen, place.shape[0]).astype(HALF)
    found = pieces[0][...].astype(FULL)
    for piece in pieces[1:]:
        found = found + piece[...].astype(FULL)
    total[...] = found


def settle_rows(ids, pieces):
    depth, width = pieces[0].shape
    return pl.pallas_call(
        settle_rows_kernel,
        out_shape=[shape((depth, ids.shape[1])), shape((depth, width), FULL)],
        compiler_params=params(LIMIT),
        cost_estimate=pl.CostEstimate(flops=10**6, bytes_accessed=0, transcendentals=0),
        name="settle_rows",
    )(ids, *pieces)


def unpack_kernel(place, total, *refs):
    pieces, out = refs[:-1], refs[-1]
    found = total[...]
    for piece in pieces:
        found = found + piece[...].astype(FULL)
    out[...] = tn_dot(place[...], found.astype(HALF)).astype(HALF)


def unpack(place, total, pieces):
    (depth, width), count = total.shape, place.shape[1]
    step = 1536
    column = lambda j: (0, j)
    return pl.pallas_call(
        unpack_kernel,
        grid=(width // step,),
        in_specs=[pl.BlockSpec(place.shape, lambda j: (0, 0))]
        + [pl.BlockSpec((depth, step), column) for _ in range(1 + len(pieces))],
        out_specs=pl.BlockSpec((count, step), column),
        out_shape=shape((count, width)),
        compiler_params=params(LIMIT),
        name="unpack",
    )(place, total, *pieces)


def padded_rows(n):
    return MAIN * n + -(-REST * n // 16) * 16


def assemble(blocks, rows, scaled):
    n, width = len(blocks), rows.shape[1]
    for i, block in enumerate(blocks):
        rows[MAIN * i : MAIN * (i + 1), :] = block[0:MAIN, :]
        scaled[MAIN * i : MAIN * (i + 1), :] = block[MAIN : 2 * MAIN, :]
    first = lax.broadcasted_iota(jnp.int32, (2 * REST, width), 0) < REST
    tails = [block[2 * MAIN : 2 * CAP, :].astype(FULL) for block in blocks]
    row_tails, scaled_tails = [], []
    for a, b in zip(tails[0::2], tails[1::2]):
        row_tails.append(jnp.where(first, a, pltpu.roll(b, REST, 0)))
        scaled_tails.append(jnp.where(first, pltpu.roll(a, REST, 0), b))
    if len(row_tails) % 2:
        row_tails.append(jnp.zeros((2 * REST, width), FULL))
        scaled_tails.append(jnp.zeros((2 * REST, width), FULL))
    for i in range(0, len(row_tails), 2):
        here = slice(MAIN * n + 8 * i, MAIN * n + 8 * i + 16)
        rows[here, :] = jnp.concatenate(row_tails[i : i + 2], axis=0).astype(HALF)
        scaled[here, :] = jnp.concatenate(scaled_tails[i : i + 2], axis=0).astype(HALF)


def activations(rows, scaled, gate, up, down):
    gate_pre = jnp.dot(rows, gate, preferred_element_type=FULL)
    up_pre = jnp.dot(rows, up, preferred_element_type=FULL)
    hidden_back = nt_dot(scaled, down)
    sigma = jax.nn.sigmoid(gate_pre)
    gate_act = gate_pre * sigma
    hidden = (gate_act * up_pre).astype(HALF)
    gate_back = (hidden_back * up_pre * sigma * (1.0 + gate_pre * (1.0 - sigma))).astype(HALF)
    up_back = (hidden_back * gate_act).astype(HALF)
    return hidden, gate_back, up_back


def forward_kernel(n, back, place, *refs):
    arrays, weights, refs = refs[:n], refs[n : n + 3], refs[n + 3 :]
    blocks = []
    for array in arrays:
        blocks += [array] if len(array.shape) == 2 else [array.at[0], array.at[1]]
    n = len(blocks)
    acts, own = refs[:2]
    refs = refs[2:]
    if back == "halves":
        send, keep = refs[:2]
        refs = refs[2:]
    elif back == "pieces":
        pieces, refs = refs[:n], refs[n:]
    rows, scaled = refs
    gate, up, down = weights
    width, part = rows.shape[1], own.shape[1] // 2
    assemble(blocks, rows, scaled)
    base = 3 * gate.shape[1]
    for out, start, index in ((own, 0, 0), (acts, base, 1)):
        columns = pl.ds(pl.multiple_of(place[index] * part, part), part)
        out[:, start : start + part] = rows[:, columns]
        out[:, start + part : start + 2 * part] = scaled[:, columns]
    tiles = gate.shape[1] // TILE
    for j in range(tiles):
        here = slice(TILE * j, TILE * (j + 1))
        found = activations(rows[...], scaled[...], gate[:, here], up[:, here], down[here, :])
        for k in range(3):
            at = TILE * (3 * j + k)
            acts[:, at : at + TILE] = found[k]
    if back:
        half = n // 2
        mid, tail, reach = MAIN * half, MAIN * n, 8 * (-(-half // 2))
        skip = 8 * half - reach
        gate_back = [acts[:, TILE * (3 * j + 1) : TILE * (3 * j + 2)] for j in range(tiles)]
        up_back = [acts[:, TILE * (3 * j + 2) : TILE * (3 * j + 3)] for j in range(tiles)]
        gate_back, up_back = jnp.concatenate(gate_back, axis=1), jnp.concatenate(up_back, axis=1)
        for i in range(0, width, 2 * TILE):
            here = slice(i, i + 2 * TILE)
            total = nt_dot(gate_back, gate[here, :]) + nt_dot(up_back, up[here, :])
            if back == "pieces":
                for k, piece in enumerate(pieces):
                    piece[0:MAIN, here] = total[MAIN * k : MAIN * (k + 1)].astype(HALF)
                    pair = total[tail + 8 * (k // 2) : tail + 8 * (k // 2) + 8]
                    pair = pair if k % 2 == 0 else pltpu.roll(pair, REST, 0)
                    piece[MAIN : MAIN + 8, here] = pair.astype(HALF)
                continue
            keep[0:mid, here] = total[0:mid].astype(HALF)
            send[0:mid, here] = total[mid : 2 * mid].astype(HALF)
            keep[mid : mid + reach, here] = total[tail : tail + reach].astype(HALF)
            send[mid : mid + reach, here] = total[tail + skip : tail + skip + reach].astype(HALF)


def forward(blocks, gate, up, down, place, part, back, cost=COST):
    given, (width, hidden) = len(blocks), gate.shape
    n = sum(1 if len(block.shape) == 2 else 2 for block in blocks)
    count = padded_rows(n)
    in_vmem = pl.BlockSpec(memory_space=pltpu.VMEM)
    out_shape = [
        shape((count, 3 * hidden + 2 * part)),
        shape((count, 2 * part)),
    ]
    if back == "pieces":
        out_shape += [shape((MAIN + 8, width))] * n
    elif back:
        half = n // 2
        out_shape += [shape((MAIN * half + 8 * (-(-half // 2)), width))] * 2
    matmuls = 5 if back else 3
    return pl.pallas_call(
        functools.partial(forward_kernel, given, back),
        in_specs=[pl.BlockSpec(memory_space=pltpu.SMEM)] + [in_vmem] * (given + 3),
        out_specs=[in_vmem] * len(out_shape),
        out_shape=out_shape,
        scratch_shapes=[
            pltpu.VMEM((count, width), HALF),
            pltpu.VMEM((count, width), HALF),
        ],
        compiler_params=params(LIMIT),
        cost_estimate=pl.CostEstimate(flops=cost, bytes_accessed=0, transcendentals=0),
        name="forward_back" if back else "forward",
    )(place, *blocks, gate, up, down)


def grads_kernel(n, early, *refs):
    own, parts, came, refs = refs[:n], refs[n : 2 * n], refs[2 * n : 3 * n], refs[3 * n :]
    sums, refs = refs[:early], refs[early:]
    gate_grad, up_grad, down_grad, act_rows, part_rows = refs
    start, reach = 0, act_rows.shape[1]
    for mine, piece, other in zip(own, parts, came):
        count = mine.shape[0]
        here, there = slice(start, start + count), slice(start + count, start + 2 * count)
        act_rows[here, :] = mine[:, 0:reach]
        part_rows[here, :] = piece[...]
        act_rows[there, :] = other[:, 0:reach]
        part_rows[there, :] = other[:, reach:]
        start += 2 * count
    part = part_rows.shape[1] // 2
    tiles = act_rows.shape[1] // (3 * TILE)

    def put(k, out, rows, columns, value):
        if early:
            value = value + sums[k][rows, columns].astype(FULL)
        out[rows, columns] = value.astype(HALF)

    for i in range(part // TILE):
        picked = part_rows[:, i * TILE : (i + 1) * TILE].T
        here = slice(i * TILE, (i + 1) * TILE)
        for j in range(tiles):
            at = 3 * TILE * j
            there = slice(j * TILE, (j + 1) * TILE)
            gate_back = act_rows[:, at + TILE : at + 2 * TILE]
            up_back = act_rows[:, at + 2 * TILE : at + 3 * TILE]
            put(0, gate_grad, here, there, jnp.dot(picked, gate_back, preferred_element_type=FULL))
            put(1, up_grad, here, there, jnp.dot(picked, up_back, preferred_element_type=FULL))
    cotan = part_rows[:, part : 2 * part]
    for j in range(tiles):
        at = 3 * TILE * j
        hidden = act_rows[:, at : at + TILE].T
        here = slice(j * TILE, (j + 1) * TILE)
        value = jnp.dot(hidden, cotan, preferred_element_type=FULL)
        put(2, down_grad, here, slice(0, part), value)


def grads(own, parts, came, hidden, early=(), cost=COST):
    n, count, part = len(own), 2 * sum(a.shape[0] for a in own), parts[0].shape[1] // 2
    in_vmem = pl.BlockSpec(memory_space=pltpu.VMEM)
    return pl.pallas_call(
        functools.partial(grads_kernel, n, len(early)),
        in_specs=[in_vmem] * (3 * n + len(early)),
        out_specs=[in_vmem] * 3,
        out_shape=[shape((part, hidden)), shape((part, hidden)), shape((hidden, part))],
        scratch_shapes=[
            pltpu.VMEM((count, 3 * hidden), HALF),
            pltpu.VMEM((count, 2 * part), HALF),
        ],
        compiler_params=params(GRADS_LIMIT),
        cost_estimate=pl.CostEstimate(flops=cost, bytes_accessed=0, transcendentals=0),
        name="grads",
    )(*own, *parts, *came, *early)


def settle_kernel(place, block, out):
    out[0] = place[0]
    out[1] = place[1]


def settle(place, block):
    in_smem = pl.BlockSpec(memory_space=pltpu.SMEM)
    return pl.pallas_call(
        settle_kernel,
        in_specs=[in_smem, pl.BlockSpec(memory_space=pl.ANY)],
        out_specs=in_smem,
        out_shape=shape((2,), jnp.int32),
        compiler_params=params(LIMIT),
        cost_estimate=pl.CostEstimate(
            flops=WAIT, bytes_accessed=0, transcendentals=0
        ),
        name="settle",
    )(place, block)


def merge_kernel(n, keep, came, *outs):
    mid = MAIN * n
    kept, other = keep[mid:, :].astype(FULL), came[mid:, :].astype(FULL)
    if n % 2:
        other = pltpu.roll(other, other.shape[0] - REST, 0)
    tails = kept + other
    for i, out in enumerate(outs):
        here = slice(MAIN * i, MAIN * (i + 1))
        out[0:MAIN, :] = (keep[here, :].astype(FULL) + came[here, :].astype(FULL)).astype(HALF)
        pair = tails[8 * (i // 2) : 8 * (i // 2) + 8]
        out[MAIN : MAIN + 8, :] = (pair if i % 2 == 0 else pltpu.roll(pair, REST, 0)).astype(HALF)


def merge(n, keep, came):
    return pl.pallas_call(
        functools.partial(merge_kernel, n),
        out_shape=[shape((MAIN + 8, keep.shape[1]))] * n,
        compiler_params=params(LIMIT),
        name="merge",
    )(keep, came)


def pair_kernel(a, b, out):
    out[0] = a[...]
    out[1] = b[...]


def pair(a, b):
    return pl.pallas_call(
        pair_kernel,
        out_shape=shape((2,) + a.shape),
        compiler_params=params(LIMIT),
        cost_estimate=pl.CostEstimate(flops=10**6, bytes_accessed=0, transcendentals=0),
        name="pair",
    )(a, b)


def add_kernel(a, b, out):
    out[...] = (a[...].astype(FULL) + b[...].astype(FULL)).astype(HALF)


def add(a, b):
    return pl.pallas_call(
        add_kernel, out_shape=shape(a.shape), compiler_params=params(LIMIT), name="add"
    )(a, b)


def after(value, *others):
    return lax.optimization_barrier((value, *others))[0]


def per_device(tokens, cotangent, route_ids, route_probs, gate_weight, up_weight, down_weight):
    n_dp, n_expert = lax.axis_size("dp"), lax.axis_size("expert")
    core_pairs = [(i, i ^ 1) for i in range(n_dp)]
    y_pairs = [(i, (i + 2) % n_dp) for i in range(n_dp)]
    x_pairs = [(i, i ^ 1) for i in range(n_expert)]

    def over_core(v):
        return lax.ppermute(v, "dp", core_pairs)

    def over_y(v):
        return lax.ppermute(v, "dp", y_pairs)

    def over_x(v):
        return lax.ppermute(v, "expert", x_pairs)

    def over_z(v, by):
        return lax.ppermute(
            v, "expert", [(i, (i + 2 * by) % n_expert) for i in range(n_expert)]
        )

    part = tokens.shape[1] // n_dp
    p = lax.axis_index("dp")
    place = jnp.stack([p, p + 1 - 2 * (p % 2)]).astype(jnp.int32)
    ids, probs = route_ids.T, route_probs.T

    b0 = pack(ids, probs, tokens, cotangent)
    place = settle(place, b0)
    z1, x0, y0 = over_z(b0, 1), over_x(b0), over_y(b0)
    z3 = over_z(after(b0, place), -1)
    z1 = after(z1, x0, y0, place)
    z2, x1 = over_z(z1, 1), over_x(z1)
    xy0 = over_y(after(x0, z1))
    x3 = over_x(z3)
    x2 = over_x(after(z2, x1))
    y3, xy3 = over_y(z3), over_y(x3)
    y2 = over_y(after(z2, x1))
    xy2 = over_y(x2)
    y1 = over_z(after(y0, z2), 1)

    run = functools.partial(
        forward, gate=gate_weight, up=up_weight, down=down_weight, place=place, part=part
    )
    act0, own0, send0, keep0 = run(
        [after(z1, xy0, z2), z3, x1, x3], back="halves", cost=COSTS[0]
    )
    came0 = over_x(send0)
    xy1 = over_z(after(xy0, send0), 1)
    act1, own1, keep2, near, send2, aside = run(
        [after(z2, send0, y3, y1, y2), b0, x2, x0], back="pieces", cost=COSTS[1]
    )
    came2 = over_x(send2)
    other0 = over_core(act0)
    p1, p3 = merge(2, keep0, after(came0, send2))
    r1, r3 = over_z(p1, -1), over_z(p3, 1)
    other1 = over_core(act1)
    y0 = after(y0, p1, other0, y2, xy1)
    act2, own2 = run([y0, xy0, y3, xy3], back=False, cost=COSTS[2])
    other2 = over_core(act2)
    y2 = after(y2, act2)
    act3, own3 = run([y2, xy2, y1, xy1], back=False, cost=COSTS[3])
    other3 = over_core(act3)
    p2 = add(keep2, after(came2, act3, r1, r3))
    r2 = over_z(p2, 2)
    beside = over_x(after(aside, p2))
    hidden = gate_weight.shape[1]
    early = grads([act0, act1], [own0, own1], [other0, other1], hidden, cost=COSTS[4])
    gate_grad, up_grad, down_grad = grads(
        [act2, act3], [own2, own3], [other2, other3], hidden, early, cost=COSTS[5]
    )
    row_place, row_total = settle_rows(after(ids, gate_grad), [near, r1, r3])
    token_grad = unpack(row_place, row_total, [beside, r2])
    return token_grad, gate_grad, up_grad, down_grad


def pick_rows(placer, values):
    return lax.dot_general(
        placer, values, (((0,), (0,)), ((), ())), preferred_element_type=jnp.float32
    ).astype(jnp.bfloat16)


def per_device_general(tokens, cotangent, route_ids, route_probs, gate_weight, up_weight, down_weight):
    hits = route_ids == 0
    chosen = jnp.any(hits, axis=1).astype(jnp.int32)
    share = jnp.sum(jnp.where(hits, route_probs, 0.0), axis=1)
    slots = jnp.cumsum(chosen) - chosen
    placer_mask = (slots[:, None] == jnp.arange(CAP, dtype=jnp.int32)[None, :]) & (
        chosen[:, None] == 1
    )
    placer = placer_mask.astype(jnp.float32)
    placer_half = placer_mask.astype(jnp.bfloat16)
    local_rows = pick_rows(placer_half, tokens)
    local_cotan = pick_rows(placer_half, cotangent)
    local_shares = jnp.sum(placer * share[:, None], axis=0)
    routed, routed_cotan, routed_shares = (
        lax.all_gather(local_rows, "expert", axis=0, tiled=True),
        lax.all_gather(local_cotan, "expert", axis=0, tiled=True),
        lax.all_gather(local_shares.astype(jnp.bfloat16), "expert", axis=0, tiled=True).astype(
            local_shares.dtype
        ),
    )
    gate_pre = jnp.dot(routed, gate_weight, preferred_element_type=jnp.float32)
    up_pre = jnp.dot(routed, up_weight, preferred_element_type=jnp.float32)
    sigma = jax.nn.sigmoid(gate_pre)
    gate_act = gate_pre * sigma
    hidden = (gate_act * up_pre).astype(jnp.bfloat16)
    gate_pre, up_pre, sigma, gate_act, hidden = (gate_pre, up_pre, sigma, gate_act, hidden)
    scaled = (routed_shares[:, None] * routed_cotan.astype(jnp.float32)).astype(jnp.bfloat16)
    down_part = lax.dot_general(
        hidden, scaled, (((0,), (0,)), ((), ())), preferred_element_type=jnp.float32
    )
    hidden_back = lax.dot_general(
        scaled, down_weight, (((1,), (1,)), ((), ())), preferred_element_type=jnp.float32
    )
    gate_back = (hidden_back * up_pre * sigma * (1.0 + gate_pre * (1.0 - sigma))).astype(
        jnp.bfloat16
    )
    up_back = (hidden_back * gate_act).astype(jnp.bfloat16)
    gate_part = lax.dot_general(
        routed, gate_back, (((0,), (0,)), ((), ())), preferred_element_type=jnp.float32
    )
    up_part = lax.dot_general(
        routed, up_back, (((0,), (0,)), ((), ())), preferred_element_type=jnp.float32
    )
    gate_sum, up_sum, down_sum = (
        lax.psum_scatter(
            gate_part.astype(jnp.bfloat16), "dp", scatter_dimension=0, tiled=True
        ).astype(jnp.float32),
        lax.psum_scatter(
            up_part.astype(jnp.bfloat16), "dp", scatter_dimension=0, tiled=True
        ).astype(jnp.float32),
        lax.psum_scatter(
            down_part.astype(jnp.bfloat16), "dp", scatter_dimension=1, tiled=True
        ).astype(jnp.float32),
    )
    partial_value = lax.dot_general(
        gate_back, gate_weight, (((1,), (1,)), ((), ())), preferred_element_type=jnp.float32
    )
    partial_value = partial_value + lax.dot_general(
        up_back, up_weight, (((1,), (1,)), ((), ())), preferred_element_type=jnp.float32
    )
    returned = lax.psum_scatter(
        partial_value.astype(jnp.bfloat16), "expert", scatter_dimension=0, tiled=True
    ).astype(jnp.float32)
    token_grad = jnp.dot(placer, returned, precision=lax.Precision.HIGHEST).astype(jnp.bfloat16)
    return (
        token_grad,
        gate_sum.astype(jnp.bfloat16),
        up_sum.astype(jnp.bfloat16),
        down_sum.astype(jnp.bfloat16),
    )


def solution(mesh):
    in_specs = (
        P(("dp", "expert"), None),
        P(("dp", "expert"), None),
        P(("dp", "expert"), None),
        P(("dp", "expert"), None),
        P(None, "expert"),
        P(None, "expert"),
        P("expert", None),
    )
    out_specs = (P(("dp", "expert"), None), P("dp", "expert"), P("dp", "expert"), P("expert", "dp"))
    fast = mesh.shape["dp"] == 4 and mesh.shape["expert"] == 8
    body = per_device if fast else per_device_general
    return jax.shard_map(
        body, mesh=mesh, in_specs=in_specs, out_specs=out_specs, check_vma=False
    )
```
